128 devices in a mesh: cable: 32 (over x, y_lo, z), seg: 4 (over y_hi, core).
Axes of the slice: x: 4, y: 4 (y_hi: 2, y_lo: 2; y = y_hi * 2 + y_lo), z: 4, core: 2. Of those that a mesh axis runs over, the one named last changes fastest.
Arguments:
- frames: bfloat16 [4096, 64, 256], P('seg', 'cable'), may hold values from -6 to 6
- tension: float32 [4096, 64], P('seg', 'cable'), may hold values from 0.1 to 10
- step_index: int32 [256], replicated, may hold values from 0 to 15
- owner_map: int32 [64], replicated, may hold values from 0 to 63, each once
- old_basis: bfloat16 [4, 1024, 64, 256], P('seg', 'cable'), may hold values from -6 to 6
- singular: float32 [256], replicated, may hold values from 0.5 to 5
Outputs:
- factor: float32 [512, 512], replicated
- new_basis: bfloat16 [4, 1024, 64, 512], P('seg', 'cable')
The draws below stay inside these ranges and needn't reach their ends.
Inputs may be any that keep to these rules, and one draw needn't show every extreme that they name: `owner_map`: each streamer number appears exactly once.
All inputs are finite; a program needn't handle non-finite values.
Results may differ from the reference program's by a relative error of at most 0.001.
The reference program's roundings to bfloat16 on the way count: a program that leaves them out, or rounds other values in their place, can miss the bound.
Values may be sent and summed in bfloat16 or wider, within the bound.
A program may use at most 64 MiB of HBM per device.

```python
import math
import jax
import jax.numpy as jnp
from jax import lax

K = 256
SNAP = 256
SWEEPS = 6
NODE_DEV = 1024
STREAMERS = 64
NODES = 4096
ROWS_ALL = 262144
N_SEG = 4


def plant(array, rng, smallest, largest):
    extent = array.shape
    spot = [jax.random.randint(jax.random.fold_in(rng, axis), (), 0, extent[axis]) for axis in range(len(extent))]
    array = array.at[tuple(spot)].set(smallest)
    longest = extent.index(max(extent))
    spot[longest] = (spot[longest] + 1) % extent[longest]
    return array.at[tuple(spot)].set(largest)


def levels(rng, extent, split, least, high):
    gain, own = 1.0, jax.random.fold_in(rng, 6)
    for dim, shards_of in split:
        heights = jnp.exp(jax.random.uniform(jax.random.fold_in(own, dim), (shards_of,), jnp.float32, least / len(split), high / len(split)))
        gain = gain * jnp.repeat(heights, extent[dim] // shards_of).reshape([-1 if axis == dim else 1 for axis in range(len(extent))])
    return gain


def noise(stream_key, shape, deviation, limit, pieces=(), held_as=jnp.bfloat16):
    entries = deviation * jax.random.normal(stream_key, shape, jnp.float32)
    if pieces:
        entries = entries * levels(stream_key, shape, pieces, -0.22, 0.18)
    return jnp.clip(entries, -limit, limit).astype(held_as)


def setup_inputs(seed: int = 0) -> dict:
    key_list = jax.random.split(jax.random.key(seed), 7)
    frames = noise(key_list[0], (NODES, STREAMERS, SNAP), 1.0, 6.0, ((0, 4), (1, 32)))
    tension = jnp.clip(jnp.exp(math.log(10.0) - 4.6051702 * jax.random.uniform(key_list[1], (NODES, STREAMERS), jnp.float32) ** levels(key_list[1], (NODES, STREAMERS), ((0, 4), (1, 32)), -0.2, 0.2)), 0.1, 10.0)
    step_index = plant(jax.random.randint(key_list[2], (SNAP,), 0, 16), jax.random.fold_in(key_list[2], 1), 0, 15).astype(jnp.int32)
    owner_map = jax.random.permutation(key_list[3], STREAMERS).astype(jnp.int32)
    old_basis = noise(key_list[4], (N_SEG, NODE_DEV, STREAMERS, K), 1.0, 6.0, ((0, 4), (1, 32)))
    singular = jnp.clip(jnp.exp(jax.random.uniform(key_list[5], (K,), jnp.float32, math.log(0.5), math.log(5.0))), 0.5, 5.0)
    return {"frames": frames, "tension": tension, "step_index": step_index, "owner_map": owner_map, "old_basis": old_basis, "singular": singular}


drag_rate = 0.1

def relax_one(frames_one, tension_one, stiffness):
    source = frames_one.astype(jnp.float32)
    tension_wide = jnp.pad(tension_one, 1)
    right_weight = (0.5 * (tension_wide[1:-1] + tension_wide[2:]))[:, None]
    left_weight = (0.5 * (tension_wide[:-2] + tension_wide[1:-1]))[:, None]
    denom = 1.0 + stiffness[None, :] * (left_weight + right_weight)
    current = source
    for repeat in range(SWEEPS):
        padded = jnp.pad(current, ((1, 1), (0, 0)))
        current = (source + stiffness[None, :] * (right_weight * padded[2:] + left_weight * padded[:-2])) / denom
    return current.astype(jnp.bfloat16)

def reference(frames, tension, step_index, owner_map, old_basis, singular):
    stiffness = drag_rate * (1.0 + step_index.astype(jnp.float32))
    solved = lax.map(lambda pair: relax_one(pair[0], pair[1], stiffness), (jnp.moveaxis(frames, 1, 0), jnp.transpose(tension)))
    ordered = jnp.moveaxis(solved[owner_map.astype(jnp.int32)], 0, 1)
    width = K + SNAP
    gram_sum = jnp.zeros((width, width), jnp.float32)
    blocks = []
    for segment in range(N_SEG):
        scaled_basis = (old_basis[segment].astype(jnp.float32) * singular).astype(jnp.bfloat16)
        right_part = ordered[segment * NODE_DEV:(segment + 1) * NODE_DEV]
        flat_rows = jnp.concatenate([scaled_basis, right_part], axis=-1).reshape(-1, width)
        blocks.append(flat_rows)
        gram_sum = gram_sum + jnp.dot(flat_rows.T.astype(jnp.float32), flat_rows.astype(jnp.float32), preferred_element_type=jnp.float32)
    gram_sum = gram_sum / ROWS_ALL
    lower_chol = jnp.linalg.cholesky(gram_sum)
    factor = jnp.transpose(lower_chol)
    identity_m = jnp.eye(width, dtype=jnp.float32)
    inverse_bf = jnp.transpose(jax.scipy.linalg.solve_triangular(lower_chol, identity_m, lower=True)).astype(jnp.bfloat16)
    rotated = [jnp.dot(rows.astype(jnp.float32), inverse_bf.astype(jnp.float32), preferred_element_type=jnp.float32).astype(jnp.bfloat16).reshape(NODE_DEV, STREAMERS, width) for rows in blocks]
    return (factor, jnp.stack(rotated))
```

```python
import jax
import jax.numpy as jnp
from jax import lax
from jax.experimental import pallas as pl
from jax.experimental.pallas import tpu as pltpu
from jax.sharding import PartitionSpec as P

K = 256
SNAP = 256
SWEEPS = 6
DRAG_RATE = 0.1
STRIPS = 8
EDGE = 16
MESH = pl.DeviceIdType.MESH
HI = lax.Precision.HIGHEST
VMEM = pltpu.VMEM
F32 = jnp.float32
BF16 = jnp.bfloat16


def vmem_spec():
    return pl.BlockSpec(memory_space=pltpu.VMEM)


def nt(a, b, precision=None):
    return lax.dot_general(a, b, (((1,), (1,)), ((), ())), precision=precision, preferred_element_type=F32)


def nn(a, b, precision=None):
    return lax.dot_general(a, b, (((1,), (0,)), ((), ())), precision=precision, preferred_element_type=F32)


def tn(a, b, precision=None):
    return lax.dot_general(a, b, (((0,), (0,)), ((), ())), precision=precision, preferred_element_type=F32)


def greet(n_cable, n_seg):
    cable, seg = lax.axis_index("cable"), lax.axis_index("seg")
    barrier = pltpu.get_barrier_semaphore()

    def hail_cable(d, _):
        peer = lax.rem(cable + d, n_cable)
        pl.semaphore_signal(barrier, inc=1, device_id=(peer, seg), device_id_type=MESH)
        return 0

    def hail_seg(d, _):
        peer = lax.rem(seg + d, n_seg)
        pl.semaphore_signal(barrier, inc=1, device_id=(cable, peer), device_id_type=MESH)
        return 0

    lax.fori_loop(1, n_cable, hail_cable, 0)
    lax.fori_loop(1, n_seg, hail_seg, 0)
    pl.semaphore_wait(barrier, n_cable + n_seg - 2)


def relax_kernel(n_cable, n_seg, frames, tension, stiff, arrived,
                 padded, halo, tens_halo, tens_rows, weights, solved32, solved,
                 halo_send, halo_recv, send_sem, recv_sem):
    cable, seg = lax.axis_index("cable"), lax.axis_index("seg")
    nodes = frames.shape[0]
    strip = nodes // STRIPS
    block = nodes // n_cable
    greet(n_cable, n_seg)

    def halo_copies(side):
        peer = seg + 1 if side == 0 else seg - 1
        start = nodes - EDGE if side == 0 else 0
        lane = nodes - 128 if side == 0 else 0
        return [
            pltpu.make_async_remote_copy(
                src_ref=frames.at[pl.ds(start, EDGE), :], dst_ref=halo.at[side],
                send_sem=halo_send.at[side], recv_sem=halo_recv.at[side],
                device_id=(cable, peer), device_id_type=MESH),
            pltpu.make_async_remote_copy(
                src_ref=tension.at[:, pl.ds(lane, 128)], dst_ref=tens_halo.at[side],
                send_sem=halo_send.at[2 + side], recv_sem=halo_recv.at[2 + side],
                device_id=(cable, peer), device_id_type=MESH),
        ]

    @pl.when(seg < n_seg - 1)
    def _():
        for copy in halo_copies(0):
            copy.start()

    @pl.when(seg > 0)
    def _():
        for copy in halo_copies(1):
            copy.start()

    for tile in range(4):
        padded[tile, EDGE:EDGE + nodes, :] = frames[:, tile * 128:(tile + 1) * 128].astype(F32)
    for q in range(2):
        for s in range(STRIPS):
            tens_rows[q, 8 + s:9 + s, :] = tension[q:q + 1, s * strip:(s + 1) * strip]

    @pl.when(seg == 0)
    def _():
        halo[0] = jnp.zeros_like(halo[0])
        tens_halo[0] = jnp.zeros_like(tens_halo[0])

    @pl.when(seg == n_seg - 1)
    def _():
        halo[1] = jnp.zeros_like(halo[1])
        tens_halo[1] = jnp.zeros_like(tens_halo[1])

    @pl.when(seg > 0)
    def _():
        for copy in halo_copies(0):
            copy.wait_recv()

    @pl.when(seg < n_seg - 1)
    def _():
        for copy in halo_copies(1):
            copy.wait_recv()

    for tile in range(4):
        cols = slice(tile * 128, (tile + 1) * 128)
        padded[tile, 0:EDGE, :] = halo[0, :, cols].astype(F32)
        padded[tile, EDGE + nodes:, :] = halo[1, :, cols].astype(F32)
    reach = SWEEPS
    steps = strip + 2 * reach
    full = (STRIPS, 128)
    sub = lax.broadcasted_iota(jnp.int32, full, 0)
    lane = lax.broadcasted_iota(jnp.int32, full, 1)
    low_out = jnp.logical_and(sub == 0, seg == 0)
    high_out = jnp.logical_and(sub == STRIPS - 1, seg == n_seg - 1)
    for q in range(2):
        tens_rows[q, 7:8, :] = tens_halo[0, q:q + 1, :]
        tens_rows[q, 16:17, :] = tens_halo[1, q:q + 1, :]
        before, here, after = (tens_rows[q, 7 + i:15 + i, :] for i in range(3))

        def next_lane(x, y):
            return jnp.where(lane == 127, pltpu.roll(y, 127, 1), pltpu.roll(x, 127, 1))

        def prev_lane(x, y):
            return jnp.where(lane == 0, pltpu.roll(x, 1, 1), pltpu.roll(y, 1, 1))

        right = [0.5 * (before + next_lane(before, here)), 0.5 * (here + next_lane(here, after)),
                 0.5 * (after + next_lane(after, after))]
        left = [prev_lane(before, right[0]), prev_lane(right[0], right[1]), prev_lane(right[1], right[2])]
        for kind, rows in enumerate((left, right)):
            rows[0] = jnp.where(low_out, 0.0, rows[0])
            rows[2] = jnp.where(high_out, 0.0, rows[2])
            for step in range(steps):
                part, at = divmod(128 + step - reach, 128)
                weights[q, kind, step] = jnp.broadcast_to(rows[part][:, at:at + 1], full)

    def piece(q, peer, d):
        return pltpu.make_async_remote_copy(
            src_ref=solved.at[q, pl.ds(pl.multiple_of(peer * block, block), block), :],
            dst_ref=arrived.at[2 * cable + q],
            send_sem=send_sem.at[q, d], recv_sem=recv_sem.at[2 * cable + q],
            device_id=(peer, seg), device_id_type=MESH)

    for q in range(2):
        scale = [jnp.broadcast_to(stiff[0:1, h * 128:(h + 1) * 128], full) for h in range(2)]

        def advance(step, levels, coefs):
            lw, rw = weights[q, 0, step], weights[q, 1, step]
            total = lw + rw
            out = []
            for h in range(2):
                value = padded[2 * q + h, pl.ds(EDGE - reach + step, STRIPS, stride=strip), :]
                inv = 1.0 / (1.0 + scale[h] * total)
                si = scale[h] * inv
                coefs[h].append((si * lw, si * rw, value * inv))
                levels[h][0].append(value)
                for k in range(1, SWEEPS + 1):
                    below, above, own = coefs[h][-1 - k]
                    value = own + (above * levels[h][k - 1][-1] + below * levels[h][k - 1][-3])
                    levels[h][k].append(value)
                coefs[h][:] = coefs[h][-(SWEEPS + 1):]
                for k in range(SWEEPS + 1):
                    levels[h][k][:] = levels[h][k][-2:] if k < SWEEPS else levels[h][k][-1:]
                out.append(levels[h][SWEEPS][-1])
            return out

        zero = jnp.zeros(full, F32)
        levels = [[[zero, zero] for _ in range(SWEEPS)] + [[zero]] for _ in range(2)]
        coefs = [[(zero, zero, zero)] * (SWEEPS + 1) for _ in range(2)]
        for step in range(2 * reach):
            advance(step, levels, coefs)

        unroll = 8

        def turn(i, carry):
            levels, coefs = jax.tree.map(lambda x: x, carry)
            levels = [[list(x) for x in lv] for lv in levels]
            coefs = [[tuple(x) for x in cf] for cf in coefs]
            for u in range(unroll):
                row = i * unroll + u
                out = advance(2 * reach + row, levels, coefs)
                for h in range(2):
                    solved32[h, pl.ds(row, STRIPS, stride=strip), :] = out[h]
            return levels, coefs

        lax.fori_loop(0, strip // unroll, turn, (levels, coefs))
        for h in range(2):
            solved[q, :, h * 128:(h + 1) * 128] = solved32[h].astype(BF16)

        def send(d, _):
            piece(q, lax.rem(cable + d, n_cable), d).start()
            return 0

        lax.fori_loop(1, n_cable, send, 0)
        arrived[2 * cable + q] = solved[q, pl.ds(pl.multiple_of(cable * block, block), block), :]

    def await_piece(d, _):
        peer = lax.rem(cable + d, n_cable)
        for q in range(2):
            pltpu.make_async_remote_copy(
                src_ref=solved.at[q, pl.ds(0, block), :], dst_ref=arrived.at[2 * peer + q],
                send_sem=send_sem.at[q, d], recv_sem=recv_sem.at[2 * peer + q],
                device_id=(peer, seg), device_id_type=MESH).wait_recv()
            piece(q, peer, d).wait_send()
        return 0

    lax.fori_loop(1, n_cable, await_piece, 0)

    @pl.when(seg < n_seg - 1)
    def _():
        for copy in halo_copies(0):
            copy.wait_send()

    @pl.when(seg > 0)
    def _():
        for copy in halo_copies(1):
            copy.wait_send()


def relax_and_exchange(frames, tension, stiff):
    n_cable, n_seg = lax.axis_size("cable"), lax.axis_size("seg")
    nodes = frames.shape[0]
    steps = nodes // STRIPS + 2 * SWEEPS
    dma = pltpu.SemaphoreType.DMA
    return pl.pallas_call(
        lambda *refs: relax_kernel(n_cable, n_seg, *refs),
        out_shape=jax.ShapeDtypeStruct((2 * n_cable, nodes // n_cable, SNAP), BF16),
        in_specs=[vmem_spec()] * 3,
        out_specs=vmem_spec(),
        scratch_shapes=[
            VMEM((4, nodes + 2 * EDGE, 128), F32),
            VMEM((2, EDGE, 2 * SNAP), BF16),
            VMEM((2, 2, 128), F32),
            VMEM((2, 24, 128), F32),
            VMEM((2, 2, steps, STRIPS, 128), F32),
            VMEM((2, nodes, 128), F32),
            VMEM((2, nodes, SNAP), BF16),
            dma((4,)), dma((4,)), dma((2, n_cable)), dma((2 * n_cable,)),
        ],
        compiler_params=pltpu.CompilerParams(collective_id=0, has_side_effects=True, vmem_limit_bytes=40 * 2**20),
        name="relax_exchange",
    )(frames, tension, stiff)


def reduce_kernel(n_cable, n_seg, local, total, parts, sums, send1, recv1, send2, recv2, send3, recv3):
    cable, seg = lax.axis_index("cable"), lax.axis_index("seg")
    depth = local.shape[0] // n_cable
    greet(n_cable, n_seg)

    def rows(i):
        return pl.ds(pl.multiple_of(i * depth, depth), depth)

    def scatter(d):
        peer = lax.rem(cable + d, n_cable)
        return pltpu.make_async_remote_copy(
            src_ref=local.at[rows(peer), :], dst_ref=parts.at[cable], send_sem=send1.at[d], recv_sem=recv1.at[cable],
            device_id=(peer, seg), device_id_type=MESH)

    def scattered(d):
        peer = lax.rem(cable + d, n_cable)
        return pltpu.make_async_remote_copy(
            src_ref=local.at[rows(peer), :], dst_ref=parts.at[peer], send_sem=send1.at[d], recv_sem=recv1.at[peer],
            device_id=(peer, seg), device_id_type=MESH)

    def swap(d):
        peer = lax.rem(seg + d, n_seg)
        return pltpu.make_async_remote_copy(
            src_ref=sums.at[seg], dst_ref=sums.at[seg], send_sem=send2.at[d], recv_sem=recv2.at[seg],
            device_id=(cable, peer), device_id_type=MESH)

    def swapped(d):
        peer = lax.rem(seg + d, n_seg)
        return pltpu.make_async_remote_copy(
            src_ref=sums.at[seg], dst_ref=sums.at[peer], send_sem=send2.at[d], recv_sem=recv2.at[peer],
            device_id=(cable, peer), device_id_type=MESH)

    def gather(d):
        peer = lax.rem(cable + d, n_cable)
        return pltpu.make_async_remote_copy(
            src_ref=total.at[rows(cable), :], dst_ref=total.at[rows(cable), :], send_sem=send3.at[d],
            recv_sem=recv3.at[cable], device_id=(peer, seg), device_id_type=MESH)

    def gathered(d):
        peer = lax.rem(cable + d, n_cable)
        return pltpu.make_async_remote_copy(
            src_ref=total.at[rows(peer), :], dst_ref=total.at[rows(peer), :], send_sem=send3.at[d],
            recv_sem=recv3.at[peer], device_id=(peer, seg), device_id_type=MESH)

    def each(first, last, act):
        def turn(d, _):
            act(d)
            return 0
        lax.fori_loop(first, last, turn, 0)

    each(1, n_cable, lambda d: scatter(d).start())
    parts[cable] = local[rows(cable), :]
    each(1, n_cable, lambda d: scattered(d).wait_recv())
    acc = parts[0]
    for i in range(1, n_cable):
        acc = acc + parts[i]
    sums[seg] = acc
    each(1, n_seg, lambda d: swap(d).start())
    each(1, n_seg, lambda d: swapped(d).wait_recv())
    acc = sums[0]
    for i in range(1, n_seg):
        acc = acc + sums[i]
    total[rows(cable), :] = acc
    each(1, n_cable, lambda d: gather(d).start())
    each(1, n_cable, lambda d: gathered(d).wait_recv())
    each(1, n_cable, lambda d: scatter(d).wait_send())
    each(1, n_seg, lambda d: swap(d).wait_send())
    each(1, n_cable, lambda d: gather(d).wait_send())


def all_reduce(local):
    n_cable, n_seg = lax.axis_size("cable"), lax.axis_size("seg")
    rows, cols = local.shape
    depth = rows // n_cable
    dma = pltpu.SemaphoreType.DMA
    return pl.pallas_call(
        lambda *refs: reduce_kernel(n_cable, n_seg, *refs),
        out_shape=jax.ShapeDtypeStruct((rows, cols), F32),
        in_specs=[vmem_spec()],
        out_specs=vmem_spec(),
        scratch_shapes=[
            VMEM((n_cable, depth, cols), F32), VMEM((n_seg, depth, cols), F32),
            dma((n_cable,)), dma((n_cable,)), dma((n_seg,)), dma((n_seg,)), dma((n_cable,)), dma((n_cable,)),
        ],
        compiler_params=pltpu.CompilerParams(collective_id=1, has_side_effects=True, vmem_limit_bytes=40 * 2**20),
        name="gram_reduce",
    )(local)


def gram_kernel(owner, basis, singular, arrived, gram, ordered, by_position, staged):
    positions, block = arrived.shape[0], arrived.shape[1]
    for p in range(positions):
        rows = arrived[owner[p]].astype(F32)
        for h in range(2):
            by_position[h, p * block:(p + 1) * block, :] = rows[:, h * 128:(h + 1) * 128]

    def spread(n, _):
        for h in range(2):
            part = by_position[h, pl.ds(n, positions, stride=block), :]
            ordered[pl.ds(pl.multiple_of(n * positions, positions), positions), h * 128:(h + 1) * 128] = (
                part.astype(BF16))
        return 0

    lax.fori_loop(0, block, spread, 0)
    scaled = (basis[...].astype(F32) * singular[...]).astype(BF16)
    staged[...] = scaled
    snaps = ordered[...]
    gram[0:K, :] = tn(scaled, scaled)
    gram[K:2 * K, :] = tn(snaps, scaled)
    gram[2 * K:, :] = tn(snaps, snaps)


def gram_blocks(owner_map, basis, singular, arrived):
    rows = basis.shape[0]
    return pl.pallas_call(
        gram_kernel,
        out_shape=[jax.ShapeDtypeStruct((3 * K, K), F32), jax.ShapeDtypeStruct((rows, SNAP), BF16)],
        in_specs=[pl.BlockSpec(memory_space=pltpu.SMEM)] + [vmem_spec()] * 3,
        out_specs=[vmem_spec()] * 2,
        scratch_shapes=[VMEM((2, rows, 128), F32), VMEM((rows, K), BF16)],
        compiler_params=pltpu.CompilerParams(vmem_limit_bytes=40 * 2**20),
        name="gram_blocks",
    )(owner_map, basis, singular, arrived)


def factor_128(a, upper, inverse):
    size, n = 8, 16
    full = (size, 128)
    rows = lax.broadcasted_iota(jnp.int32, full, 0)
    lanes = lax.broadcasted_iota(jnp.int32, full, 1)
    a = list(a)
    q = [jnp.where(lanes == rows + size * t, 1.0, 0.0) for t in range(n)]
    for kb in range(n):
        at = size * kb
        r = [jnp.broadcast_to(a[kb][k:k + 1, :], full) for k in range(size)]
        s = [jnp.broadcast_to(q[kb][k:k + 1, :], full) for k in range(size)]
        col = {t: [jnp.broadcast_to(a[t][:, at + k:at + k + 1], full) for k in range(size)]
               for t in range(kb + 1, n)}
        e, m, pivot = {}, {}, []
        for j in range(size):
            own = jnp.broadcast_to(a[kb][:, at + j:at + j + 1], full)
            for i in range(j, size):
                e[i, j] = jnp.broadcast_to(own[i:i + 1, :], full)
        for k in range(size):
            pivot.append(1.0 / e[k, k])
            for i in range(k + 1, size):
                m[i, k] = e[i, k] * pivot[k]
            for i in range(k + 1, size):
                for j in range(k + 1, i + 1):
                    e[i, j] = e[i, j] - m[i, k] * e[j, k]
                r[i] = r[i] - m[i, k] * r[k]
                s[i] = s[i] - m[i, k] * s[k]
        z = [r[k] * pivot[k] for k in range(size)]
        zs = [s[k] * pivot[k] for k in range(size)]
        for k in reversed(range(size)):
            for j in range(k):
                z[j] = z[j] - m[k, j] * z[k]
                zs[j] = zs[j] - m[k, j] * zs[k]
        for t in range(kb + 1, n):
            for k in range(size):
                a[t] = a[t] - col[t][k] * z[k]
                q[t] = q[t] - col[t][k] * zs[k]
        ut, wt = jnp.zeros(full, F32), jnp.zeros(full, F32)
        for k in range(size):
            root = lax.rsqrt(e[k, k])
            ut = jnp.where(rows == k, r[k] * root, ut)
            wt = jnp.where(rows == k, s[k] * root, wt)
        upper[at:at + size, :] = jnp.where(lanes >= rows + at, ut, 0.0)
        inverse[at:at + size, :] = jnp.where(lanes <= rows + at, wt, 0.0)


def factor_256(a, upper, inverse):
    h = 128
    factor_128([a[8 * t:8 * t + 8, :h] for t in range(16)], upper.at[:h, :h], inverse.at[:h, :h])
    w1 = inverse[:h, :h]
    low = nt(a[h:, :h], w1, HI)
    upper[:h, h:] = low.T
    upper[h:, :h] = jnp.zeros((h, h), F32)
    inverse[:h, h:] = jnp.zeros((h, h), F32)
    a[h:, h:] = a[h:, h:] - nt(low, low, HI)
    t = nn(low, w1, HI)
    factor_128([a[h + 8 * t:h + 8 * t + 8, h:] for t in range(16)], upper.at[h:, h:], inverse.at[h:, h:])
    inverse[h:, :h] = -nn(inverse[h:, h:], t, HI)


def factor_kernel(rows_all, gram, basis, singular, snaps, factor, new_basis, a, inv1, inv2):
    scale = 1.0 / rows_all
    a[...] = gram[0:K, :] * scale
    factor_256(a, factor.at[:K, :K], inv1)
    w1 = inv1[...]
    low = nt(gram[K:2 * K, :] * scale, w1, HI)
    factor[:K, K:] = low.T
    factor[K:, :K] = jnp.zeros((K, K), F32)
    a[...] = gram[2 * K:, :] * scale - nt(low, low, HI)
    t = nn(low, w1, HI)
    factor_256(a, factor.at[K:, K:], inv2)
    w2 = inv2[...]
    cross = (-nn(w2, t, HI)).astype(BF16)
    w1b, w2b = w1.astype(BF16), w2.astype(BF16)
    scaled = (basis[...].astype(F32) * singular[...]).astype(BF16)
    new_basis[:, :K] = nt(scaled, w1b).astype(BF16)
    new_basis[:, K:] = (nt(scaled, cross) + nt(snaps[...], w2b)).astype(BF16)


def factor_and_rotate(rows_all, gram, basis, singular, snaps):
    rows, width = basis.shape[0], 2 * K
    return pl.pallas_call(
        lambda *refs: factor_kernel(rows_all, *refs),
        out_shape=[jax.ShapeDtypeStruct((width, width), F32), jax.ShapeDtypeStruct((rows, width), BF16)],
        in_specs=[vmem_spec()] * 4,
        out_specs=[vmem_spec()] * 2,
        scratch_shapes=[VMEM((K, K), F32)] * 3,
        compiler_params=pltpu.CompilerParams(vmem_limit_bytes=40 * 2**20),
        name="factor_rotate",
    )(gram, basis, singular, snaps)


def body(frames, tension, step_index, owner_map, old_basis, singular):
    stiff = (DRAG_RATE * (1.0 + step_index.astype(F32)))[None, :]
    nodes = frames.shape[0]
    arrived = relax_and_exchange(frames.reshape(nodes, 2 * SNAP), tension.T, stiff)
    basis = old_basis.reshape(-1, K)
    gain = singular[None, :]
    local, snaps = gram_blocks(owner_map, basis, gain, arrived)
    gram = all_reduce(local)
    rows_all = basis.shape[0] * lax.axis_size("cable") * lax.axis_size("seg")
    factor, rotated = factor_and_rotate(rows_all, gram, basis, gain, snaps)
    return factor, rotated.reshape(old_basis.shape[:3] + (2 * K,))


def solution(mesh):
    return jax.shard_map(
        body,
        mesh=mesh,
        in_specs=(P("seg", "cable", None), P("seg", "cable"), P(), P(), P("seg", "cable", None, None), P()),
        out_specs=(P(), P("seg", "cable", None, None)),
        check_vma=False,
    )
```

```python
import jax
import jax.numpy as jnp
from jax import lax
from jax.experimental import pallas as pl
from jax.experimental.pallas import tpu as pltpu
from jax.sharding import PartitionSpec as P

K = 256
SNAP = 256
SWEEPS = 6
DRAG_RATE = 0.1
STRIPS = 8
EDGE = 16
MESH = pl.DeviceIdType.MESH
HI = lax.Precision.HIGHEST
VMEM = pltpu.VMEM
F32 = jnp.float32
BF16 = jnp.bfloat16


def vmem_spec():
    return pl.BlockSpec(memory_space=pltpu.VMEM)


def nt(a, b, precision=None):
    return lax.dot_general(a, b, (((1,), (1,)), ((), ())), precision=precision, preferred_element_type=F32)


def nn(a, b, precision=None):
    return lax.dot_general(a, b, (((1,), (0,)), ((), ())), precision=precision, preferred_element_type=F32)


def tn(a, b, precision=None):
    return lax.dot_general(a, b, (((0,), (0,)), ((), ())), precision=precision, preferred_element_type=F32)


def place():
    cable, seg = lax.axis_index("cable"), lax.axis_index("seg")
    return cable, seg, cable // 8, lax.rem(cable // 4, 2), lax.rem(cable, 4), seg // 2, lax.rem(seg, 2)


N_CABLE = 32
N_SEG = 4
PLANE = 16


def each(first, last, act):
    def turn(d, _):
        act(d)
        return 0
    lax.fori_loop(first, last, turn, 0)


def greet():
    cable, seg, x, y_lo, z, y_hi, core = place()
    barrier = pltpu.get_barrier_semaphore()

    def hail(device):
        pl.semaphore_signal(barrier, inc=1, device_id=device, device_id_type=MESH)

    each(1, N_CABLE, lambda d: hail((lax.rem(cable + d, N_CABLE), seg)))
    each(1, N_SEG, lambda d: hail((cable, lax.rem(seg + d, N_SEG))))
    hail((x * 8 + (1 - y_lo) * 4 + z, (1 - y_hi) * 2 + core))
    return lambda: pl.semaphore_wait(barrier, N_CABLE + N_SEG - 1)


class Reduce:
    def __init__(self, local, total, half, parts, lines, sems):
        self.local, self.total, self.half, self.parts, self.lines = local, total, half, parts, lines
        self.send, self.recv = sems
        self.rows = local.shape[0]
        self.depth = self.rows // 2 // PLANE
        self.cable, self.seg, self.x, self.y_lo, self.z, self.y_hi, self.core = place()
        self.spot = self.x * 4 + self.z
        self.y = self.y_hi * 2 + self.y_lo
        self.sister = (self.cable, self.y_hi * 2 + 1 - self.core)

    def copy(self, src, dst, slot, landing, device):
        return pltpu.make_async_remote_copy(
            src_ref=src, dst_ref=dst, send_sem=self.send.at[slot], recv_sem=self.recv.at[landing],
            device_id=device, device_id_type=MESH)

    def plane(self, d):
        spot = lax.rem(self.spot + d, PLANE)
        return spot, ((spot // 4) * 8 + self.y_lo * 4 + lax.rem(spot, 4), self.seg)

    def line(self, d):
        y = lax.rem(self.y + d, 4)
        return y, (self.x * 8 + lax.rem(y, 2) * 4 + self.z, (y // 2) * 2 + self.core)

    def part(self, spot):
        at = self.core * (self.rows // 2) + spot * self.depth
        return pl.ds(pl.multiple_of(at, self.depth), self.depth)

    def own_half(self):
        return pl.ds(pl.multiple_of(self.core * (self.rows // 2), self.rows // 2), self.rows // 2)

    def other_half(self):
        return pl.ds(pl.multiple_of((1 - self.core) * (self.rows // 2), self.rows // 2), self.rows // 2)

    def c1(self):
        return self.copy(self.local.at[self.other_half(), :], self.half, 0, 0, self.sister)

    def p1(self, d, mine):
        spot, device = self.plane(d)
        return self.copy(self.half.at[pl.ds(pl.multiple_of(spot * self.depth, self.depth), self.depth), :],
                         self.parts.at[self.spot if mine else spot], 16 + d, 16 + (self.spot if mine else spot), device)

    def l1(self, d, mine):
        y, device = self.line(d)
        return self.copy(self.lines.at[self.y], self.lines.at[self.y if mine else y], 4 + d,
                         4 + (self.y if mine else y), device)

    def p2(self, d, mine):
        spot, device = self.plane(d)
        rows = self.part(self.spot if mine else spot)
        return self.copy(self.total.at[rows, :], self.total.at[rows, :], 32 + d,
                         32 + (self.spot if mine else spot), device)

    def c2(self, mine):
        rows = self.own_half() if mine else self.other_half()
        return self.copy(self.total.at[rows, :], self.total.at[rows, :], 1, 1, self.sister)

    def s0(self):
        self.c1().start()

    def s1(self):
        self.c1().wait_recv()
        self.half[...] = self.half[...] + self.local[self.own_half(), :]
        each(1, PLANE, lambda d: self.p1(d, True).start())
        self.parts[self.spot] = self.half[pl.ds(pl.multiple_of(self.spot * self.depth, self.depth), self.depth), :]

    def s2(self):
        each(1, PLANE, lambda d: self.p1(d, False).wait_recv())
        acc = self.parts[0]
        for i in range(1, PLANE):
            acc = acc + self.parts[i]
        self.lines[self.y] = acc
        each(1, 4, lambda d: self.l1(d, True).start())

    def s3(self):
        each(1, 4, lambda d: self.l1(d, False).wait_recv())
        acc = (self.lines[0] + self.lines[1]) + (self.lines[2] + self.lines[3])
        self.total[self.part(self.spot), :] = acc
        each(1, PLANE, lambda d: self.p2(d, True).start())

    def s4(self):
        each(1, PLANE, lambda d: self.p2(d, False).wait_recv())
        self.c2(True).start()

    def s5(self):
        self.c2(False).wait_recv()

    def drain(self):
        self.c1().wait_send()
        each(1, PLANE, lambda d: self.p1(d, True).wait_send())
        each(1, 4, lambda d: self.l1(d, True).wait_send())
        each(1, PLANE, lambda d: self.p2(d, True).wait_send())
        self.c2(True).wait_send()


def reduce_scratch(rows):
    depth = rows // 2 // PLANE
    return [VMEM((rows // 2, K), F32), VMEM((PLANE, depth, K), F32), VMEM((4, depth, K), F32),
            pltpu.SemaphoreType.DMA((48,)), pltpu.SemaphoreType.DMA((48,))]


def factor_128(a, upper, inverse):
    size, n = 8, 16
    rows = lax.broadcasted_iota(jnp.int32, (size, 128), 0)
    lanes = lax.broadcasted_iota(jnp.int32, (size, 128), 1)
    depth = lax.broadcasted_iota(jnp.int32, (n, size, 128), 0)
    q = jnp.where(lanes[None] == rows[None] + size * depth, 1.0, 0.0).astype(F32)
    for kb in range(n):
        at = size * kb
        own, own_q = a[0], q[0]
        a, q = a[1:], q[1:]
        stack = lambda x: jnp.broadcast_to(x[:, None, :], (size, size, 128))
        rest = n - 1 - kb
        r, s = stack(own), stack(own_q)
        cols = [stack(jnp.broadcast_to(own[:, at + j:at + j + 1], (size, 128))) for j in range(size)]
        side = [jnp.broadcast_to(a[:, :, at + k:at + k + 1], (rest, size, 128)) for k in range(size)] if rest else []
        m, rr, ss, pivot, root = [], [], [], [], []
        ut, wt = jnp.zeros((size, 128), F32), jnp.zeros((size, 128), F32)
        for k in range(size):
            d = cols[k][0]
            pivot.append(1.0 / d)
            rr.append(r[0]); ss.append(s[0])
            if k < size - 1:
                below = cols[k][1:]
                mk = below * pivot[k][None]
                m.append(mk)
                for j in range(k + 1, size):
                    cols[j] = cols[j][1:] if j == k + 1 and False else cols[j][1:] - mk * below[j - k - 1][None]
                r = r[1:] - mk * r[0][None]
                s = s[1:] - mk * s[0][None]
            rt = lax.rsqrt(d)
            ut = jnp.where(rows == k, rr[k] * rt, ut)
            wt = jnp.where(rows == k, ss[k] * rt, wt)
        z, zs = [None] * size, [None] * size
        for k in reversed(range(size)):
            zk, zsk = rr[k] * pivot[k], ss[k] * pivot[k]
            for j in range(k + 1, size):
                zk = zk - m[k][j - k - 1] * z[j]
                zsk = zsk - m[k][j - k - 1] * zs[j]
            z[k], zs[k] = zk, zsk
        if rest:
            for k in range(size):
                a = a - side[k] * z[k][None]
                q = q - side[k] * zs[k][None]
        upper[at:at + size, :] = jnp.where(lanes >= rows + at, ut, 0.0)
        inverse[at:at + size, :] = jnp.where(lanes <= rows + at, wt, 0.0)


def factor_256(a, upper, inverse, between=None):
    h = 128
    factor_128(a[:h, :h].reshape(16, 8, h), upper.at[:h, :h], inverse.at[:h, :h])
    if between is not None:
        between[0]()
    w1 = inverse[:h, :h]
    low = nt(a[h:, :h], w1, HI)
    upper[:h, h:] = low.T
    upper[h:, :h] = jnp.zeros((h, h), F32)
    inverse[:h, h:] = jnp.zeros((h, h), F32)
    a[h:, h:] = a[h:, h:] - nt(low, low, HI)
    t = nn(low, w1, HI)
    if between is not None:
        between[1]()
    factor_128(a[h:, h:].reshape(16, 8, h), upper.at[h:, h:], inverse.at[h:, h:])
    if between is not None:
        between[2]()
    inverse[h:, :h] = -nn(inverse[h:, h:], t, HI)


class Halo:
    def __init__(self, frames, tension, halo, tens_halo, send, recv):
        self.refs = frames, tension, halo, tens_halo, send, recv
        self.cable, self.seg = lax.axis_index("cable"), lax.axis_index("seg")

    def copies(self, side):
        frames, tension, halo, tens_halo, send, recv = self.refs
        nodes = frames.shape[0]
        peer = self.seg + 1 if side == 0 else self.seg - 1
        return [
            pltpu.make_async_remote_copy(
                src_ref=frames.at[pl.ds(nodes - EDGE if side == 0 else 0, EDGE), :], dst_ref=halo.at[side],
                send_sem=send.at[side], recv_sem=recv.at[side],
                device_id=(self.cable, peer), device_id_type=MESH),
            pltpu.make_async_remote_copy(
                src_ref=tension.at[:, pl.ds(nodes - 128 if side == 0 else 0, 128)], dst_ref=tens_halo.at[side],
                send_sem=send.at[2 + side], recv_sem=recv.at[2 + side],
                device_id=(self.cable, peer), device_id_type=MESH),
        ]

    def guarded(self, sends, act):
        for side in range(2):
            has_right, has_left = self.seg < N_SEG - 1, self.seg > 0
            here = (has_right, has_left) if sends else (has_left, has_right)

            @pl.when(here[side])
            def _():
                for copy in self.copies(side):
                    act(copy)

    def start(self):
        self.guarded(True, lambda copy: copy.start())

    def wait_recv(self):
        self.guarded(False, lambda copy: copy.wait_recv())

    def wait_send(self):
        self.guarded(True, lambda copy: copy.wait_send())

    def zero_ends(self):
        halo, tens_halo = self.refs[2:4]

        @pl.when(self.seg == 0)
        def _():
            halo[0] = jnp.zeros_like(halo[0])
            tens_halo[0] = jnp.zeros_like(tens_halo[0])

        @pl.when(self.seg == N_SEG - 1)
        def _():
            halo[1] = jnp.zeros_like(halo[1])
            tens_halo[1] = jnp.zeros_like(tens_halo[1])


def make_weights(seg, tens_halo, tens_rows, weights, steps):
    reach = SWEEPS
    full = (STRIPS, 128)
    sub = lax.broadcasted_iota(jnp.int32, full, 0)
    lane = lax.broadcasted_iota(jnp.int32, full, 1)
    low_out = jnp.logical_and(sub == 0, seg == 0)
    high_out = jnp.logical_and(sub == STRIPS - 1, seg == N_SEG - 1)
    for q in range(2):
        tens_rows[q, 7:8, :] = tens_halo[0, q:q + 1, :]
        tens_rows[q, 16:17, :] = tens_halo[1, q:q + 1, :]
        before, here, after = (tens_rows[q, 7 + i:15 + i, :] for i in range(3))

        def next_lane(x, y):
            return jnp.where(lane == 127, pltpu.roll(y, 127, 1), pltpu.roll(x, 127, 1))

        def prev_lane(x, y):
            return jnp.where(lane == 0, pltpu.roll(x, 1, 1), pltpu.roll(y, 1, 1))

        right = [0.5 * (before + next_lane(before, here)), 0.5 * (here + next_lane(here, after)),
                 0.5 * (after + next_lane(after, after))]
        left = [prev_lane(before, right[0]), prev_lane(right[0], right[1]), prev_lane(right[1], right[2])]
        for kind, rows in enumerate((left, right)):
            rows[0] = jnp.where(low_out, 0.0, rows[0])
            rows[2] = jnp.where(high_out, 0.0, rows[2])
            for step in range(steps):
                part, at = divmod(128 + step - reach, 128)
                weights[q, kind, step] = jnp.broadcast_to(rows[part][:, at:at + 1], full)


def relax(q, scale, padded, weights, solved32, solved, strip, block):
    reach = SWEEPS
    full = (STRIPS, 128)

    def advance(step, levels, coefs):
        lw, rw = weights[q, 0, step], weights[q, 1, step]
        total = lw + rw
        out = []
        for h in range(2):
            value = padded[2 * q + h, pl.ds(EDGE - reach + step, STRIPS, stride=strip), :]
            inv = 1.0 / (1.0 + scale[h] * total)
            si = scale[h] * inv
            coefs[h].append((si * lw, si * rw, value * inv))
            levels[h][0].append(value)
            for k in range(1, SWEEPS + 1):
                below, above, own = coefs[h][-1 - k]
                value = own + (above * levels[h][k - 1][-1] + below * levels[h][k - 1][-3])
                levels[h][k].append(value)
            coefs[h][:] = coefs[h][-(SWEEPS + 1):]
            for k in range(SWEEPS + 1):
                levels[h][k][:] = levels[h][k][-2:] if k < SWEEPS else levels[h][k][-1:]
            out.append(levels[h][SWEEPS][-1])
        return out

    zero = jnp.zeros(full, F32)
    levels = [[[zero, zero] for _ in range(SWEEPS)] + [[zero]] for _ in range(2)]
    coefs = [[(zero, zero, zero)] * (SWEEPS + 1) for _ in range(2)]
    for step in range(2 * reach):
        advance(step, levels, coefs)
    unroll = 8

    def turn(i, carry):
        levels, coefs = carry
        levels = [[list(x) for x in lv] for lv in levels]
        coefs = [[tuple(x) for x in cf] for cf in coefs]
        for u in range(unroll):
            row = i * unroll + u
            out = advance(2 * reach + row, levels, coefs)
            for h in range(2):
                solved32[h, pl.ds(row, STRIPS, stride=strip), :] = out[h]
        return levels, coefs

    lax.fori_loop(0, strip // unroll, turn, (levels, coefs))

    def pack(b, _):
        rows = pl.ds(pl.multiple_of(b * block, block), block)
        for h in range(2):
            solved[b, q * block:(q + 1) * block, h * 128:(h + 1) * 128] = solved32[h, rows, :].astype(BF16)
        return 0

    lax.fori_loop(0, N_CABLE, pack, 0)


def main_kernel(rows_all, frames, tension, step_index, owner, basis, singular,
                upper, inverse, rest, snaps,
                padded, halo, tens_halo, tens_rows, weights, solved32, solved, scaled, rows32, basis_out, basis_in,
                snaps_in, a, local1, total1, local2, half1, parts1, lines1, send1, recv1,
                half2, parts2, lines2, send2, recv2, halo_send, halo_recv, b_send, b_recv, s_send, s_recv):
    cable, seg = lax.axis_index("cable"), lax.axis_index("seg")
    nodes = frames.shape[0]
    strip = nodes // STRIPS
    block = nodes // N_CABLE
    positions = 2 * N_CABLE
    met = greet()

    pick = (lax.broadcasted_iota(jnp.int32, (positions, positions), 0) == owner[...]).astype(F32)
    pick_bf = pick.astype(BF16)
    unpick_bf = pick.T.astype(BF16)
    scaled[...] = (basis[...].astype(F32) * singular[...]).astype(BF16)

    def by_streamer(n, _):
        rows = scaled[pl.ds(pl.multiple_of(n * positions, positions), positions), :]
        moved = nn(pick_bf, rows)
        for h in range(2):
            rows32[h, pl.ds(n, positions, stride=block), :] = moved[:, h * 128:(h + 1) * 128]
        return 0

    lax.fori_loop(0, block, by_streamer, 0, unroll=4)
    for h in range(2):
        basis_out[:, :, h * 128:(h + 1) * 128] = rows32[h].astype(BF16).reshape(N_CABLE, 2 * block, 128)

    met()
    edges = Halo(frames, tension, halo, tens_halo, halo_send, halo_recv)
    edges.start()

    def exchange(d, out, into, send, recv, mine):
        peer = lax.rem(cable + d, N_CABLE)
        return pltpu.make_async_remote_copy(
            src_ref=out.at[peer], dst_ref=into.at[cable if mine else peer], send_sem=send.at[d],
            recv_sem=recv.at[cable if mine else peer], device_id=(peer, seg), device_id_type=MESH)

    each(1, N_CABLE, lambda d: exchange(d, basis_out, basis_in, b_send, b_recv, True).start())
    basis_in[cable] = basis_out[cable]

    local1[...] = tn(scaled[...], scaled[...])
    first = Reduce(local1, total1, half1, parts1, lines1, (send1, recv1))
    second = Reduce(local2, rest, half2, parts2, lines2, (send2, recv2))
    first.s0()
    for tile in range(4):
        padded[tile, EDGE:EDGE + nodes, :] = frames[:, tile * 128:(tile + 1) * 128].astype(F32)
    for q in range(2):
        for s in range(STRIPS):
            tens_rows[q, 8 + s:9 + s, :] = tension[q:q + 1, s * strip:(s + 1) * strip]
    edges.zero_ends()
    first.s1()
    edges.wait_recv()
    for tile in range(4):
        cols = slice(tile * 128, (tile + 1) * 128)
        padded[tile, 0:EDGE, :] = halo[0, :, cols].astype(F32)
        padded[tile, EDGE + nodes:, :] = halo[1, :, cols].astype(F32)
    make_weights(seg, tens_halo, tens_rows, weights, strip + 2 * SWEEPS)
    stiff = DRAG_RATE * (1.0 + step_index[...].astype(F32))
    scale = [jnp.broadcast_to(stiff[:, h * 128:(h + 1) * 128], (STRIPS, 128)) for h in range(2)]
    relax(0, scale, padded, weights, solved32, solved, strip, block)
    first.s2()
    relax(1, scale, padded, weights, solved32, solved, strip, block)
    first.s3()
    flat = solved[...].reshape(2 * nodes, SNAP)
    local2[K:, :] = tn(flat, flat)
    first.s4()
    first.s5()
    a[...] = total1[...] * (1.0 / rows_all)

    def cross():
        each(1, N_CABLE, lambda d: exchange(d, basis_out, basis_in, b_send, b_recv, False).wait_recv())
        local2[:K, :] = tn(solved[...].reshape(2 * nodes, SNAP), basis_in[...].reshape(2 * nodes, K))
        second.s0()

    def scatter():
        second.s1()
        each(1, N_CABLE, lambda d: exchange(d, solved, snaps_in, s_send, s_recv, True).start())
        snaps_in[cable] = solved[cable]

    factor_256(a, upper, inverse, (cross, scatter, second.s2))
    second.s3()
    each(1, N_CABLE, lambda d: exchange(d, solved, snaps_in, s_send, s_recv, False).wait_recv())

    for h in range(2):
        rows32[h] = snaps_in[:, :, h * 128:(h + 1) * 128].astype(F32).reshape(positions * block, 128)

    def by_position(n, _):
        rows = jnp.concatenate([rows32[h, pl.ds(n, positions, stride=block), :] for h in range(2)], axis=1)
        snaps[pl.ds(pl.multiple_of(n * positions, positions), positions), :] = (
            nn(unpick_bf, rows.astype(BF16)).astype(BF16))
        return 0

    lax.fori_loop(0, block, by_position, 0, unroll=4)
    second.s4()
    second.s5()

    first.drain()
    second.drain()
    edges.wait_send()
    each(1, N_CABLE, lambda d: exchange(d, basis_out, basis_in, b_send, b_recv, True).wait_send())
    each(1, N_CABLE, lambda d: exchange(d, solved, snaps_in, s_send, s_recv, True).wait_send())


def exchange_and_reduce(rows_all, frames, tension, step_index, owner_map, basis, singular):
    nodes = frames.shape[0]
    rows = basis.shape[0]
    block = nodes // N_CABLE
    steps = nodes // STRIPS + 2 * SWEEPS
    dma = pltpu.SemaphoreType.DMA
    square = jax.ShapeDtypeStruct((K, K), F32)
    return pl.pallas_call(
        lambda *refs: main_kernel(rows_all, *refs),
        out_shape=[square, square, jax.ShapeDtypeStruct((2 * K, K), F32), jax.ShapeDtypeStruct((rows, SNAP), BF16)],
        in_specs=[vmem_spec()] * 6,
        out_specs=[vmem_spec()] * 4,
        scratch_shapes=[
            VMEM((4, nodes + 2 * EDGE, 128), F32),
            VMEM((2, EDGE, 2 * SNAP), BF16),
            VMEM((2, 2, 128), F32),
            VMEM((2, 24, 128), F32),
            VMEM((2, 2, steps, STRIPS, 128), F32),
            VMEM((2, nodes, 128), F32),
            VMEM((N_CABLE, 2 * block, SNAP), BF16),
            VMEM((rows, K), BF16),
            VMEM((2, rows, 128), F32),
            VMEM((N_CABLE, 2 * block, K), BF16),
            VMEM((N_CABLE, 2 * block, K), BF16),
            VMEM((N_CABLE, 2 * block, SNAP), BF16),
            VMEM((K, K), F32),
            VMEM((K, K), F32),
            VMEM((K, K), F32),
            VMEM((2 * K, K), F32),
            *reduce_scratch(K), *reduce_scratch(2 * K),
            dma((4,)), dma((4,)), *[dma((N_CABLE,))] * 4,
        ],
        compiler_params=pltpu.CompilerParams(collective_id=0, has_side_effects=True, vmem_limit_bytes=48 * 2**20),
        name="relax_exchange_reduce",
    )(frames, tension, step_index, owner_map, basis, singular)


def rotate_kernel(rows_all, upper1, w1_ref, rest, basis, singular, snaps, factor, new_basis, a, inv2):
    scale = 1.0 / rows_all
    w1 = w1_ref[...]
    factor[:K, :K] = upper1[...]
    low = nt(rest[:K, :] * scale, w1, HI)
    factor[:K, K:] = low.T
    factor[K:, :K] = jnp.zeros((K, K), F32)
    a[...] = rest[K:, :] * scale - nt(low, low, HI)
    t = nn(low, w1, HI)
    factor_256(a, factor.at[K:, K:], inv2)
    w2 = inv2[...]
    cross = (-nn(w2, t, HI)).astype(BF16)
    w1b, w2b = w1.astype(BF16), w2.astype(BF16)
    scaled = (basis[...].astype(F32) * singular[...]).astype(BF16)
    new_basis[:, :K] = nt(scaled, w1b).astype(BF16)
    new_basis[:, K:] = (nt(scaled, cross) + nt(snaps[...], w2b)).astype(BF16)


def factor_and_rotate(rows_all, upper, inverse, rest, basis, singular, snaps):
    rows, width = basis.shape[0], 2 * K
    return pl.pallas_call(
        lambda *refs: rotate_kernel(rows_all, *refs),
        out_shape=[jax.ShapeDtypeStruct((width, width), F32), jax.ShapeDtypeStruct((rows, width), BF16)],
        in_specs=[vmem_spec()] * 6,
        out_specs=[vmem_spec()] * 2,
        scratch_shapes=[VMEM((K, K), F32)] * 2,
        compiler_params=pltpu.CompilerParams(vmem_limit_bytes=40 * 2**20),
        name="factor_rotate",
    )(upper, inverse, rest, basis, singular, snaps)


def body(frames, tension, step_index, owner_map, old_basis, singular):
    nodes = frames.shape[0]
    basis = old_basis.reshape(-1, K)
    gain = singular[None, :]
    rows_all = basis.shape[0] * lax.axis_size("cable") * lax.axis_size("seg")
    upper, inverse, rest, snaps = exchange_and_reduce(
        rows_all, frames.reshape(nodes, 2 * SNAP), tension.T, step_index[None, :], owner_map[None, :], basis, gain)
    factor, rotated = factor_and_rotate(rows_all, upper, inverse, rest, basis, gain, snaps)
    return factor, rotated.reshape(old_basis.shape[:3] + (2 * K,))


def solution(mesh):
    return jax.shard_map(
        body,
        mesh=mesh,
        in_specs=(P("seg", "cable", None), P("seg", "cable"), P(), P(), P("seg", "cable", None, None), P()),
        out_specs=(P(), P("seg", "cable", None, None)),
        check_vma=False,
    )
```

```python
import jax
import jax.numpy as jnp
from jax import lax
from jax.experimental import pallas as pl
from jax.experimental.pallas import tpu as pltpu
from jax.sharding import PartitionSpec as P

K = 256
SNAP = 256
SWEEPS = 6
DRAG_RATE = 0.1
STRIPS = 8
EDGE = 16
MESH = pl.DeviceIdType.MESH
HI = lax.Precision.HIGHEST
VMEM = pltpu.VMEM
F32 = jnp.float32
BF16 = jnp.bfloat16


def vmem_spec():
    return pl.BlockSpec(memory_space=pltpu.VMEM)


def nt(a, b, precision=None):
    return lax.dot_general(a, b, (((1,), (1,)), ((), ())), precision=precision, preferred_element_type=F32)


def nn(a, b, precision=None):
    return lax.dot_general(a, b, (((1,), (0,)), ((), ())), precision=precision, preferred_element_type=F32)


def tn(a, b, precision=None):
    return lax.dot_general(a, b, (((0,), (0,)), ((), ())), precision=precision, preferred_element_type=F32)


def place():
    cable, seg = lax.axis_index("cable"), lax.axis_index("seg")
    return cable, seg, cable // 8, lax.rem(cable // 4, 2), lax.rem(cable, 4), seg // 2, lax.rem(seg, 2)


N_CABLE = 32
N_SEG = 4
PLANE = 16


def each(first, last, act):
    def turn(d, _):
        act(d)
        return 0
    lax.fori_loop(first, last, turn, 0)


def greet():
    cable, seg, x, y_lo, z, y_hi, core = place()
    barrier = pltpu.get_barrier_semaphore()

    def hail(device):
        pl.semaphore_signal(barrier, inc=1, device_id=device, device_id_type=MESH)

    each(1, N_CABLE, lambda d: hail((lax.rem(cable + d, N_CABLE), seg)))
    each(1, N_SEG, lambda d: hail((cable, lax.rem(seg + d, N_SEG))))
    hail((x * 8 + (1 - y_lo) * 4 + z, (1 - y_hi) * 2 + core))
    return lambda: pl.semaphore_wait(barrier, N_CABLE + N_SEG - 1)


class Reduce:
    def __init__(self, local, total, half, parts, lines, sems):
        self.local, self.total, self.half, self.parts, self.lines = local, total, half, parts, lines
        self.send, self.recv = sems
        self.rows = local.shape[0]
        self.depth = self.rows // 2 // PLANE
        self.cable, self.seg, self.x, self.y_lo, self.z, self.y_hi, self.core = place()
        self.spot = self.x * 4 + self.z
        self.y = self.y_hi * 2 + self.y_lo
        self.sister = (self.cable, self.y_hi * 2 + 1 - self.core)

    def copy(self, src, dst, slot, landing, device):
        return pltpu.make_async_remote_copy(
            src_ref=src, dst_ref=dst, send_sem=self.send.at[slot], recv_sem=self.recv.at[landing],
            device_id=device, device_id_type=MESH)

    def plane(self, d):
        spot = lax.rem(self.spot + d, PLANE)
        return spot, ((spot // 4) * 8 + self.y_lo * 4 + lax.rem(spot, 4), self.seg)

    def line(self, d):
        y = lax.rem(self.y + d, 4)
        return y, (self.x * 8 + lax.rem(y, 2) * 4 + self.z, (y // 2) * 2 + self.core)

    def part(self, spot):
        at = self.core * (self.rows // 2) + spot * self.depth
        return pl.ds(pl.multiple_of(at, self.depth), self.depth)

    def own_half(self):
        return pl.ds(pl.multiple_of(self.core * (self.rows // 2), self.rows // 2), self.rows // 2)

    def other_half(self):
        return pl.ds(pl.multiple_of((1 - self.core) * (self.rows // 2), self.rows // 2), self.rows // 2)

    def c1(self):
        return self.copy(self.local.at[self.other_half(), :], self.half, 0, 0, self.sister)

    def p1(self, d, mine):
        spot, device = self.plane(d)
        return self.copy(self.half.at[pl.ds(pl.multiple_of(spot * self.depth, self.depth), self.depth), :],
                         self.parts.at[self.spot if mine else spot], 16 + d, 16 + (self.spot if mine else spot), device)

    def l1(self, d, mine):
        y, device = self.line(d)
        return self.copy(self.lines.at[self.y], self.lines.at[self.y if mine else y], 4 + d,
                         4 + (self.y if mine else y), device)

    def p2(self, d, mine):
        spot, device = self.plane(d)
        rows = self.part(self.spot if mine else spot)
        return self.copy(self.total.at[rows, :], self.total.at[rows, :], 32 + d,
                         32 + (self.spot if mine else spot), device)

    def c2(self, mine):
        rows = self.own_half() if mine else self.other_half()
        return self.copy(self.total.at[rows, :], self.total.at[rows, :], 1, 1, self.sister)

    def s0(self):
        self.c1().start()

    def s1(self):
        self.c1().wait_recv()
        self.half[...] = self.half[...] + self.local[self.own_half(), :]
        each(1, PLANE, lambda d: self.p1(d, True).start())
        self.parts[self.spot] = self.half[pl.ds(pl.multiple_of(self.spot * self.depth, self.depth), self.depth), :]

    def s2(self):
        each(1, PLANE, lambda d: self.p1(d, False).wait_recv())
        acc = self.parts[0]
        for i in range(1, PLANE):
            acc = acc + self.parts[i]
        self.lines[self.y] = acc
        each(1, 4, lambda d: self.l1(d, True).start())

    def s3(self):
        each(1, 4, lambda d: self.l1(d, False).wait_recv())
        acc = (self.lines[0] + self.lines[1]) + (self.lines[2] + self.lines[3])
        self.total[self.part(self.spot), :] = acc
        each(1, PLANE, lambda d: self.p2(d, True).start())

    def s4(self):
        each(1, PLANE, lambda d: self.p2(d, False).wait_recv())
        self.c2(True).start()

    def s5(self):
        self.c2(False).wait_recv()

    def drain(self):
        self.c1().wait_send()
        each(1, PLANE, lambda d: self.p1(d, True).wait_send())
        each(1, 4, lambda d: self.l1(d, True).wait_send())
        each(1, PLANE, lambda d: self.p2(d, True).wait_send())
        self.c2(True).wait_send()


def reduce_scratch(rows):
    depth = rows // 2 // PLANE
    return [VMEM((rows // 2, K), F32), VMEM((PLANE, depth, K), F32), VMEM((4, depth, K), F32),
            pltpu.SemaphoreType.DMA((48,)), pltpu.SemaphoreType.DMA((48,))]


def factor_128(a, upper, inverse, hooks=None, base=0):
    size, n = 8, 16
    rows = lax.broadcasted_iota(jnp.int32, (size, 128), 0)
    lanes = lax.broadcasted_iota(jnp.int32, (size, 128), 1)
    depth = lax.broadcasted_iota(jnp.int32, (n, size, 128), 0)
    q = jnp.where(lanes[None] == rows[None] + size * depth, 1.0, 0.0).astype(F32)
    for kb in range(n):
        if hooks is not None and base + kb in hooks:
            hooks[base + kb]()
        at = size * kb
        own, own_q = a[0], q[0]
        a, q = a[1:], q[1:]
        stack = lambda x: jnp.broadcast_to(x[:, None, :], (size, size, 128))
        rest = n - 1 - kb
        r, s = stack(own), stack(own_q)
        cols = [stack(jnp.broadcast_to(own[:, at + j:at + j + 1], (size, 128))) for j in range(size)]
        side = [jnp.broadcast_to(a[:, :, at + k:at + k + 1], (rest, size, 128)) for k in range(size)] if rest else []
        m, rr, ss, pivot, root = [], [], [], [], []
        ut, wt = jnp.zeros((size, 128), F32), jnp.zeros((size, 128), F32)
        for k in range(size):
            d = cols[k][0]
            pivot.append(1.0 / d)
            rr.append(r[0]); ss.append(s[0])
            if k < size - 1:
                below = cols[k][1:]
                mk = below * pivot[k][None]
                m.append(mk)
                for j in range(k + 1, size):
                    cols[j] = cols[j][1:] if j == k + 1 and False else cols[j][1:] - mk * below[j - k - 1][None]
                r = r[1:] - mk * r[0][None]
                s = s[1:] - mk * s[0][None]
            rt = lax.rsqrt(d)
            ut = jnp.where(rows == k, rr[k] * rt, ut)
            wt = jnp.where(rows == k, ss[k] * rt, wt)
        z, zs = [None] * size, [None] * size
        for k in reversed(range(size)):
            zk, zsk = rr[k] * pivot[k], ss[k] * pivot[k]
            for j in range(k + 1, size):
                zk = zk - m[k][j - k - 1] * z[j]
                zsk = zsk - m[k][j - k - 1] * zs[j]
            z[k], zs[k] = zk, zsk
        if rest:
            for k in range(size):
                a = a - side[k] * z[k][None]
                q = q - side[k] * zs[k][None]
        upper[at:at + size, :] = jnp.where(lanes >= rows + at, ut, 0.0)
        inverse[at:at + size, :] = jnp.where(lanes <= rows + at, wt, 0.0)


def factor_256(a, upper, inverse, hooks=None):
    h = 128
    factor_128(a[:h, :h].reshape(16, 8, h), upper.at[:h, :h], inverse.at[:h, :h], hooks)
    w1 = inverse[:h, :h]
    low = nt(a[h:, :h], w1, HI)
    upper[:h, h:] = low.T
    upper[h:, :h] = jnp.zeros((h, h), F32)
    inverse[:h, h:] = jnp.zeros((h, h), F32)
    a[h:, h:] = a[h:, h:] - nt(low, low, HI)
    t = nn(low, w1, HI)
    factor_128(a[h:, h:].reshape(16, 8, h), upper.at[h:, h:], inverse.at[h:, h:], hooks, 16)
    inverse[h:, :h] = -nn(inverse[h:, h:], t, HI)


class Halo:
    def __init__(self, frames, tension, halo, tens_halo, send, recv):
        self.refs = frames, tension, halo, tens_halo, send, recv
        self.cable, self.seg = lax.axis_index("cable"), lax.axis_index("seg")

    def copies(self, side):
        frames, tension, halo, tens_halo, send, recv = self.refs
        nodes = frames.shape[0] // 4
        peer = self.seg + 1 if side == 0 else self.seg - 1
        return [
            pltpu.make_async_remote_copy(
                src_ref=frames.at[pl.ds(4 * (nodes - EDGE) if side == 0 else 0, 4 * EDGE), :], dst_ref=halo.at[side],
                send_sem=send.at[side], recv_sem=recv.at[side],
                device_id=(self.cable, peer), device_id_type=MESH),
            pltpu.make_async_remote_copy(
                src_ref=tension.at[:, pl.ds(nodes - 128 if side == 0 else 0, 128)], dst_ref=tens_halo.at[side],
                send_sem=send.at[2 + side], recv_sem=recv.at[2 + side],
                device_id=(self.cable, peer), device_id_type=MESH),
        ]

    def guarded(self, sends, act):
        for side in range(2):
            has_right, has_left = self.seg < N_SEG - 1, self.seg > 0
            here = (has_right, has_left) if sends else (has_left, has_right)

            @pl.when(here[side])
            def _():
                for copy in self.copies(side):
                    act(copy)

    def start(self):
        self.guarded(True, lambda copy: copy.start())

    def wait_recv(self):
        self.guarded(False, lambda copy: copy.wait_recv())

    def wait_send(self):
        self.guarded(True, lambda copy: copy.wait_send())

    def zero_ends(self):
        halo, tens_halo = self.refs[2:4]

        @pl.when(self.seg == 0)
        def _():
            halo[0] = jnp.zeros_like(halo[0])
            tens_halo[0] = jnp.zeros_like(tens_halo[0])

        @pl.when(self.seg == N_SEG - 1)
        def _():
            halo[1] = jnp.zeros_like(halo[1])
            tens_halo[1] = jnp.zeros_like(tens_halo[1])


def make_weights(seg, tens_halo, tens_rows, weights, steps):
    reach = SWEEPS
    full = (STRIPS, 128)
    sub = lax.broadcasted_iota(jnp.int32, full, 0)
    lane = lax.broadcasted_iota(jnp.int32, full, 1)
    low_out = jnp.logical_and(sub == 0, seg == 0)
    high_out = jnp.logical_and(sub == STRIPS - 1, seg == N_SEG - 1)
    for q in range(2):
        tens_rows[q, 7:8, :] = tens_halo[0, q:q + 1, :]
        tens_rows[q, 16:17, :] = tens_halo[1, q:q + 1, :]
        before, here, after = (tens_rows[q, 7 + i:15 + i, :] for i in range(3))

        def next_lane(x, y):
            return jnp.where(lane == 127, pltpu.roll(y, 127, 1), pltpu.roll(x, 127, 1))

        def prev_lane(x, y):
            return jnp.where(lane == 0, pltpu.roll(x, 1, 1), pltpu.roll(y, 1, 1))

        right = [0.5 * (before + next_lane(before, here)), 0.5 * (here + next_lane(here, after)),
                 0.5 * (after + next_lane(after, after))]
        left = [prev_lane(before, right[0]), prev_lane(right[0], right[1]), prev_lane(right[1], right[2])]
        for kind, rows in enumerate((left, right)):
            rows[0] = jnp.where(low_out, 0.0, rows[0])
            rows[2] = jnp.where(high_out, 0.0, rows[2])
            for step in range(steps):
                part, at = divmod(128 + step - reach, 128)
                weights[q, kind, step] = jnp.broadcast_to(rows[part][:, at:at + 1], full)


def relax(q, scale, padded, weights, solved32, solved, strip, block):
    reach = SWEEPS
    full = (STRIPS, 128)

    def advance(step, levels, coefs):
        lw, rw = weights[q, 0, step], weights[q, 1, step]
        total = lw + rw
        out = []
        for h in range(2):
            value = padded[pl.ds(4 * (EDGE - reach + step) + 2 * h + q, STRIPS, stride=4 * strip), :]
            inv = 1.0 / (1.0 + scale[h] * total)
            si = scale[h] * inv
            coefs[h].append((si * lw, si * rw, value * inv))
            levels[h][0].append(value)
            for k in range(1, SWEEPS + 1):
                below, above, own = coefs[h][-1 - k]
                value = own + (above * levels[h][k - 1][-1] + below * levels[h][k - 1][-3])
                levels[h][k].append(value)
            coefs[h][:] = coefs[h][-(SWEEPS + 1):]
            for k in range(SWEEPS + 1):
                levels[h][k][:] = levels[h][k][-2:] if k < SWEEPS else levels[h][k][-1:]
            out.append(levels[h][SWEEPS][-1])
        return out

    zero = jnp.zeros(full, F32)
    levels = [[[zero, zero] for _ in range(SWEEPS)] + [[zero]] for _ in range(2)]
    coefs = [[(zero, zero, zero)] * (SWEEPS + 1) for _ in range(2)]
    for step in range(2 * reach):
        advance(step, levels, coefs)
    unroll = 8

    def turn(i, carry):
        levels, coefs = carry
        levels = [[list(x) for x in lv] for lv in levels]
        coefs = [[tuple(x) for x in cf] for cf in coefs]
        for u in range(unroll):
            row = i * unroll + u
            out = advance(2 * reach + row, levels, coefs)
            for h in range(2):
                solved32[h, pl.ds(row, STRIPS, stride=strip), :] = out[h]
        return levels, coefs

    lax.fori_loop(0, strip // unroll, turn, (levels, coefs))

    def pack(b, _):
        rows = pl.ds(pl.multiple_of(b * block, block), block)
        for h in range(2):
            solved[b, q * block:(q + 1) * block, h * 128:(h + 1) * 128] = solved32[h, rows, :].astype(BF16)
        return 0

    lax.fori_loop(0, N_CABLE, pack, 0)


def main_kernel(rows_all, frames, tension, step_index, owner, basis, singular,
                factor, w1_out, w2_out, cross_out, snaps,
                padded, halo, tens_halo, tens_rows, weights, solved32, solved, scaled, rows32, basis_out, basis_in,
                snaps_in, a, inverse1, inverse2, local1, total1, local2, total2, half1, parts1, lines1, send1, recv1,
                half2, parts2, lines2, send2, recv2, halo_send, halo_recv, b_send, b_recv, s_send, s_recv):
    cable, seg = lax.axis_index("cable"), lax.axis_index("seg")
    nodes = frames.shape[0] // 4
    strip = nodes // STRIPS
    block = nodes // N_CABLE
    positions = 2 * N_CABLE
    scale_all = 1.0 / rows_all
    met = greet()

    scaled[...] = (basis[...].astype(F32) * singular[...]).astype(BF16)
    local1[...] = tn(scaled[...], scaled[...])
    padded[4 * EDGE:4 * (EDGE + nodes), :] = frames[...].astype(F32)
    for q in range(2):
        for s in range(STRIPS):
            tens_rows[q, 8 + s:9 + s, :] = tension[q:q + 1, s * strip:(s + 1) * strip]
    first = Reduce(local1, total1, half1, parts1, lines1, (send1, recv1))
    second = Reduce(local2, total2, half2, parts2, lines2, (send2, recv2))
    edges = Halo(frames, tension, halo, tens_halo, halo_send, halo_recv)
    edges.zero_ends()
    met()
    first.s0()
    edges.start()

    pick = (lax.broadcasted_iota(jnp.int32, (positions, positions), 0) == owner[...]).astype(F32)
    pick_bf = pick.astype(BF16)
    unpick_bf = pick.T.astype(BF16)

    def by_streamer(n, _):
        rows = scaled[pl.ds(pl.multiple_of(n * positions, positions), positions), :]
        moved = nn(pick_bf, rows)
        for h in range(2):
            rows32[h, pl.ds(n, positions, stride=block), :] = moved[:, h * 128:(h + 1) * 128]
        return 0

    lax.fori_loop(0, block, by_streamer, 0, unroll=4)
    for h in range(2):
        basis_out[:, :, h * 128:(h + 1) * 128] = rows32[h].astype(BF16).reshape(N_CABLE, 2 * block, 128)
    first.s1()

    def exchange(d, out, into, send, recv, mine):
        peer = lax.rem(cable + d, N_CABLE)
        return pltpu.make_async_remote_copy(
            src_ref=out.at[peer], dst_ref=into.at[cable if mine else peer], send_sem=send.at[d],
            recv_sem=recv.at[cable if mine else peer], device_id=(peer, seg), device_id_type=MESH)

    def basis_trip(d, mine):
        return exchange(d, basis_out, basis_in, b_send, b_recv, mine)

    def snaps_trip(d, mine):
        return exchange(d, solved, snaps_in, s_send, s_recv, mine)

    each(1, N_CABLE, lambda d: basis_trip(d, True).start())
    basis_in[cable] = basis_out[cable]

    edges.wait_recv()
    padded[0:4 * EDGE, :] = halo[0].astype(F32)
    padded[4 * (EDGE + nodes):, :] = halo[1].astype(F32)
    make_weights(seg, tens_halo, tens_rows, weights, strip + 2 * SWEEPS)
    stiff = DRAG_RATE * (1.0 + step_index[...].astype(F32))
    scale = [jnp.broadcast_to(stiff[:, h * 128:(h + 1) * 128], (STRIPS, 128)) for h in range(2)]
    relax(0, scale, padded, weights, solved32, solved, strip, block)
    first.s2()
    relax(1, scale, padded, weights, solved32, solved, strip, block)
    flat = solved[...].reshape(2 * nodes, SNAP)
    local2[K:, :] = tn(flat, flat)
    first.s3()
    each(1, N_CABLE, lambda d: basis_trip(d, False).wait_recv())
    local2[:K, :] = tn(flat, basis_in[...].reshape(2 * nodes, K))
    second.s0()
    second.s1()
    first.s4()
    first.s5()
    a[...] = total1[...] * scale_all

    def send_snaps():
        second.s3()
        each(1, N_CABLE, lambda d: snaps_trip(d, True).start())
        snaps_in[cable] = solved[cable]

    factor_256(a, factor.at[:K, :K], inverse1, {16: second.s2, 28: send_snaps})
    w1 = inverse1[...]
    w1_out[...] = w1.astype(BF16)
    factor[K:, :K] = jnp.zeros((K, K), F32)
    second.s4()
    second.s5()
    low = nt(total2[:K, :] * scale_all, w1, HI)
    factor[:K, K:] = low.T
    a[...] = total2[K:, :] * scale_all - nt(low, low, HI)
    t = nn(low, w1, HI)
    factor_256(a, factor.at[K:, K:], inverse2)
    w2 = inverse2[...]
    w2_out[...] = w2.astype(BF16)
    cross_out[...] = (-nn(w2, t, HI)).astype(BF16)
    each(1, N_CABLE, lambda d: snaps_trip(d, False).wait_recv())

    for h in range(2):
        rows32[h] = snaps_in[:, :, h * 128:(h + 1) * 128].astype(F32).reshape(positions * block, 128)

    def by_position(n, _):
        rows = jnp.concatenate([rows32[h, pl.ds(n, positions, stride=block), :] for h in range(2)], axis=1)
        snaps[pl.ds(pl.multiple_of(n * positions, positions), positions), :] = (
            nn(unpick_bf, rows.astype(BF16)).astype(BF16))
        return 0

    lax.fori_loop(0, block, by_position, 0, unroll=4)
    first.drain()
    second.drain()
    edges.wait_send()
    each(1, N_CABLE, lambda d: basis_trip(d, True).wait_send())
    each(1, N_CABLE, lambda d: snaps_trip(d, True).wait_send())


def exchange_and_factor(rows_all, frames, tension, step_index, owner_map, basis, singular):
    nodes = frames.shape[0] // 4
    rows = basis.shape[0]
    block = nodes // N_CABLE
    steps = nodes // STRIPS + 2 * SWEEPS
    dma = pltpu.SemaphoreType.DMA
    square = jax.ShapeDtypeStruct((K, K), BF16)
    return pl.pallas_call(
        lambda *refs: main_kernel(rows_all, *refs),
        out_shape=[jax.ShapeDtypeStruct((2 * K, 2 * K), F32), square, square, square,
                   jax.ShapeDtypeStruct((rows, SNAP), BF16)],
        in_specs=[vmem_spec()] * 6,
        out_specs=[vmem_spec()] * 5,
        scratch_shapes=[
            VMEM((4 * (nodes + 2 * EDGE), 128), F32),
            VMEM((2, 4 * EDGE, 128), BF16),
            VMEM((2, 2, 128), F32),
            VMEM((2, 24, 128), F32),
            VMEM((2, 2, steps, STRIPS, 128), F32),
            VMEM((2, nodes, 128), F32),
            VMEM((N_CABLE, 2 * block, SNAP), BF16),
            VMEM((rows, K), BF16),
            VMEM((2, rows, 128), F32),
            VMEM((N_CABLE, 2 * block, K), BF16),
            VMEM((N_CABLE, 2 * block, K), BF16),
            VMEM((N_CABLE, 2 * block, SNAP), BF16),
            VMEM((K, K), F32),
            VMEM((K, K), F32),
            VMEM((K, K), F32),
            VMEM((K, K), F32),
            VMEM((K, K), F32),
            VMEM((2 * K, K), F32),
            VMEM((2 * K, K), F32),
            *reduce_scratch(K), *reduce_scratch(2 * K),
            dma((4,)), dma((4,)), *[dma((N_CABLE,))] * 4,
        ],
        compiler_params=pltpu.CompilerParams(collective_id=0, has_side_effects=True, vmem_limit_bytes=48 * 2**20),
        name="relax_exchange_factor",
    )(frames, tension, step_index, owner_map, basis, singular)


def rotate_kernel(factor_in, w1, w2, cross, basis, singular, snaps, factor, new_basis, sem):
    copy = pltpu.make_async_copy(factor_in, factor, sem)
    copy.start()
    scaled = (basis[...].astype(F32) * singular[...]).astype(BF16)
    new_basis[:, :K] = nt(scaled, w1[...]).astype(BF16)
    new_basis[:, K:] = (nt(scaled, cross[...]) + nt(snaps[...], w2[...])).astype(BF16)
    copy.wait()


def rotate(factor, w1, w2, cross, basis, singular, snaps):
    rows, width = basis.shape[0], 2 * K
    anywhere = pl.BlockSpec(memory_space=pl.ANY)
    return pl.pallas_call(
        rotate_kernel,
        out_shape=[jax.ShapeDtypeStruct((width, width), F32), jax.ShapeDtypeStruct((rows, width), BF16)],
        in_specs=[anywhere] + [vmem_spec()] * 6,
        out_specs=[anywhere, vmem_spec()],
        scratch_shapes=[pltpu.SemaphoreType.DMA],
        compiler_params=pltpu.CompilerParams(vmem_limit_bytes=40 * 2**20),
        name="rotate",
    )(factor, w1, w2, cross, basis, singular, snaps)


def body(frames, tension, step_index, owner_map, old_basis, singular):
    nodes = frames.shape[0]
    basis = old_basis.reshape(-1, K)
    gain = singular[None, :]
    rows_all = basis.shape[0] * lax.axis_size("cable") * lax.axis_size("seg")
    lines = frames.reshape(nodes, 2, 2, 128).transpose(0, 2, 1, 3).reshape(4 * nodes, 128)
    factor, w1, w2, cross, snaps = exchange_and_factor(
        rows_all, lines, tension.T, step_index[None, :], owner_map[None, :], basis, gain)
    factor, rotated = rotate(factor, w1, w2, cross, basis, gain, snaps)
    return factor, rotated.reshape(old_basis.shape[:3] + (2 * K,))


def solution(mesh):
    return jax.shard_map(
        body,
        mesh=mesh,
        in_specs=(P("seg", "cable", None), P("seg", "cable"), P(), P(), P("seg", "cable", None, None), P()),
        out_specs=(P(), P("seg", "cable", None, None)),
        check_vma=False,
    )
```

```python
import jax
import jax.numpy as jnp
from jax import lax
from jax.experimental import pallas as pl
from jax.experimental.pallas import tpu as pltpu
from jax.sharding import PartitionSpec as P

K = 256
SNAP = 256
SWEEPS = 6
DRAG_RATE = 0.1
STRIPS = 8
EDGE = 16
MESH = pl.DeviceIdType.MESH
HI = lax.Precision.HIGHEST
VMEM = pltpu.VMEM
F32 = jnp.float32
BF16 = jnp.bfloat16


def vmem_spec():
    return pl.BlockSpec(memory_space=pltpu.VMEM)


def nt(a, b, precision=None):
    return lax.dot_general(a, b, (((1,), (1,)), ((), ())), precision=precision, preferred_element_type=F32)


def nn(a, b, precision=None):
    return lax.dot_general(a, b, (((1,), (0,)), ((), ())), precision=precision, preferred_element_type=F32)


def tn(a, b, precision=None):
    return lax.dot_general(a, b, (((0,), (0,)), ((), ())), precision=precision, preferred_element_type=F32)


def place():
    cable, seg = lax.axis_index("cable"), lax.axis_index("seg")
    return cable, seg, cable // 8, lax.rem(cable // 4, 2), lax.rem(cable, 4), seg // 2, lax.rem(seg, 2)


N_CABLE = 32
N_SEG = 4
PLANE = 16


def each(first, last, act):
    def turn(d, _):
        act(d)
        return 0
    lax.fori_loop(first, last, turn, 0)


def greet():
    cable, seg, x, y_lo, z, y_hi, core = place()
    barrier = pltpu.get_barrier_semaphore()

    def hail(device):
        pl.semaphore_signal(barrier, inc=1, device_id=device, device_id_type=MESH)

    each(1, N_CABLE, lambda d: hail((lax.rem(cable + d, N_CABLE), seg)))
    each(1, N_SEG, lambda d: hail((cable, lax.rem(seg + d, N_SEG))))
    hail((x * 8 + (1 - y_lo) * 4 + z, (1 - y_hi) * 2 + core))
    return lambda: pl.semaphore_wait(barrier, N_CABLE + N_SEG - 1)


class Reduce:
    def __init__(self, local, total, half, parts, lines, sems):
        self.local, self.total, self.half, self.parts, self.lines = local, total, half, parts, lines
        self.send, self.recv = sems
        self.rows = local.shape[0]
        self.depth = self.rows // 2 // PLANE
        self.cable, self.seg, self.x, self.y_lo, self.z, self.y_hi, self.core = place()
        self.spot = self.x * 4 + self.z
        self.y = self.y_hi * 2 + self.y_lo
        self.sister = (self.cable, self.y_hi * 2 + 1 - self.core)

    def copy(self, src, dst, slot, landing, device):
        return pltpu.make_async_remote_copy(
            src_ref=src, dst_ref=dst, send_sem=self.send.at[slot], recv_sem=self.recv.at[landing],
            device_id=device, device_id_type=MESH)

    def plane(self, d):
        spot = lax.rem(self.spot + d, PLANE)
        return spot, ((spot // 4) * 8 + self.y_lo * 4 + lax.rem(spot, 4), self.seg)

    def line(self, d):
        y = lax.rem(self.y + d, 4)
        return y, (self.x * 8 + lax.rem(y, 2) * 4 + self.z, (y // 2) * 2 + self.core)

    def part(self, spot):
        at = self.core * (self.rows // 2) + spot * self.depth
        return pl.ds(pl.multiple_of(at, self.depth), self.depth)

    def own_half(self):
        return pl.ds(pl.multiple_of(self.core * (self.rows // 2), self.rows // 2), self.rows // 2)

    def other_half(self):
        return pl.ds(pl.multiple_of((1 - self.core) * (self.rows // 2), self.rows // 2), self.rows // 2)

    def c1(self):
        return self.copy(self.local.at[self.other_half(), :], self.half, 0, 0, self.sister)

    def p1(self, d, mine):
        spot, device = self.plane(d)
        return self.copy(self.half.at[pl.ds(pl.multiple_of(spot * self.depth, self.depth), self.depth), :],
                         self.parts.at[self.spot if mine else spot], 16 + d, 16 + (self.spot if mine else spot), device)

    def l1(self, d, mine):
        y, device = self.line(d)
        return self.copy(self.lines.at[self.y], self.lines.at[self.y if mine else y], 4 + d,
                         4 + (self.y if mine else y), device)

    def p2(self, d, mine):
        spot, device = self.plane(d)
        rows = self.part(self.spot if mine else spot)
        return self.copy(self.total.at[rows, :], self.total.at[rows, :], 32 + d,
                         32 + (self.spot if mine else spot), device)

    def c2(self, mine):
        rows = self.own_half() if mine else self.other_half()
        return self.copy(self.total.at[rows, :], self.total.at[rows, :], 1, 1, self.sister)

    def s0(self):
        self.c1().start()

    def s1(self):
        self.c1().wait_recv()
        self.half[...] = self.half[...] + self.local[self.own_half(), :]
        each(1, PLANE, lambda d: self.p1(d, True).start())
        self.parts[self.spot] = self.half[pl.ds(pl.multiple_of(self.spot * self.depth, self.depth), self.depth), :]

    def s2(self):
        each(1, PLANE, lambda d: self.p1(d, False).wait_recv())
        acc = self.parts[0]
        for i in range(1, PLANE):
            acc = acc + self.parts[i]
        self.lines[self.y] = acc
        each(1, 4, lambda d: self.l1(d, True).start())

    def s3(self):
        each(1, 4, lambda d: self.l1(d, False).wait_recv())
        acc = (self.lines[0] + self.lines[1]) + (self.lines[2] + self.lines[3])
        self.total[self.part(self.spot), :] = acc
        each(1, PLANE, lambda d: self.p2(d, True).start())

    def s4(self):
        each(1, PLANE, lambda d: self.p2(d, False).wait_recv())
        self.c2(True).start()

    def s5(self):
        self.c2(False).wait_recv()

    def drain(self):
        self.c1().wait_send()
        each(1, PLANE, lambda d: self.p1(d, True).wait_send())
        each(1, 4, lambda d: self.l1(d, True).wait_send())
        each(1, PLANE, lambda d: self.p2(d, True).wait_send())
        self.c2(True).wait_send()


def reduce_scratch(rows):
    depth = rows // 2 // PLANE
    return [VMEM((rows // 2, K), F32), VMEM((PLANE, depth, K), F32), VMEM((4, depth, K), F32),
            pltpu.SemaphoreType.DMA((48,)), pltpu.SemaphoreType.DMA((48,))]


def factor_128(a, upper, inverse, hooks=None, base=0):
    size, n = 8, 16
    rows = lax.broadcasted_iota(jnp.int32, (size, 128), 0)
    lanes = lax.broadcasted_iota(jnp.int32, (size, 128), 1)
    depth = lax.broadcasted_iota(jnp.int32, (n, size, 128), 0)
    q = jnp.where(lanes[None] == rows[None] + size * depth, 1.0, 0.0).astype(F32)
    for kb in range(n):
        if hooks is not None and base + kb in hooks:
            hooks[base + kb]()
        at = size * kb
        own, own_q = a[0], q[0]
        a, q = a[1:], q[1:]
        stack = lambda x: jnp.broadcast_to(x[:, None, :], (size, size, 128))
        rest = n - 1 - kb
        r, s = stack(own), stack(own_q)
        cols = [stack(jnp.broadcast_to(own[:, at + j:at + j + 1], (size, 128))) for j in range(size)]
        side = [jnp.broadcast_to(a[:, :, at + k:at + k + 1], (rest, size, 128)) for k in range(size)] if rest else []
        m, rr, ss, pivot, root = [], [], [], [], []
        ut, wt = jnp.zeros((size, 128), F32), jnp.zeros((size, 128), F32)
        for k in range(size):
            d = cols[k][0]
            pivot.append(1.0 / d)
            rr.append(r[0]); ss.append(s[0])
            if k < size - 1:
                below = cols[k][1:]
                mk = below * pivot[k][None]
                m.append(mk)
                for j in range(k + 1, size):
                    cols[j] = cols[j][1:] if j == k + 1 and False else cols[j][1:] - mk * below[j - k - 1][None]
                r = r[1:] - mk * r[0][None]
                s = s[1:] - mk * s[0][None]
            rt = lax.rsqrt(d)
            ut = jnp.where(rows == k, rr[k] * rt, ut)
            wt = jnp.where(rows == k, ss[k] * rt, wt)
        z, zs = [None] * size, [None] * size
        for k in reversed(range(size)):
            zk, zsk = rr[k] * pivot[k], ss[k] * pivot[k]
            for j in range(k + 1, size):
                zk = zk - m[k][j - k - 1] * z[j]
                zsk = zsk - m[k][j - k - 1] * zs[j]
            z[k], zs[k] = zk, zsk
        if rest:
            for k in range(size):
                a = a - side[k] * z[k][None]
                q = q - side[k] * zs[k][None]
        upper[at:at + size, :] = jnp.where(lanes >= rows + at, ut, 0.0)
        inverse[at:at + size, :] = jnp.where(lanes <= rows + at, wt, 0.0)


def factor_256(a, upper, inverse, hooks=None):
    h = 128
    factor_128(a[:h, :h].reshape(16, 8, h), upper.at[:h, :h], inverse.at[:h, :h], hooks)
    w1 = inverse[:h, :h]
    low = nt(a[h:, :h], w1, HI)
    upper[:h, h:] = low.T
    upper[h:, :h] = jnp.zeros((h, h), F32)
    inverse[:h, h:] = jnp.zeros((h, h), F32)
    a[h:, h:] = a[h:, h:] - nt(low, low, HI)
    t = nn(low, w1, HI)
    factor_128(a[h:, h:].reshape(16, 8, h), upper.at[h:, h:], inverse.at[h:, h:], hooks, 16)
    inverse[h:, :h] = -nn(inverse[h:, h:], t, HI)


class Halo:
    def __init__(self, frames, tension, halo, tens_halo, send, recv):
        self.refs = frames, tension, halo, tens_halo, send, recv
        self.cable, self.seg = lax.axis_index("cable"), lax.axis_index("seg")

    def copies(self, side):
        frames, tension, halo, tens_halo, send, recv = self.refs
        nodes = frames.shape[0] // 4
        peer = self.seg + 1 if side == 0 else self.seg - 1
        return [
            pltpu.make_async_remote_copy(
                src_ref=frames.at[pl.ds(4 * (nodes - EDGE) if side == 0 else 0, 4 * EDGE), :], dst_ref=halo.at[side],
                send_sem=send.at[side], recv_sem=recv.at[side],
                device_id=(self.cable, peer), device_id_type=MESH),
            pltpu.make_async_remote_copy(
                src_ref=tension.at[:, pl.ds(nodes - 128 if side == 0 else 0, 128)], dst_ref=tens_halo.at[side],
                send_sem=send.at[2 + side], recv_sem=recv.at[2 + side],
                device_id=(self.cable, peer), device_id_type=MESH),
        ]

    def guarded(self, sends, act):
        for side in range(2):
            has_right, has_left = self.seg < N_SEG - 1, self.seg > 0
            here = (has_right, has_left) if sends else (has_left, has_right)

            @pl.when(here[side])
            def _():
                for copy in self.copies(side):
                    act(copy)

    def start(self):
        self.guarded(True, lambda copy: copy.start())

    def wait_recv(self):
        self.guarded(False, lambda copy: copy.wait_recv())

    def wait_send(self):
        self.guarded(True, lambda copy: copy.wait_send())

    def zero_ends(self):
        halo, tens_halo = self.refs[2:4]

        @pl.when(self.seg == 0)
        def _():
            halo[0] = jnp.zeros_like(halo[0])
            tens_halo[0] = jnp.zeros_like(tens_halo[0])

        @pl.when(self.seg == N_SEG - 1)
        def _():
            halo[1] = jnp.zeros_like(halo[1])
            tens_halo[1] = jnp.zeros_like(tens_halo[1])


def make_weights(seg, tens_halo, tens_rows, weights, steps):
    reach = SWEEPS
    full = (STRIPS, 128)
    sub = lax.broadcasted_iota(jnp.int32, full, 0)
    lane = lax.broadcasted_iota(jnp.int32, full, 1)
    low_out = jnp.logical_and(sub == 0, seg == 0)
    high_out = jnp.logical_and(sub == STRIPS - 1, seg == N_SEG - 1)
    for q in range(2):
        tens_rows[q, 7:8, :] = tens_halo[0, q:q + 1, :]
        tens_rows[q, 16:17, :] = tens_halo[1, q:q + 1, :]
        before, here, after = (tens_rows[q, 7 + i:15 + i, :] for i in range(3))

        def next_lane(x, y):
            return jnp.where(lane == 127, pltpu.roll(y, 127, 1), pltpu.roll(x, 127, 1))

        def prev_lane(x, y):
            return jnp.where(lane == 0, pltpu.roll(x, 1, 1), pltpu.roll(y, 1, 1))

        right = [0.5 * (before + next_lane(before, here)), 0.5 * (here + next_lane(here, after)),
                 0.5 * (after + next_lane(after, after))]
        left = [prev_lane(before, right[0]), prev_lane(right[0], right[1]), prev_lane(right[1], right[2])]
        for kind, rows in enumerate((left, right)):
            rows[0] = jnp.where(low_out, 0.0, rows[0])
            rows[2] = jnp.where(high_out, 0.0, rows[2])
            for step in range(steps):
                part, at = divmod(128 + step - reach, 128)
                weights[q, kind, step] = jnp.broadcast_to(rows[part][:, at:at + 1], full)


def relax(q, scale, padded, weights, solved32, solved, strip, block):
    reach = SWEEPS
    full = (STRIPS, 128)

    def advance(step, levels, coefs):
        lw, rw = weights[q, 0, step], weights[q, 1, step]
        total = lw + rw
        out = []
        for h in range(2):
            value = padded[pl.ds(4 * (EDGE - reach + step) + 2 * h + q, STRIPS, stride=4 * strip), :]
            inv = 1.0 / (1.0 + scale[h] * total)
            si = scale[h] * inv
            coefs[h].append((si * lw, si * rw, value * inv))
            levels[h][0].append(value)
            for k in range(1, SWEEPS + 1):
                below, above, own = coefs[h][-1 - k]
                value = own + (above * levels[h][k - 1][-1] + below * levels[h][k - 1][-3])
                levels[h][k].append(value)
            coefs[h][:] = coefs[h][-(SWEEPS + 1):]
            for k in range(SWEEPS + 1):
                levels[h][k][:] = levels[h][k][-2:] if k < SWEEPS else levels[h][k][-1:]
            out.append(levels[h][SWEEPS][-1])
        return out

    zero = jnp.zeros(full, F32)
    levels = [[[zero, zero] for _ in range(SWEEPS)] + [[zero]] for _ in range(2)]
    coefs = [[(zero, zero, zero)] * (SWEEPS + 1) for _ in range(2)]
    for step in range(2 * reach):
        advance(step, levels, coefs)
    unroll = 8

    def turn(i, carry):
        levels, coefs = carry
        levels = [[list(x) for x in lv] for lv in levels]
        coefs = [[tuple(x) for x in cf] for cf in coefs]
        for u in range(unroll):
            row = i * unroll + u
            out = advance(2 * reach + row, levels, coefs)
            for h in range(2):
                solved32[h, pl.ds(row, STRIPS, stride=strip), :] = out[h]
        return levels, coefs

    lax.fori_loop(0, strip // unroll, turn, (levels, coefs))

    def pack(b, _):
        rows = pl.ds(pl.multiple_of(b * block, block), block)
        for h in range(2):
            solved[b, q * block:(q + 1) * block, h * 128:(h + 1) * 128] = solved32[h, rows, :].astype(BF16)
        return 0

    lax.fori_loop(0, N_CABLE, pack, 0)


def main_kernel(rows_all, frames_in, tension_in, step_in, owner_in, basis_hbm, singular_in,
                factor, w1_out, w2_out, cross_out, snaps,
                frames, tension, step_index, owner, basis, singular, load_sem, padded, halo, tens_halo, tens_rows, weights, solved32, solved, scaled, rows32, basis_out, basis_in,
                snaps_in, a, inverse1, inverse2, local1, total1, local2, total2, half1, parts1, lines1, send1, recv1,
                half2, parts2, lines2, send2, recv2, halo_send, halo_recv, b_send, b_recv, s_send, s_recv):
    cable, seg = lax.axis_index("cable"), lax.axis_index("seg")
    nodes = frames_in.shape[0] // 4
    strip = nodes // STRIPS
    block = nodes // N_CABLE
    positions = 2 * N_CABLE
    scale_all = 1.0 / rows_all
    met = greet()
    loads = [pltpu.make_async_copy(src, dst, load_sem.at[i]) for i, (src, dst) in enumerate((
        (basis_hbm, basis), (singular_in, singular), (owner_in, owner), (frames_in, frames), (tension_in, tension),
        (step_in, step_index)))]
    for load in loads:
        load.start()

    for load in loads[:3]:
        load.wait()
    scaled[...] = (basis[...].astype(F32) * singular[...]).astype(BF16)
    pick = (lax.broadcasted_iota(jnp.int32, (positions, positions), 0) == owner[...]).astype(F32)
    pick_bf = pick.astype(BF16)
    unpick_bf = pick.T.astype(BF16)

    def by_streamer(n, _):
        rows = scaled[pl.ds(pl.multiple_of(n * positions, positions), positions), :]
        moved = nn(pick_bf, rows)
        for h in range(2):
            rows32[h, pl.ds(n, positions, stride=block), :] = moved[:, h * 128:(h + 1) * 128]
        return 0

    lax.fori_loop(0, block, by_streamer, 0, unroll=4)
    for h in range(2):
        basis_out[:, :, h * 128:(h + 1) * 128] = rows32[h].astype(BF16).reshape(N_CABLE, 2 * block, 128)
    for load in loads[3:]:
        load.wait()
    first = Reduce(local1, total1, half1, parts1, lines1, (send1, recv1))
    second = Reduce(local2, total2, half2, parts2, lines2, (send2, recv2))
    edges = Halo(frames, tension, halo, tens_halo, halo_send, halo_recv)
    edges.zero_ends()

    def exchange(d, out, into, q, send, recv, mine):
        peer = lax.rem(cable + d, N_CABLE)
        rows = pl.ds(q * block, block)
        return pltpu.make_async_remote_copy(
            src_ref=out.at[peer, rows, :], dst_ref=into.at[cable if mine else peer, rows, :], send_sem=send.at[q, d],
            recv_sem=recv.at[q, cable if mine else peer], device_id=(peer, seg), device_id_type=MESH)

    def basis_trip(d, mine):
        return exchange(d, basis_out, basis_in, 0, b_send, b_recv, mine)

    def snaps_trip(q, d, mine):
        return exchange(d, solved, snaps_in, q, s_send, s_recv, mine)

    def send_snaps(q):
        each(1, N_CABLE, lambda d: snaps_trip(q, d, True).start())
        snaps_in[cable, q * block:(q + 1) * block, :] = solved[cable, q * block:(q + 1) * block, :]

    def half(ref, q):
        return ref[:, q * block:(q + 1) * block, :].reshape(nodes, K)

    met()
    edges.start()
    each(1, N_CABLE, lambda d: basis_trip(d, True).start())
    local1[...] = tn(scaled[...], scaled[...])
    first.s0()
    basis_in[cable, 0:block, :] = basis_out[cable, 0:block, :]
    padded[4 * EDGE:4 * (EDGE + nodes), :] = frames[...].astype(F32)
    for q in range(2):
        for s in range(STRIPS):
            tens_rows[q, 8 + s:9 + s, :] = tension[q:q + 1, s * strip:(s + 1) * strip]
    first.s1()
    edges.wait_recv()
    padded[0:4 * EDGE, :] = halo[0].astype(F32)
    padded[4 * (EDGE + nodes):, :] = halo[1].astype(F32)
    make_weights(seg, tens_halo, tens_rows, weights, strip + 2 * SWEEPS)
    stiff = DRAG_RATE * (1.0 + step_index[...].astype(F32))
    scale = [jnp.broadcast_to(stiff[:, h * 128:(h + 1) * 128], (STRIPS, 128)) for h in range(2)]
    relax(1, scale, padded, weights, solved32, solved, strip, block)
    send_snaps(1)
    first.s2()
    relax(0, scale, padded, weights, solved32, solved, strip, block)
    flat = solved[...].reshape(2 * nodes, SNAP)
    local2[K:, :] = tn(flat, flat)
    first.s3()
    each(1, N_CABLE, lambda d: basis_trip(d, False).wait_recv())
    local2[:K, :] = tn(half(solved, 0), half(basis_in, 0))
    each(1, N_CABLE, lambda d: snaps_trip(1, d, False).wait_recv())
    local2[:K, :] += tn(half(snaps_in, 1), half(basis_out, 1))
    second.s0()
    second.s1()
    first.s4()
    first.s5()
    a[...] = total1[...] * scale_all

    def spread_second():
        second.s3()
        send_snaps(0)

    factor_256(a, factor.at[:K, :K], inverse1, {12: second.s2, 24: spread_second})
    w1 = inverse1[...]
    w1_out[...] = w1.astype(BF16)
    factor[K:, :K] = jnp.zeros((K, K), F32)
    second.s4()
    second.s5()
    low = nt(total2[:K, :] * scale_all, w1, HI)
    factor[:K, K:] = low.T
    a[...] = total2[K:, :] * scale_all - nt(low, low, HI)
    t = nn(low, w1, HI)
    factor_256(a, factor.at[K:, K:], inverse2)
    w2 = inverse2[...]
    w2_out[...] = w2.astype(BF16)
    cross_out[...] = (-nn(w2, t, HI)).astype(BF16)
    each(1, N_CABLE, lambda d: snaps_trip(0, d, False).wait_recv())

    for h in range(2):
        rows32[h] = snaps_in[:, :, h * 128:(h + 1) * 128].astype(F32).reshape(positions * block, 128)

    def by_position(n, _):
        rows = jnp.concatenate([rows32[h, pl.ds(n, positions, stride=block), :] for h in range(2)], axis=1)
        snaps[pl.ds(pl.multiple_of(n * positions, positions), positions), :] = (
            nn(unpick_bf, rows.astype(BF16)).astype(BF16))
        return 0

    lax.fori_loop(0, block, by_position, 0, unroll=4)
    first.drain()
    second.drain()
    edges.wait_send()
    each(1, N_CABLE, lambda d: basis_trip(d, True).wait_send())
    for q in range(2):
        each(1, N_CABLE, lambda d: snaps_trip(q, d, True).wait_send())


def exchange_and_factor(rows_all, frames, tension, step_index, owner_map, basis, singular):
    nodes = frames.shape[0] // 4
    rows = basis.shape[0]
    block = nodes // N_CABLE
    steps = nodes // STRIPS + 2 * SWEEPS
    dma = pltpu.SemaphoreType.DMA
    square = jax.ShapeDtypeStruct((K, K), BF16)
    return pl.pallas_call(
        lambda *refs: main_kernel(rows_all, *refs),
        out_shape=[jax.ShapeDtypeStruct((2 * K, 2 * K), F32), square, square, square,
                   jax.ShapeDtypeStruct((rows, SNAP), BF16)],
        in_specs=[pl.BlockSpec(memory_space=pltpu.HBM)] * 6,
        out_specs=[vmem_spec()] * 5,
        scratch_shapes=[
            *[VMEM(x.shape, x.dtype) for x in (frames, tension, step_index, owner_map, basis, singular)],
            dma((6,)),
            VMEM((4 * (nodes + 2 * EDGE), 128), F32),
            VMEM((2, 4 * EDGE, 128), BF16),
            VMEM((2, 2, 128), F32),
            VMEM((2, 24, 128), F32),
            VMEM((2, 2, steps, STRIPS, 128), F32),
            VMEM((2, nodes, 128), F32),
            VMEM((N_CABLE, 2 * block, SNAP), BF16),
            VMEM((rows, K), BF16),
            VMEM((2, rows, 128), F32),
            VMEM((N_CABLE, 2 * block, K), BF16),
            VMEM((N_CABLE, 2 * block, K), BF16),
            VMEM((N_CABLE, 2 * block, SNAP), BF16),
            VMEM((K, K), F32),
            VMEM((K, K), F32),
            VMEM((K, K), F32),
            VMEM((K, K), F32),
            VMEM((K, K), F32),
            VMEM((2 * K, K), F32),
            VMEM((2 * K, K), F32),
            *reduce_scratch(K), *reduce_scratch(2 * K),
            dma((4,)), dma((4,)), *[dma((2, N_CABLE))] * 4,
        ],
        compiler_params=pltpu.CompilerParams(collective_id=0, has_side_effects=True, vmem_limit_bytes=48 * 2**20),
        name="relax_exchange_factor",
    )(frames, tension, step_index, owner_map, basis, singular)


def rotate_kernel(factor_in, w1, w2, cross, basis, singular, snaps, factor, new_basis, sem):
    copy = pltpu.make_async_copy(factor_in, factor, sem)
    copy.start()
    scaled = (basis[...].astype(F32) * singular[...]).astype(BF16)
    new_basis[:, :K] = nt(scaled, w1[...]).astype(BF16)
    new_basis[:, K:] = (nt(scaled, cross[...]) + nt(snaps[...], w2[...])).astype(BF16)
    copy.wait()


def rotate(factor, w1, w2, cross, basis, singular, snaps):
    rows, width = basis.shape[0], 2 * K
    anywhere = pl.BlockSpec(memory_space=pl.ANY)
    return pl.pallas_call(
        rotate_kernel,
        out_shape=[jax.ShapeDtypeStruct((width, width), F32), jax.ShapeDtypeStruct((rows, width), BF16)],
        in_specs=[anywhere] + [vmem_spec()] * 6,
        out_specs=[anywhere, vmem_spec()],
        scratch_shapes=[pltpu.SemaphoreType.DMA],
        compiler_params=pltpu.CompilerParams(vmem_limit_bytes=40 * 2**20),
        name="rotate",
    )(factor, w1, w2, cross, basis, singular, snaps)


def body(frames, tension, step_index, owner_map, old_basis, singular):
    nodes = frames.shape[0]
    basis = old_basis.reshape(-1, K)
    gain = singular[None, :]
    rows_all = basis.shape[0] * lax.axis_size("cable") * lax.axis_size("seg")
    lines = frames.reshape(nodes, 2, 2, 128).transpose(0, 2, 1, 3).reshape(4 * nodes, 128)
    operands = (pltpu.with_memory_space_constraint(value, pltpu.HBM) for value in (
        lines, tension.T, step_index[None, :], owner_map[None, :], basis, gain))
    factor, w1, w2, cross, snaps = exchange_and_factor(rows_all, *operands)
    factor, rotated = rotate(factor, w1, w2, cross, basis, gain, snaps)
    return factor, rotated.reshape(old_basis.shape[:3] + (2 * K,))


def solution(mesh):
    return jax.shard_map(
        body,
        mesh=mesh,
        in_specs=(P("seg", "cable", None), P("seg", "cable"), P(), P(), P("seg", "cable", None, None), P()),
        out_specs=(P(), P("seg", "cable", None, None)),
        check_vma=False,
    )
```

```python
import jax
import jax.numpy as jnp
from jax import lax
from jax.experimental import pallas as pl
from jax.experimental.pallas import tpu as pltpu
from jax.sharding import PartitionSpec as P

K = 256
SNAP = 256
SWEEPS = 6
DRAG_RATE = 0.1
STRIPS = 8
EDGE = 16
MESH = pl.DeviceIdType.MESH
HI = lax.Precision.HIGHEST
VMEM = pltpu.VMEM
F32 = jnp.float32
BF16 = jnp.bfloat16


def vmem_spec():
    return pl.BlockSpec(memory_space=pltpu.VMEM)


def nt(a, b, precision=None):
    return lax.dot_general(a, b, (((1,), (1,)), ((), ())), precision=precision, preferred_element_type=F32)


def nn(a, b, precision=None):
    return lax.dot_general(a, b, (((1,), (0,)), ((), ())), precision=precision, preferred_element_type=F32)


def tn(a, b, precision=None):
    return lax.dot_general(a, b, (((0,), (0,)), ((), ())), precision=precision, preferred_element_type=F32)


def place():
    cable, seg = lax.axis_index("cable"), lax.axis_index("seg")
    return cable, seg, cable // 8, lax.rem(cable // 4, 2), lax.rem(cable, 4), seg // 2, lax.rem(seg, 2)


N_CABLE = 32
N_SEG = 4
PLANE = 16


def each(first, last, act):
    def turn(d, _):
        act(d)
        return 0
    lax.fori_loop(first, last, turn, 0)


def greet():
    cable, seg, x, y_lo, z, y_hi, core = place()
    barrier = pltpu.get_barrier_semaphore()

    def hail(device):
        pl.semaphore_signal(barrier, inc=1, device_id=device, device_id_type=MESH)

    each(1, N_CABLE, lambda d: hail((lax.rem(cable + d, N_CABLE), seg)))
    each(1, N_SEG, lambda d: hail((cable, lax.rem(seg + d, N_SEG))))
    hail((x * 8 + (1 - y_lo) * 4 + z, (1 - y_hi) * 2 + core))
    return lambda: pl.semaphore_wait(barrier, N_CABLE + N_SEG - 1)


class Reduce:
    def __init__(self, local, total, half, parts, lines, sems):
        self.local, self.total, self.half, self.parts, self.lines = local, total, half, parts, lines
        self.send, self.recv = sems
        self.rows = local.shape[0]
        self.depth = self.rows // 2 // PLANE
        self.cable, self.seg, self.x, self.y_lo, self.z, self.y_hi, self.core = place()
        self.spot = self.x * 4 + self.z
        self.y = self.y_hi * 2 + self.y_lo
        self.sister = (self.cable, self.y_hi * 2 + 1 - self.core)

    def copy(self, src, dst, slot, landing, device):
        return pltpu.make_async_remote_copy(
            src_ref=src, dst_ref=dst, send_sem=self.send.at[slot], recv_sem=self.recv.at[landing],
            device_id=device, device_id_type=MESH)

    def plane(self, d):
        spot = lax.rem(self.spot + d, PLANE)
        return spot, ((spot // 4) * 8 + self.y_lo * 4 + lax.rem(spot, 4), self.seg)

    def line(self, d):
        y = lax.rem(self.y + d, 4)
        return y, (self.x * 8 + lax.rem(y, 2) * 4 + self.z, (y // 2) * 2 + self.core)

    def part(self, spot):
        at = self.core * (self.rows // 2) + spot * self.depth
        return pl.ds(pl.multiple_of(at, self.depth), self.depth)

    def own_half(self):
        return pl.ds(pl.multiple_of(self.core * (self.rows // 2), self.rows // 2), self.rows // 2)

    def other_half(self):
        return pl.ds(pl.multiple_of((1 - self.core) * (self.rows // 2), self.rows // 2), self.rows // 2)

    def c1(self):
        return self.copy(self.local.at[self.other_half(), :], self.half, 0, 0, self.sister)

    def p1(self, d, mine):
        spot, device = self.plane(d)
        return self.copy(self.half.at[pl.ds(pl.multiple_of(spot * self.depth, self.depth), self.depth), :],
                         self.parts.at[self.spot if mine else spot], 16 + d, 16 + (self.spot if mine else spot), device)

    def l1(self, d, mine):
        y, device = self.line(d)
        return self.copy(self.lines.at[self.y], self.lines.at[self.y if mine else y], 4 + d,
                         4 + (self.y if mine else y), device)

    def p2(self, d, mine):
        spot, device = self.plane(d)
        rows = self.part(self.spot if mine else spot)
        return self.copy(self.total.at[rows, :], self.total.at[rows, :], 32 + d,
                         32 + (self.spot if mine else spot), device)

    def c2(self, mine):
        rows = self.own_half() if mine else self.other_half()
        return self.copy(self.total.at[rows, :], self.total.at[rows, :], 1, 1, self.sister)

    def s0(self):
        self.c1().start()

    def s1(self):
        self.c1().wait_recv()
        self.half[...] = self.half[...] + self.local[self.own_half(), :]
        each(1, PLANE, lambda d: self.p1(d, True).start())
        self.parts[self.spot] = self.half[pl.ds(pl.multiple_of(self.spot * self.depth, self.depth), self.depth), :]

    def s2(self):
        each(1, PLANE, lambda d: self.p1(d, False).wait_recv())
        acc = self.parts[0]
        for i in range(1, PLANE):
            acc = acc + self.parts[i]
        self.lines[self.y] = acc
        each(1, 4, lambda d: self.l1(d, True).start())

    def s3(self):
        each(1, 4, lambda d: self.l1(d, False).wait_recv())
        acc = (self.lines[0] + self.lines[1]) + (self.lines[2] + self.lines[3])
        self.total[self.part(self.spot), :] = acc
        each(1, PLANE, lambda d: self.p2(d, True).start())

    def s4(self):
        each(1, PLANE, lambda d: self.p2(d, False).wait_recv())
        self.c2(True).start()

    def s5(self):
        self.c2(False).wait_recv()

    def drain(self):
        self.c1().wait_send()
        each(1, PLANE, lambda d: self.p1(d, True).wait_send())
        each(1, 4, lambda d: self.l1(d, True).wait_send())
        each(1, PLANE, lambda d: self.p2(d, True).wait_send())
        self.c2(True).wait_send()


def reduce_scratch(rows):
    depth = rows // 2 // PLANE
    return [VMEM((rows // 2, K), F32), VMEM((PLANE, depth, K), F32), VMEM((4, depth, K), F32),
            pltpu.SemaphoreType.DMA((48,)), pltpu.SemaphoreType.DMA((48,))]


def factor_128(a, upper, inverse, hooks=None, base=0):
    size, n = 8, 16
    rows = lax.broadcasted_iota(jnp.int32, (size, 128), 0)
    lanes = lax.broadcasted_iota(jnp.int32, (size, 128), 1)
    depth = lax.broadcasted_iota(jnp.int32, (n, size, 128), 0)
    q = jnp.where(lanes[None] == rows[None] + size * depth, 1.0, 0.0).astype(F32)
    for kb in range(n):
        if hooks is not None and base + kb in hooks:
            hooks[base + kb]()
        at = size * kb
        own, own_q = a[0], q[0]
        a, q = a[1:], q[1:]
        stack = lambda x: jnp.broadcast_to(x[:, None, :], (size, size, 128))
        rest = n - 1 - kb
        r, s = stack(own), stack(own_q)
        cols = [stack(jnp.broadcast_to(own[:, at + j:at + j + 1], (size, 128))) for j in range(size)]
        side = [jnp.broadcast_to(a[:, :, at + k:at + k + 1], (rest, size, 128)) for k in range(size)] if rest else []
        m, rr, ss, pivot, root = [], [], [], [], []
        ut, wt = jnp.zeros((size, 128), F32), jnp.zeros((size, 128), F32)
        for k in range(size):
            d = cols[k][0]
            pivot.append(1.0 / d)
            rr.append(r[0]); ss.append(s[0])
            if k < size - 1:
                below = cols[k][1:]
                mk = below * pivot[k][None]
                m.append(mk)
                for j in range(k + 1, size):
                    cols[j] = cols[j][1:] if j == k + 1 and False else cols[j][1:] - mk * below[j - k - 1][None]
                r = r[1:] - mk * r[0][None]
                s = s[1:] - mk * s[0][None]
            rt = lax.rsqrt(d)
            ut = jnp.where(rows == k, rr[k] * rt, ut)
            wt = jnp.where(rows == k, ss[k] * rt, wt)
        z, zs = [None] * size, [None] * size
        for k in reversed(range(size)):
            zk, zsk = rr[k] * pivot[k], ss[k] * pivot[k]
            for j in range(k + 1, size):
                zk = zk - m[k][j - k - 1] * z[j]
                zsk = zsk - m[k][j - k - 1] * zs[j]
            z[k], zs[k] = zk, zsk
        if rest:
            for k in range(size):
                a = a - side[k] * z[k][None]
                q = q - side[k] * zs[k][None]
        upper[at:at + size, :] = jnp.where(lanes >= rows + at, ut, 0.0)
        inverse[at:at + size, :] = jnp.where(lanes <= rows + at, wt, 0.0)


def factor_256(a, upper, inverse, hooks=None):
    h = 128
    factor_128(a[:h, :h].reshape(16, 8, h), upper.at[:h, :h], inverse.at[:h, :h], hooks)
    w1 = inverse[:h, :h]
    low = nt(a[h:, :h], w1, HI)
    upper[:h, h:] = low.T
    upper[h:, :h] = jnp.zeros((h, h), F32)
    inverse[:h, h:] = jnp.zeros((h, h), F32)
    a[h:, h:] = a[h:, h:] - nt(low, low, HI)
    t = nn(low, w1, HI)
    factor_128(a[h:, h:].reshape(16, 8, h), upper.at[h:, h:], inverse.at[h:, h:], hooks, 16)
    inverse[h:, :h] = -nn(inverse[h:, h:], t, HI)


class Halo:
    def __init__(self, frames, tension, halo, tens_halo, send, recv):
        self.refs = frames, tension, halo, tens_halo, send, recv
        self.cable, self.seg = lax.axis_index("cable"), lax.axis_index("seg")

    def copies(self, side):
        frames, tension, halo, tens_halo, send, recv = self.refs
        nodes = frames.shape[0] // 4
        peer = self.seg + 1 if side == 0 else self.seg - 1
        return [
            pltpu.make_async_remote_copy(
                src_ref=frames.at[pl.ds(4 * (nodes - EDGE) if side == 0 else 0, 4 * EDGE), :], dst_ref=halo.at[side],
                send_sem=send.at[side], recv_sem=recv.at[side],
                device_id=(self.cable, peer), device_id_type=MESH),
            pltpu.make_async_remote_copy(
                src_ref=tension.at[:, pl.ds(nodes - 128 if side == 0 else 0, 128)], dst_ref=tens_halo.at[side],
                send_sem=send.at[2 + side], recv_sem=recv.at[2 + side],
                device_id=(self.cable, peer), device_id_type=MESH),
        ]

    def guarded(self, sends, act):
        for side in range(2):
            has_right, has_left = self.seg < N_SEG - 1, self.seg > 0
            here = (has_right, has_left) if sends else (has_left, has_right)

            @pl.when(here[side])
            def _():
                for copy in self.copies(side):
                    act(copy)

    def start(self):
        self.guarded(True, lambda copy: copy.start())

    def wait_recv(self):
        self.guarded(False, lambda copy: copy.wait_recv())

    def wait_send(self):
        self.guarded(True, lambda copy: copy.wait_send())

    def zero_ends(self):
        halo, tens_halo = self.refs[2:4]

        @pl.when(self.seg == 0)
        def _():
            halo[0] = jnp.zeros_like(halo[0])
            tens_halo[0] = jnp.zeros_like(tens_halo[0])

        @pl.when(self.seg == N_SEG - 1)
        def _():
            halo[1] = jnp.zeros_like(halo[1])
            tens_halo[1] = jnp.zeros_like(tens_halo[1])


def make_weights(seg, tens_halo, tens_rows, weights, steps):
    reach = SWEEPS
    full = (STRIPS, 128)
    sub = lax.broadcasted_iota(jnp.int32, full, 0)
    lane = lax.broadcasted_iota(jnp.int32, full, 1)
    low_out = jnp.logical_and(sub == 0, seg == 0)
    high_out = jnp.logical_and(sub == STRIPS - 1, seg == N_SEG - 1)
    for q in range(2):
        tens_rows[q, 7:8, :] = tens_halo[0, q:q + 1, :]
        tens_rows[q, 16:17, :] = tens_halo[1, q:q + 1, :]
        before, here, after = (tens_rows[q, 7 + i:15 + i, :] for i in range(3))

        def next_lane(x, y):
            return jnp.where(lane == 127, pltpu.roll(y, 127, 1), pltpu.roll(x, 127, 1))

        def prev_lane(x, y):
            return jnp.where(lane == 0, pltpu.roll(x, 1, 1), pltpu.roll(y, 1, 1))

        right = [0.5 * (before + next_lane(before, here)), 0.5 * (here + next_lane(here, after)),
                 0.5 * (after + next_lane(after, after))]
        left = [prev_lane(before, right[0]), prev_lane(right[0], right[1]), prev_lane(right[1], right[2])]
        for kind, rows in enumerate((left, right)):
            rows[0] = jnp.where(low_out, 0.0, rows[0])
            rows[2] = jnp.where(high_out, 0.0, rows[2])
            for step in range(steps):
                part, at = divmod(128 + step - reach, 128)
                weights[q, kind, step] = jnp.broadcast_to(rows[part][:, at:at + 1], full)


def relax(q, scale, padded, weights, solved32, solved, strip, block):
    reach = SWEEPS
    full = (STRIPS, 128)

    def advance(step, levels, coefs):
        lw, rw = weights[q, 0, step], weights[q, 1, step]
        total = lw + rw
        out = []
        for h in range(2):
            value = padded[pl.ds(4 * (EDGE - reach + step) + 2 * h + q, STRIPS, stride=4 * strip), :]
            inv = 1.0 / (1.0 + scale[h] * total)
            si = scale[h] * inv
            coefs[h].append((si * lw, si * rw, value * inv))
            levels[h][0].append(value)
            for k in range(1, SWEEPS + 1):
                below, above, own = coefs[h][-1 - k]
                value = own + (above * levels[h][k - 1][-1] + below * levels[h][k - 1][-3])
                levels[h][k].append(value)
            coefs[h][:] = coefs[h][-(SWEEPS + 1):]
            for k in range(SWEEPS + 1):
                levels[h][k][:] = levels[h][k][-2:] if k < SWEEPS else levels[h][k][-1:]
            out.append(levels[h][SWEEPS][-1])
        return out

    zero = jnp.zeros(full, F32)
    levels = [[[zero, zero] for _ in range(SWEEPS)] + [[zero]] for _ in range(2)]
    coefs = [[(zero, zero, zero)] * (SWEEPS + 1) for _ in range(2)]
    for step in range(2 * reach):
        advance(step, levels, coefs)
    unroll = 8

    def turn(i, carry):
        levels, coefs = carry
        levels = [[list(x) for x in lv] for lv in levels]
        coefs = [[tuple(x) for x in cf] for cf in coefs]
        for u in range(unroll):
            row = i * unroll + u
            out = advance(2 * reach + row, levels, coefs)
            for h in range(2):
                solved32[h, pl.ds(row, STRIPS, stride=strip), :] = out[h]
        return levels, coefs

    lax.fori_loop(0, strip // unroll, turn, (levels, coefs))

    def pack(b, _):
        rows = pl.ds(pl.multiple_of(b * block, block), block)
        for h in range(2):
            solved[b, q * block:(q + 1) * block, h * 128:(h + 1) * 128] = solved32[h, rows, :].astype(BF16)
        return 0

    lax.fori_loop(0, N_CABLE, pack, 0)


def main_kernel(rows_all, frames_in, tension_in, step_in, owner_in, basis_hbm, singular_in,
                factor, w1_out, w2_out, cross_out, snaps,
                frames, tension, step_index, owner, basis, singular, load_sem, padded, halo, tens_halo, tens_rows, weights, solved32, solved, scaled, rows32, basis_out, basis_in,
                snaps_in, a, inverse1, inverse2, local1, total1, local2, total2, half1, parts1, lines1, send1, recv1,
                half2, parts2, lines2, send2, recv2, halo_send, halo_recv, b_send, b_recv, s_send, s_recv):
    cable, seg = lax.axis_index("cable"), lax.axis_index("seg")
    nodes = frames_in.shape[0] // 4
    strip = nodes // STRIPS
    block = nodes // N_CABLE
    positions = 2 * N_CABLE
    scale_all = 1.0 / rows_all
    met = greet()
    loads = [pltpu.make_async_copy(src, dst, load_sem.at[i]) for i, (src, dst) in enumerate((
        (basis_hbm, basis), (singular_in, singular), (owner_in, owner), (frames_in, frames), (tension_in, tension),
        (step_in, step_index)))]
    for load in loads:
        load.start()

    for load in loads[:3]:
        load.wait()
    scaled[...] = (basis[...].astype(F32) * singular[...]).astype(BF16)
    pick = (lax.broadcasted_iota(jnp.int32, (positions, positions), 0) == owner[...]).astype(F32)
    pick_bf = pick.astype(BF16)
    unpick_bf = pick.T.astype(BF16)

    def by_streamer(n, _):
        rows = scaled[pl.ds(pl.multiple_of(n * positions, positions), positions), :]
        moved = nn(pick_bf, rows)
        for h in range(2):
            rows32[h, pl.ds(n, positions, stride=block), :] = moved[:, h * 128:(h + 1) * 128]
        return 0

    lax.fori_loop(0, block, by_streamer, 0, unroll=4)
    for h in range(2):
        basis_out[:, :, h * 128:(h + 1) * 128] = rows32[h].astype(BF16).reshape(N_CABLE, 2 * block, 128)
    for load in loads[3:]:
        load.wait()
    first = Reduce(local1, total1, half1, parts1, lines1, (send1, recv1))
    second = Reduce(local2, total2, half2, parts2, lines2, (send2, recv2))
    edges = Halo(frames, tension, halo, tens_halo, halo_send, halo_recv)
    edges.zero_ends()

    def exchange(d, out, into, q, send, recv, mine):
        peer = lax.rem(cable + d, N_CABLE)
        rows = pl.ds(q * block, block)
        return pltpu.make_async_remote_copy(
            src_ref=out.at[peer, rows, :], dst_ref=into.at[cable if mine else peer, rows, :], send_sem=send.at[q, d],
            recv_sem=recv.at[q, cable if mine else peer], device_id=(peer, seg), device_id_type=MESH)

    def basis_trip(d, mine):
        return exchange(d, basis_out, basis_in, 0, b_send, b_recv, mine)

    def snaps_trip(q, d, mine):
        return exchange(d, solved, snaps_in, q, s_send, s_recv, mine)

    def send_snaps(q):
        each(1, N_CABLE, lambda d: snaps_trip(q, d, True).start())
        snaps_in[cable, q * block:(q + 1) * block, :] = solved[cable, q * block:(q + 1) * block, :]

    def half(ref, q):
        return ref[:, q * block:(q + 1) * block, :].reshape(nodes, K)

    met()
    edges.start()
    each(1, N_CABLE, lambda d: basis_trip(d, True).start())
    local1[...] = tn(scaled[...], scaled[...])
    first.s0()
    basis_in[cable, 0:block, :] = basis_out[cable, 0:block, :]
    padded[4 * EDGE:4 * (EDGE + nodes), :] = frames[...].astype(F32)
    for q in range(2):
        for s in range(STRIPS):
            tens_rows[q, 8 + s:9 + s, :] = tension[q:q + 1, s * strip:(s + 1) * strip]
    first.s1()
    edges.wait_recv()
    padded[0:4 * EDGE, :] = halo[0].astype(F32)
    padded[4 * (EDGE + nodes):, :] = halo[1].astype(F32)
    make_weights(seg, tens_halo, tens_rows, weights, strip + 2 * SWEEPS)
    stiff = DRAG_RATE * (1.0 + step_index[...].astype(F32))
    scale = [jnp.broadcast_to(stiff[:, h * 128:(h + 1) * 128], (STRIPS, 128)) for h in range(2)]
    relax(1, scale, padded, weights, solved32, solved, strip, block)
    send_snaps(1)
    first.s2()
    relax(0, scale, padded, weights, solved32, solved, strip, block)
    flat = solved[...].reshape(2 * nodes, SNAP)
    local2[K:, :] = tn(flat, flat)
    first.s3()
    each(1, N_CABLE, lambda d: basis_trip(d, False).wait_recv())
    local2[:K, :] = tn(half(solved, 0), half(basis_in, 0))
    each(1, N_CABLE, lambda d: snaps_trip(1, d, False).wait_recv())
    local2[:K, :] += tn(half(snaps_in, 1), half(basis_out, 1))
    second.s0()
    second.s1()
    first.s4()
    first.s5()
    a[...] = total1[...] * scale_all

    factor_256(a, factor.at[:K, :K], inverse1, {12: second.s2, 24: second.s3})
    w1 = inverse1[...]
    w1_out[...] = w1.astype(BF16)
    factor[K:, :K] = jnp.zeros((K, K), F32)
    second.s4()
    send_snaps(0)
    second.s5()
    low = nt(total2[:K, :] * scale_all, w1, HI)
    factor[:K, K:] = low.T
    a[...] = total2[K:, :] * scale_all - nt(low, low, HI)
    t = nn(low, w1, HI)
    factor_256(a, factor.at[K:, K:], inverse2)
    w2 = inverse2[...]
    w2_out[...] = w2.astype(BF16)
    cross_out[...] = (-nn(w2, t, HI)).astype(BF16)
    each(1, N_CABLE, lambda d: snaps_trip(0, d, False).wait_recv())

    for h in range(2):
        rows32[h] = snaps_in[:, :, h * 128:(h + 1) * 128].astype(F32).reshape(positions * block, 128)

    def by_position(n, _):
        rows = jnp.concatenate([rows32[h, pl.ds(n, positions, stride=block), :] for h in range(2)], axis=1)
        snaps[pl.ds(pl.multiple_of(n * positions, positions), positions), :] = (
            nn(unpick_bf, rows.astype(BF16)).astype(BF16))
        return 0

    lax.fori_loop(0, block, by_position, 0, unroll=4)
    first.drain()
    second.drain()
    edges.wait_send()
    each(1, N_CABLE, lambda d: basis_trip(d, True).wait_send())
    for q in range(2):
        each(1, N_CABLE, lambda d: snaps_trip(q, d, True).wait_send())


def exchange_and_factor(rows_all, frames, tension, step_index, owner_map, basis, singular):
    nodes = frames.shape[0] // 4
    rows = basis.shape[0]
    block = nodes // N_CABLE
    steps = nodes // STRIPS + 2 * SWEEPS
    dma = pltpu.SemaphoreType.DMA
    square = jax.ShapeDtypeStruct((K, K), BF16)
    return pl.pallas_call(
        lambda *refs: main_kernel(rows_all, *refs),
        out_shape=[jax.ShapeDtypeStruct((2 * K, 2 * K), F32), square, square, square,
                   jax.ShapeDtypeStruct((rows, SNAP), BF16)],
        in_specs=[pl.BlockSpec(memory_space=pltpu.HBM)] * 6,
        out_specs=[vmem_spec()] * 5,
        scratch_shapes=[
            *[VMEM(x.shape, x.dtype) for x in (frames, tension, step_index, owner_map, basis, singular)],
            dma((6,)),
            VMEM((4 * (nodes + 2 * EDGE), 128), F32),
            VMEM((2, 4 * EDGE, 128), BF16),
            VMEM((2, 2, 128), F32),
            VMEM((2, 24, 128), F32),
            VMEM((2, 2, steps, STRIPS, 128), F32),
            VMEM((2, nodes, 128), F32),
            VMEM((N_CABLE, 2 * block, SNAP), BF16),
            VMEM((rows, K), BF16),
            VMEM((2, rows, 128), F32),
            VMEM((N_CABLE, 2 * block, K), BF16),
            VMEM((N_CABLE, 2 * block, K), BF16),
            VMEM((N_CABLE, 2 * block, SNAP), BF16),
            VMEM((K, K), F32),
            VMEM((K, K), F32),
            VMEM((K, K), F32),
            VMEM((K, K), F32),
            VMEM((K, K), F32),
            VMEM((2 * K, K), F32),
            VMEM((2 * K, K), F32),
            *reduce_scratch(K), *reduce_scratch(2 * K),
            dma((4,)), dma((4,)), *[dma((2, N_CABLE))] * 4,
        ],
        compiler_params=pltpu.CompilerParams(collective_id=0, has_side_effects=True, vmem_limit_bytes=48 * 2**20),
        name="relax_exchange_factor",
    )(frames, tension, step_index, owner_map, basis, singular)


def rotate_kernel(factor_in, w1, w2, cross, basis, singular, snaps, factor, new_basis, sem):
    copy = pltpu.make_async_copy(factor_in, factor, sem)
    copy.start()
    scaled = (basis[...].astype(F32) * singular[...]).astype(BF16)
    new_basis[:, :K] = nt(scaled, w1[...]).astype(BF16)
    new_basis[:, K:] = (nt(scaled, cross[...]) + nt(snaps[...], w2[...])).astype(BF16)
    copy.wait()


def rotate(factor, w1, w2, cross, basis, singular, snaps):
    rows, width = basis.shape[0], 2 * K
    anywhere = pl.BlockSpec(memory_space=pl.ANY)
    return pl.pallas_call(
        rotate_kernel,
        out_shape=[jax.ShapeDtypeStruct((width, width), F32), jax.ShapeDtypeStruct((rows, width), BF16)],
        in_specs=[anywhere] + [vmem_spec()] * 6,
        out_specs=[anywhere, vmem_spec()],
        scratch_shapes=[pltpu.SemaphoreType.DMA],
        compiler_params=pltpu.CompilerParams(vmem_limit_bytes=40 * 2**20),
        name="rotate",
    )(factor, w1, w2, cross, basis, singular, snaps)


def body(frames, tension, step_index, owner_map, old_basis, singular):
    nodes = frames.shape[0]
    basis = old_basis.reshape(-1, K)
    gain = singular[None, :]
    rows_all = basis.shape[0] * lax.axis_size("cable") * lax.axis_size("seg")
    lines = frames.reshape(nodes, 2, 2, 128).transpose(0, 2, 1, 3).reshape(4 * nodes, 128)
    operands = (pltpu.with_memory_space_constraint(value, pltpu.HBM) for value in (
        lines, tension.T, step_index[None, :], owner_map[None, :], basis, gain))
    factor, w1, w2, cross, snaps = exchange_and_factor(rows_all, *operands)
    factor, rotated = rotate(factor, w1, w2, cross, basis, gain, snaps)
    return factor, rotated.reshape(old_basis.shape[:3] + (2 * K,))


def solution(mesh):
    return jax.shard_map(
        body,
        mesh=mesh,
        in_specs=(P("seg", "cable", None), P("seg", "cable"), P(), P(), P("seg", "cable", None, None), P()),
        out_specs=(P(), P("seg", "cable", None, None)),
        check_vma=False,
    )
```

```python
import jax
import jax.numpy as jnp
from jax import lax
from jax.experimental import pallas as pl
from jax.experimental.pallas import tpu as pltpu
from jax.sharding import PartitionSpec as P

K = 256
SNAP = 256
SWEEPS = 6
DRAG_RATE = 0.1
STRIPS = 8
EDGE = 16
MESH = pl.DeviceIdType.MESH
HI = lax.Precision.HIGHEST
VMEM = pltpu.VMEM
F32 = jnp.float32
BF16 = jnp.bfloat16


def vmem_spec():
    return pl.BlockSpec(memory_space=pltpu.VMEM)


def nt(a, b, precision=None):
    return lax.dot_general(a, b, (((1,), (1,)), ((), ())), precision=precision, preferred_element_type=F32)


def nn(a, b, precision=None):
    return lax.dot_general(a, b, (((1,), (0,)), ((), ())), precision=precision, preferred_element_type=F32)


def tn(a, b, precision=None):
    return lax.dot_general(a, b, (((0,), (0,)), ((), ())), precision=precision, preferred_element_type=F32)


def place():
    cable, seg = lax.axis_index("cable"), lax.axis_index("seg")
    return cable, seg, cable // 8, lax.rem(cable // 4, 2), lax.rem(cable, 4), seg // 2, lax.rem(seg, 2)


N_CABLE = 32
N_SEG = 4
PLANE = 16


def each(first, last, act):
    def turn(d, _):
        act(d)
        return 0
    lax.fori_loop(first, last, turn, 0)


def greet():
    cable, seg, x, y_lo, z, y_hi, core = place()
    barrier = pltpu.get_barrier_semaphore()

    def hail(device):
        pl.semaphore_signal(barrier, inc=1, device_id=device, device_id_type=MESH)

    each(1, N_CABLE, lambda d: hail((lax.rem(cable + d, N_CABLE), seg)))
    each(1, N_SEG, lambda d: hail((cable, lax.rem(seg + d, N_SEG))))
    hail((x * 8 + (1 - y_lo) * 4 + z, (1 - y_hi) * 2 + core))
    return lambda: pl.semaphore_wait(barrier, N_CABLE + N_SEG - 1)


class Reduce:
    def __init__(self, local, total, half, parts, lines, sems):
        self.local, self.total, self.half, self.parts, self.lines = local, total, half, parts, lines
        self.send, self.recv = sems
        self.rows = local.shape[0]
        self.depth = self.rows // 2 // PLANE
        self.cable, self.seg, self.x, self.y_lo, self.z, self.y_hi, self.core = place()
        self.spot = self.x * 4 + self.z
        self.y = self.y_hi * 2 + self.y_lo
        self.sister = (self.cable, self.y_hi * 2 + 1 - self.core)

    def copy(self, src, dst, slot, landing, device):
        return pltpu.make_async_remote_copy(
            src_ref=src, dst_ref=dst, send_sem=self.send.at[slot], recv_sem=self.recv.at[landing],
            device_id=device, device_id_type=MESH)

    def plane(self, d):
        spot = lax.rem(self.spot + d, PLANE)
        return spot, ((spot // 4) * 8 + self.y_lo * 4 + lax.rem(spot, 4), self.seg)

    def line(self, d):
        y = lax.rem(self.y + d, 4)
        return y, (self.x * 8 + lax.rem(y, 2) * 4 + self.z, (y // 2) * 2 + self.core)

    def part(self, spot):
        at = self.core * (self.rows // 2) + spot * self.depth
        return pl.ds(pl.multiple_of(at, self.depth), self.depth)

    def own_half(self):
        return pl.ds(pl.multiple_of(self.core * (self.rows // 2), self.rows // 2), self.rows // 2)

    def other_half(self):
        return pl.ds(pl.multiple_of((1 - self.core) * (self.rows // 2), self.rows // 2), self.rows // 2)

    def c1(self):
        return self.copy(self.local.at[self.other_half(), :], self.half, 0, 0, self.sister)

    def p1(self, d, mine):
        spot, device = self.plane(d)
        return self.copy(self.half.at[pl.ds(pl.multiple_of(spot * self.depth, self.depth), self.depth), :],
                         self.parts.at[self.spot if mine else spot], 16 + d, 16 + (self.spot if mine else spot), device)

    def l1(self, d, mine):
        y, device = self.line(d)
        return self.copy(self.lines.at[self.y], self.lines.at[self.y if mine else y], 4 + d,
                         4 + (self.y if mine else y), device)

    def p2(self, d, mine):
        spot, device = self.plane(d)
        rows = self.part(self.spot if mine else spot)
        return self.copy(self.total.at[rows, :], self.total.at[rows, :], 32 + d,
                         32 + (self.spot if mine else spot), device)

    def c2(self, mine):
        rows = self.own_half() if mine else self.other_half()
        return self.copy(self.total.at[rows, :], self.total.at[rows, :], 1, 1, self.sister)

    def s0(self):
        self.c1().start()

    def s1(self):
        self.c1().wait_recv()
        self.half[...] = self.half[...] + self.local[self.own_half(), :]
        each(1, PLANE, lambda d: self.p1(d, True).start())
        self.parts[self.spot] = self.half[pl.ds(pl.multiple_of(self.spot * self.depth, self.depth), self.depth), :]

    def s2(self):
        each(1, PLANE, lambda d: self.p1(d, False).wait_recv())
        acc = self.parts[0]
        for i in range(1, PLANE):
            acc = acc + self.parts[i]
        self.lines[self.y] = acc
        each(1, 4, lambda d: self.l1(d, True).start())

    def s3(self):
        each(1, 4, lambda d: self.l1(d, False).wait_recv())
        acc = (self.lines[0] + self.lines[1]) + (self.lines[2] + self.lines[3])
        self.total[self.part(self.spot), :] = acc
        each(1, PLANE, lambda d: self.p2(d, True).start())

    def s4(self):
        each(1, PLANE, lambda d: self.p2(d, False).wait_recv())
        self.c2(True).start()

    def s5(self):
        self.c2(False).wait_recv()

    def drain(self):
        self.c1().wait_send()
        each(1, PLANE, lambda d: self.p1(d, True).wait_send())
        each(1, 4, lambda d: self.l1(d, True).wait_send())
        each(1, PLANE, lambda d: self.p2(d, True).wait_send())
        self.c2(True).wait_send()


def reduce_scratch(rows):
    depth = rows // 2 // PLANE
    return [VMEM((rows // 2, K), F32), VMEM((PLANE, depth, K), F32), VMEM((4, depth, K), F32),
            pltpu.SemaphoreType.DMA((48,)), pltpu.SemaphoreType.DMA((48,))]


def factor_128(a, upper, inverse, hooks=None, base=0):
    size, n = 8, 16
    tile = (size, 128)
    rows = lax.broadcasted_iota(jnp.int32, tile, 0)
    lanes = lax.broadcasted_iota(jnp.int32, tile, 1)
    depth = lax.broadcasted_iota(jnp.int32, (n, size, 128), 0)
    q = jnp.where(lanes[None] == rows[None] + size * depth, 1.0, 0.0).astype(F32)

    def over_lanes(x, j):
        return jnp.broadcast_to(x[..., j:j + 1], x.shape)

    def over_rows(x):
        return jnp.broadcast_to(x[:, None, :], (x.shape[0], size, 128))

    for kb in range(n):
        if hooks is not None and base + kb in hooks:
            hooks[base + kb]()
        at = size * kb
        rest = n - 1 - kb
        own, own_q, a, q = a[0], q[0], a[1:], q[1:]
        r, s = over_rows(own), over_rows(own_q)
        cols = [over_rows(over_lanes(own, at + j)[j:]) for j in range(size)]
        if rest:
            near = [over_lanes(a[0], at + k) for k in range(size)]
            next_a, next_q = a[0], q[0]
        far = [over_lanes(a[1:], at + k) for k in range(size)] if rest > 1 else []
        m, rr, ss, pivot = [], [], [], []
        ut, wt = jnp.zeros(tile, F32), jnp.zeros(tile, F32)
        for k in range(size):
            d = cols[k][0]
            pivot.append(1.0 / d)
            rr.append(r[0])
            ss.append(s[0])
            if rest:
                scaled = near[k] * pivot[k]
                next_a = next_a - scaled * r[0]
                next_q = next_q - scaled * s[0]
                for j in range(k + 1, size):
                    near[j] = near[j] - scaled * cols[k][j - k]
            if k < size - 1:
                below = cols[k][1:]
                m.append(below * pivot[k][None])
                for j in range(k + 1, size):
                    cols[j] = cols[j] - m[k][j - k - 1:] * below[j - k - 1][None]
                r = r[1:] - m[k] * r[0][None]
                s = s[1:] - m[k] * s[0][None]
            root = lax.rsqrt(d)
            ut = jnp.where(rows == k, rr[k] * root, ut)
            wt = jnp.where(rows == k, ss[k] * root, wt)
        if rest > 1:
            z, zs = [None] * size, [None] * size
            for k in reversed(range(size)):
                zk, zsk = rr[k] * pivot[k], ss[k] * pivot[k]
                for j in range(k + 1, size):
                    zk = zk - m[k][j - k - 1] * z[j]
                    zsk = zsk - m[k][j - k - 1] * zs[j]
                z[k], zs[k] = zk, zsk
            far_a, far_q = a[1:], q[1:]
            for k in range(size):
                far_a = far_a - far[k] * z[k][None]
                far_q = far_q - far[k] * zs[k][None]
            a = jnp.concatenate([next_a[None], far_a])
            q = jnp.concatenate([next_q[None], far_q])
        elif rest:
            a, q = next_a[None], next_q[None]
        upper[at:at + size, :] = jnp.where(lanes >= rows + at, ut, 0.0)
        inverse[at:at + size, :] = jnp.where(lanes <= rows + at, wt, 0.0)


def factor_256(a, upper, inverse, hooks=None):
    h = 128
    factor_128(a[:h, :h].reshape(16, 8, h), upper.at[:h, :h], inverse.at[:h, :h], hooks)
    w1 = inverse[:h, :h]
    low = nt(a[h:, :h], w1, HI)
    upper[:h, h:] = low.T
    upper[h:, :h] = jnp.zeros((h, h), F32)
    inverse[:h, h:] = jnp.zeros((h, h), F32)
    a[h:, h:] = a[h:, h:] - nt(low, low, HI)
    t = nn(low, w1, HI)
    factor_128(a[h:, h:].reshape(16, 8, h), upper.at[h:, h:], inverse.at[h:, h:], hooks, 16)
    inverse[h:, :h] = -nn(inverse[h:, h:], t, HI)


class Halo:
    def __init__(self, frames, tension, halo, tens_halo, send, recv):
        self.refs = frames, tension, halo, tens_halo, send, recv
        self.cable, self.seg = lax.axis_index("cable"), lax.axis_index("seg")

    def copies(self, side):
        frames, tension, halo, tens_halo, send, recv = self.refs
        nodes = frames.shape[0] // 4
        peer = self.seg + 1 if side == 0 else self.seg - 1
        return [
            pltpu.make_async_remote_copy(
                src_ref=frames.at[pl.ds(4 * (nodes - EDGE) if side == 0 else 0, 4 * EDGE), :], dst_ref=halo.at[side],
                send_sem=send.at[side], recv_sem=recv.at[side],
                device_id=(self.cable, peer), device_id_type=MESH),
            pltpu.make_async_remote_copy(
                src_ref=tension.at[:, pl.ds(nodes - 128 if side == 0 else 0, 128)], dst_ref=tens_halo.at[side],
                send_sem=send.at[2 + side], recv_sem=recv.at[2 + side],
                device_id=(self.cable, peer), device_id_type=MESH),
        ]

    def guarded(self, sends, act):
        for side in range(2):
            has_right, has_left = self.seg < N_SEG - 1, self.seg > 0
            here = (has_right, has_left) if sends else (has_left, has_right)

            @pl.when(here[side])
            def _():
                for copy in self.copies(side):
                    act(copy)

    def start(self):
        self.guarded(True, lambda copy: copy.start())

    def wait_recv(self):
        self.guarded(False, lambda copy: copy.wait_recv())

    def wait_send(self):
        self.guarded(True, lambda copy: copy.wait_send())

    def zero_ends(self):
        halo, tens_halo = self.refs[2:4]

        @pl.when(self.seg == 0)
        def _():
            halo[0] = jnp.zeros_like(halo[0])
            tens_halo[0] = jnp.zeros_like(tens_halo[0])

        @pl.when(self.seg == N_SEG - 1)
        def _():
            halo[1] = jnp.zeros_like(halo[1])
            tens_halo[1] = jnp.zeros_like(tens_halo[1])


def make_weights(seg, tens_halo, tens_rows, weights, steps):
    reach = SWEEPS
    full = (STRIPS, 128)
    sub = lax.broadcasted_iota(jnp.int32, full, 0)
    lane = lax.broadcasted_iota(jnp.int32, full, 1)
    low_out = jnp.logical_and(sub == 0, seg == 0)
    high_out = jnp.logical_and(sub == STRIPS - 1, seg == N_SEG - 1)
    for q in range(2):
        tens_rows[q, 7:8, :] = tens_halo[0, q:q + 1, :]
        tens_rows[q, 16:17, :] = tens_halo[1, q:q + 1, :]
        before, here, after = (tens_rows[q, 7 + i:15 + i, :] for i in range(3))

        def next_lane(x, y):
            return jnp.where(lane == 127, pltpu.roll(y, 127, 1), pltpu.roll(x, 127, 1))

        def prev_lane(x, y):
            return jnp.where(lane == 0, pltpu.roll(x, 1, 1), pltpu.roll(y, 1, 1))

        right = [0.5 * (before + next_lane(before, here)), 0.5 * (here + next_lane(here, after)),
                 0.5 * (after + next_lane(after, after))]
        left = [prev_lane(before, right[0]), prev_lane(right[0], right[1]), prev_lane(right[1], right[2])]
        for kind, rows in enumerate((left, right)):
            rows[0] = jnp.where(low_out, 0.0, rows[0])
            rows[2] = jnp.where(high_out, 0.0, rows[2])
            for step in range(steps):
                part, at = divmod(128 + step - reach, 128)
                weights[q, kind, step] = jnp.broadcast_to(rows[part][:, at:at + 1], full)


def relax(q, scale, padded, weights, solved32, solved, strip, block):
    reach = SWEEPS
    full = (STRIPS, 128)

    def advance(step, levels, coefs):
        lw, rw = weights[q, 0, step], weights[q, 1, step]
        total = lw + rw
        out = []
        for h in range(2):
            value = padded[pl.ds(4 * (EDGE - reach + step) + 2 * h + q, STRIPS, stride=4 * strip), :]
            inv = 1.0 / (1.0 + scale[h] * total)
            si = scale[h] * inv
            coefs[h].append((si * lw, si * rw, value * inv))
            levels[h][0].append(value)
            for k in range(1, SWEEPS + 1):
                below, above, own = coefs[h][-1 - k]
                value = own + (above * levels[h][k - 1][-1] + below * levels[h][k - 1][-3])
                levels[h][k].append(value)
            coefs[h][:] = coefs[h][-(SWEEPS + 1):]
            for k in range(SWEEPS + 1):
                levels[h][k][:] = levels[h][k][-2:] if k < SWEEPS else levels[h][k][-1:]
            out.append(levels[h][SWEEPS][-1])
        return out

    zero = jnp.zeros(full, F32)
    levels = [[[zero, zero] for _ in range(SWEEPS)] + [[zero]] for _ in range(2)]
    coefs = [[(zero, zero, zero)] * (SWEEPS + 1) for _ in range(2)]
    for step in range(2 * reach):
        advance(step, levels, coefs)
    unroll = 8

    def turn(i, carry):
        levels, coefs = carry
        levels = [[list(x) for x in lv] for lv in levels]
        coefs = [[tuple(x) for x in cf] for cf in coefs]
        for u in range(unroll):
            row = i * unroll + u
            out = advance(2 * reach + row, levels, coefs)
            for h in range(2):
                solved32[h, pl.ds(row, STRIPS, stride=strip), :] = out[h]
        return levels, coefs

    lax.fori_loop(0, strip // unroll, turn, (levels, coefs))

    def pack(b, _):
        rows = pl.ds(pl.multiple_of(b * block, block), block)
        for h in range(2):
            solved[q, b, :, h * 128:(h + 1) * 128] = solved32[h, rows, :].astype(BF16)
        return 0

    lax.fori_loop(0, N_CABLE, pack, 0)


def main_kernel(rows_all, frames_in, tension_in, step_in, owner_in, basis_hbm, singular_in,
                factor, w1_out, w2_out, cross_out, snaps, scaled,
                frames, tension, step_index, owner, basis, singular, load_sem, padded, halo, tens_halo, tens_rows, weights, solved32, solved, rows32, basis_out, basis_in,
                snaps_in, a, inverse1, inverse2, local1, total1, local2, total2, half1, parts1, lines1, send1, recv1,
                half2, parts2, lines2, send2, recv2, halo_send, halo_recv, b_send, b_recv, s_send, s_recv):
    cable, seg = lax.axis_index("cable"), lax.axis_index("seg")
    nodes = frames_in.shape[0] // 4
    strip = nodes // STRIPS
    block = nodes // N_CABLE
    positions = 2 * N_CABLE
    scale_all = 1.0 / rows_all
    met = greet()
    loads = [pltpu.make_async_copy(src, dst, load_sem.at[i]) for i, (src, dst) in enumerate((
        (basis_hbm, basis), (singular_in, singular), (owner_in, owner), (frames_in, frames), (tension_in, tension),
        (step_in, step_index)))]
    for load in loads:
        load.start()

    for load in loads[:3]:
        load.wait()
    scaled[...] = (basis[...].astype(F32) * singular[...]).astype(BF16)
    line = lax.broadcasted_iota(jnp.int32, (positions, positions), 0)
    pick = (2 * lax.rem(line, N_CABLE) + line // N_CABLE == owner[...]).astype(F32)
    pick_bf = pick.astype(BF16)

    def by_streamer(q):
        def turn(n, _):
            rows = scaled[pl.ds(pl.multiple_of(n * positions, positions), positions), :]
            moved = nn(pick_bf[q * N_CABLE:(q + 1) * N_CABLE], rows)
            for h in range(2):
                rows32[h, pl.ds(q * nodes + n, N_CABLE, stride=block), :] = moved[:, h * 128:(h + 1) * 128]
            return 0

        lax.fori_loop(0, block, turn, 0, unroll=8)
        for h in range(2):
            basis_out[q, :, :, h * 128:(h + 1) * 128] = (
                rows32[h, q * nodes:(q + 1) * nodes, :].astype(BF16).reshape(N_CABLE, block, 128))

    by_streamer(0)
    for load in loads[3:]:
        load.wait()
    first = Reduce(local1, total1, half1, parts1, lines1, (send1, recv1))
    second = Reduce(local2, total2, half2, parts2, lines2, (send2, recv2))
    edges = Halo(frames, tension, halo, tens_halo, halo_send, halo_recv)
    edges.zero_ends()

    def exchange(d, out, into, q, send, recv, mine):
        peer = lax.rem(cable + d, N_CABLE)
        return pltpu.make_async_remote_copy(
            src_ref=out.at[q, peer], dst_ref=into.at[q, cable if mine else peer], send_sem=send.at[q, d],
            recv_sem=recv.at[q, cable if mine else peer], device_id=(peer, seg), device_id_type=MESH)

    def basis_trip(d, mine):
        return exchange(d, basis_out, basis_in, 0, b_send, b_recv, mine)

    def snaps_trip(q, d, mine):
        return exchange(d, solved, snaps_in, q, s_send, s_recv, mine)

    def send_snaps(q):
        each(1, N_CABLE, lambda d: snaps_trip(q, d, True).start())
        snaps_in[q, cable] = solved[q, cable]

    def half(ref, q):
        return ref[q].reshape(nodes, K)

    met()
    edges.start()
    each(1, N_CABLE, lambda d: basis_trip(d, True).start())
    local1[...] = tn(scaled[...], scaled[...])
    first.s0()
    basis_in[0, cable] = basis_out[0, cable]
    padded[4 * EDGE:4 * (EDGE + nodes), :] = frames[...].astype(F32)
    for q in range(2):
        for s in range(STRIPS):
            tens_rows[q, 8 + s:9 + s, :] = tension[q:q + 1, s * strip:(s + 1) * strip]
    first.s1()
    by_streamer(1)
    edges.wait_recv()
    padded[0:4 * EDGE, :] = halo[0].astype(F32)
    padded[4 * (EDGE + nodes):, :] = halo[1].astype(F32)
    make_weights(seg, tens_halo, tens_rows, weights, strip + 2 * SWEEPS)
    stiff = DRAG_RATE * (1.0 + step_index[...].astype(F32))
    scale = [jnp.broadcast_to(stiff[:, h * 128:(h + 1) * 128], (STRIPS, 128)) for h in range(2)]
    relax(1, scale, padded, weights, solved32, solved, strip, block)
    first.s2()
    send_snaps(1)
    relax(0, scale, padded, weights, solved32, solved, strip, block)
    flat = solved[...].reshape(2 * nodes, SNAP)
    local2[K:, :] = tn(flat, flat)
    first.s3()
    each(1, N_CABLE, lambda d: basis_trip(d, False).wait_recv())
    local2[:K, :] = tn(half(solved, 0), half(basis_in, 0))
    each(1, N_CABLE, lambda d: snaps_trip(1, d, False).wait_recv())
    local2[:K, :] += tn(half(snaps_in, 1), half(basis_out, 1))
    second.s0()
    second.s1()
    first.s4()
    first.s5()
    a[...] = total1[...] * scale_all

    factor_256(a, factor.at[:K, :K], inverse1, {12: second.s2, 24: second.s3})
    w1 = inverse1[...]
    w1_out[...] = w1.astype(BF16)
    factor[K:, :K] = jnp.zeros((K, K), F32)
    second.s4()
    send_snaps(0)
    second.s5()
    low = nt(total2[:K, :] * scale_all, w1, HI)
    factor[:K, K:] = low.T
    a[...] = total2[K:, :] * scale_all - nt(low, low, HI)
    t = nn(low, w1, HI)
    factor_256(a, factor.at[K:, K:], inverse2)
    w2 = inverse2[...]
    w2_out[...] = w2.astype(BF16)
    cross_out[...] = (-nn(w2, t, HI)).astype(BF16)
    each(1, N_CABLE, lambda d: snaps_trip(0, d, False).wait_recv())

    for h in range(2):
        rows32[h] = snaps_in[:, :, :, h * 128:(h + 1) * 128].astype(F32).reshape(positions * block, 128)

    unpick_bf = pick.T.astype(BF16)

    def by_position(n, _):
        rows = jnp.concatenate([rows32[h, pl.ds(n, positions, stride=block), :] for h in range(2)], axis=1)
        snaps[pl.ds(pl.multiple_of(n * positions, positions), positions), :] = (
            nn(unpick_bf, rows.astype(BF16)).astype(BF16))
        return 0

    lax.fori_loop(0, block, by_position, 0, unroll=8)
    first.drain()
    second.drain()
    edges.wait_send()
    each(1, N_CABLE, lambda d: basis_trip(d, True).wait_send())
    for q in range(2):
        each(1, N_CABLE, lambda d: snaps_trip(q, d, True).wait_send())


def exchange_and_factor(rows_all, frames, tension, step_index, owner_map, basis, singular):
    nodes = frames.shape[0] // 4
    rows = basis.shape[0]
    block = nodes // N_CABLE
    steps = nodes // STRIPS + 2 * SWEEPS
    dma = pltpu.SemaphoreType.DMA
    square = jax.ShapeDtypeStruct((K, K), BF16)
    return pl.pallas_call(
        lambda *refs: main_kernel(rows_all, *refs),
        out_shape=[jax.ShapeDtypeStruct((2 * K, 2 * K), F32), square, square, square,
                   jax.ShapeDtypeStruct((rows, SNAP), BF16), jax.ShapeDtypeStruct((rows, K), BF16)],
        in_specs=[pl.BlockSpec(memory_space=pltpu.HBM)] * 6,
        out_specs=[vmem_spec()] * 6,
        scratch_shapes=[
            *[VMEM(x.shape, x.dtype) for x in (frames, tension, step_index, owner_map, basis, singular)],
            dma((6,)),
            VMEM((4 * (nodes + 2 * EDGE), 128), F32),
            VMEM((2, 4 * EDGE, 128), BF16),
            VMEM((2, 2, 128), F32),
            VMEM((2, 24, 128), F32),
            VMEM((2, 2, steps, STRIPS, 128), F32),
            VMEM((2, nodes, 128), F32),
            VMEM((2, N_CABLE, block, SNAP), BF16),
            VMEM((2, rows, 128), F32),
            VMEM((2, N_CABLE, block, K), BF16),
            VMEM((2, N_CABLE, block, K), BF16),
            VMEM((2, N_CABLE, block, SNAP), BF16),
            VMEM((K, K), F32),
            VMEM((K, K), F32),
            VMEM((K, K), F32),
            VMEM((K, K), F32),
            VMEM((K, K), F32),
            VMEM((2 * K, K), F32),
            VMEM((2 * K, K), F32),
            *reduce_scratch(K), *reduce_scratch(2 * K),
            dma((4,)), dma((4,)), *[dma((2, N_CABLE))] * 4,
        ],
        compiler_params=pltpu.CompilerParams(collective_id=0, has_side_effects=True, vmem_limit_bytes=48 * 2**20),
        name="relax_exchange_factor",
    )(frames, tension, step_index, owner_map, basis, singular)


def rotate_kernel(factor_in, w1, w2, cross, scaled, snaps, factor, new_basis, sem):
    copy = pltpu.make_async_copy(factor_in, factor, sem)
    copy.start()
    new_basis[:, :K] = nt(scaled[...], w1[...]).astype(BF16)
    new_basis[:, K:] = (nt(scaled[...], cross[...]) + nt(snaps[...], w2[...])).astype(BF16)
    copy.wait()


def rotate(factor, w1, w2, cross, scaled, snaps):
    rows, width = scaled.shape[0], 2 * K
    return pl.pallas_call(
        rotate_kernel,
        out_shape=[jax.ShapeDtypeStruct((width, width), F32), jax.ShapeDtypeStruct((rows, width), BF16)],
        in_specs=[vmem_spec()] * 6,
        out_specs=[pl.BlockSpec(memory_space=pltpu.HBM), vmem_spec()],
        scratch_shapes=[pltpu.SemaphoreType.DMA],
        compiler_params=pltpu.CompilerParams(vmem_limit_bytes=40 * 2**20),
        name="rotate",
    )(factor, w1, w2, cross, scaled, snaps)


def body(frames, tension, step_index, owner_map, old_basis, singular):
    nodes = frames.shape[0]
    basis = old_basis.reshape(-1, K)
    gain = singular[None, :]
    rows_all = basis.shape[0] * lax.axis_size("cable") * lax.axis_size("seg")
    lines = frames.reshape(nodes, 2, 2, 128).transpose(0, 2, 1, 3).reshape(4 * nodes, 128)
    operands = (pltpu.with_memory_space_constraint(value, pltpu.HBM) for value in (
        lines, tension.T, step_index[None, :], owner_map[None, :], basis, gain))
    factor, w1, w2, cross, snaps, scaled = exchange_and_factor(rows_all, *operands)
    factor, rotated = rotate(factor, w1, w2, cross, scaled, snaps)
    return factor, rotated.reshape(old_basis.shape[:3] + (2 * K,))


def solution(mesh):
    return jax.shard_map(
        body,
        mesh=mesh,
        in_specs=(P("seg", "cable", None), P("seg", "cable"), P(), P(), P("seg", "cable", None, None), P()),
        out_specs=(P(), P("seg", "cable", None, None)),
        check_vma=False,
    )
```

```python
import jax
import jax.numpy as jnp
from jax import lax
from jax.experimental import pallas as pl
from jax.experimental.pallas import tpu as pltpu
from jax.sharding import PartitionSpec as P

K = 256
SNAP = 256
SWEEPS = 6
DRAG_RATE = 0.1
STRIPS = 8
EDGE = 16
MESH = pl.DeviceIdType.MESH
HI = lax.Precision.HIGHEST
VMEM = pltpu.VMEM
F32 = jnp.float32
BF16 = jnp.bfloat16


def vmem_spec():
    return pl.BlockSpec(memory_space=pltpu.VMEM)


def nt(a, b, precision=None):
    return lax.dot_general(a, b, (((1,), (1,)), ((), ())), precision=precision, preferred_element_type=F32)


def nn(a, b, precision=None):
    return lax.dot_general(a, b, (((1,), (0,)), ((), ())), precision=precision, preferred_element_type=F32)


def tn(a, b, precision=None):
    return lax.dot_general(a, b, (((0,), (0,)), ((), ())), precision=precision, preferred_element_type=F32)


def place():
    cable, seg = lax.axis_index("cable"), lax.axis_index("seg")
    return cable, seg, cable // 8, lax.rem(cable // 4, 2), lax.rem(cable, 4), seg // 2, lax.rem(seg, 2)


N_CABLE = 32
N_SEG = 4
PLANE = 16


def each(first, last, act):
    def turn(d, _):
        act(d)
        return 0
    lax.fori_loop(first, last, turn, 0)


def greet():
    cable, seg, x, y_lo, z, y_hi, core = place()
    barrier = pltpu.get_barrier_semaphore()

    def hail(device):
        pl.semaphore_signal(barrier, inc=1, device_id=device, device_id_type=MESH)

    each(1, N_CABLE, lambda d: hail((lax.rem(cable + d, N_CABLE), seg)))
    each(1, N_SEG, lambda d: hail((cable, lax.rem(seg + d, N_SEG))))
    hail((x * 8 + (1 - y_lo) * 4 + z, (1 - y_hi) * 2 + core))
    return lambda: pl.semaphore_wait(barrier, N_CABLE + N_SEG - 1)


class Reduce:
    def __init__(self, local, total, half, parts, lines, sems):
        self.local, self.total, self.half, self.parts, self.lines = local, total, half, parts, lines
        self.send, self.recv = sems
        self.rows = local.shape[0]
        self.depth = self.rows // 2 // PLANE
        self.cable, self.seg, self.x, self.y_lo, self.z, self.y_hi, self.core = place()
        self.spot = self.x * 4 + self.z
        self.y = self.y_hi * 2 + self.y_lo
        self.sister = (self.cable, self.y_hi * 2 + 1 - self.core)

    def copy(self, src, dst, slot, landing, device):
        return pltpu.make_async_remote_copy(
            src_ref=src, dst_ref=dst, send_sem=self.send.at[slot], recv_sem=self.recv.at[landing],
            device_id=device, device_id_type=MESH)

    def plane(self, d):
        spot = lax.rem(self.spot + d, PLANE)
        return spot, ((spot // 4) * 8 + self.y_lo * 4 + lax.rem(spot, 4), self.seg)

    def line(self, d):
        y = lax.rem(self.y + d, 4)
        return y, (self.x * 8 + lax.rem(y, 2) * 4 + self.z, (y // 2) * 2 + self.core)

    def part(self, spot):
        at = self.core * (self.rows // 2) + spot * self.depth
        return pl.ds(pl.multiple_of(at, self.depth), self.depth)

    def own_half(self):
        return pl.ds(pl.multiple_of(self.core * (self.rows // 2), self.rows // 2), self.rows // 2)

    def other_half(self):
        return pl.ds(pl.multiple_of((1 - self.core) * (self.rows // 2), self.rows // 2), self.rows // 2)

    def c1(self):
        return self.copy(self.local.at[self.other_half(), :], self.half, 0, 0, self.sister)

    def p1(self, d):
        spot, device = self.plane(d)
        return self.copy(self.half.at[pl.ds(pl.multiple_of(spot * self.depth, self.depth), self.depth), :],
                         self.parts.at[self.spot], 2, 2, device)

    def p1_all(self):
        return self.copy(self.half.at[pl.ds(0, (PLANE - 1) * self.depth), :], self.parts.at[pl.ds(0, PLANE - 1)],
                         2, 2, self.sister)

    def l1(self, d):
        y, device = self.line(d)
        return self.copy(self.lines.at[self.y], self.lines.at[self.y], 4, 4, device)

    def l1_all(self):
        return self.copy(self.lines.at[pl.ds(0, 3)], self.lines.at[pl.ds(0, 3)], 4, 4, self.sister)

    def p2(self, d):
        spot, device = self.plane(d)
        rows = self.part(self.spot)
        return self.copy(self.total.at[rows, :], self.total.at[rows, :], 3, 3, device)

    def p2_all(self):
        rows = pl.ds(0, (PLANE - 1) * self.depth)
        return self.copy(self.total.at[rows, :], self.total.at[rows, :], 3, 3, self.sister)

    def c2(self, mine):
        rows = self.own_half() if mine else self.other_half()
        return self.copy(self.total.at[rows, :], self.total.at[rows, :], 1, 1, self.sister)

    def s0(self):
        self.c1().start()

    def s1(self):
        self.c1().wait_recv()
        self.half[...] = self.half[...] + self.local[self.own_half(), :]
        each(1, PLANE, lambda d: self.p1(d).start())
        self.parts[self.spot] = self.half[pl.ds(pl.multiple_of(self.spot * self.depth, self.depth), self.depth), :]

    def s2(self):
        self.p1_all().wait_recv()
        acc = self.parts[0]
        for i in range(1, PLANE):
            acc = acc + self.parts[i]
        self.lines[self.y] = acc
        each(1, 4, lambda d: self.l1(d).start())

    def s3(self):
        self.l1_all().wait_recv()
        acc = (self.lines[0] + self.lines[1]) + (self.lines[2] + self.lines[3])
        self.total[self.part(self.spot), :] = acc
        each(1, PLANE, lambda d: self.p2(d).start())

    def s4(self):
        self.p2_all().wait_recv()
        self.c2(True).start()

    def s5(self):
        self.c2(False).wait_recv()

    def drain(self):
        for copy in (self.c1(), self.p1_all(), self.l1_all(), self.p2_all(), self.c2(True)):
            copy.wait_send()


def reduce_scratch(rows):
    depth = rows // 2 // PLANE
    return [VMEM((rows // 2, K), F32), VMEM((PLANE, depth, K), F32), VMEM((4, depth, K), F32),
            pltpu.SemaphoreType.DMA((5,)), pltpu.SemaphoreType.DMA((5,))]


def factor_128(a, upper, inverse, hooks=None, base=0):
    size, n = 8, 16
    tile = (size, 128)
    rows = lax.broadcasted_iota(jnp.int32, tile, 0)
    lanes = lax.broadcasted_iota(jnp.int32, tile, 1)
    depth = lax.broadcasted_iota(jnp.int32, (n, size, 128), 0)
    q = jnp.where(lanes[None] == rows[None] + size * depth, 1.0, 0.0).astype(F32)

    def over_lanes(x, j):
        return jnp.broadcast_to(x[..., j:j + 1], x.shape)

    def over_rows(x):
        return jnp.broadcast_to(x[:, None, :], (x.shape[0], size, 128))

    for kb in range(n):
        if hooks is not None and base + kb in hooks:
            hooks[base + kb]()
        at = size * kb
        rest = n - 1 - kb
        own, own_q, a, q = a[0], q[0], a[1:], q[1:]
        r, s = over_rows(own), over_rows(own_q)
        cols = [over_rows(over_lanes(own, at + j)[j:]) for j in range(size)]
        if rest:
            near = [over_lanes(a[0], at + k) for k in range(size)]
            next_a, next_q = a[0], q[0]
        far = [over_lanes(a[1:], at + k) for k in range(size)] if rest > 1 else []
        m, rr, ss, pivot = [], [], [], []
        ut, wt = jnp.zeros(tile, F32), jnp.zeros(tile, F32)
        for k in range(size):
            d = cols[k][0]
            pivot.append(1.0 / d)
            rr.append(r[0])
            ss.append(s[0])
            if rest:
                scaled = near[k] * pivot[k]
                next_a = next_a - scaled * r[0]
                next_q = next_q - scaled * s[0]
                for j in range(k + 1, size):
                    near[j] = near[j] - scaled * cols[k][j - k]
            if k < size - 1:
                below = cols[k][1:]
                m.append(below * pivot[k][None])
                for j in range(k + 1, size):
                    cols[j] = cols[j] - m[k][j - k - 1:] * below[j - k - 1][None]
                r = r[1:] - m[k] * r[0][None]
                s = s[1:] - m[k] * s[0][None]
            root = lax.rsqrt(d)
            ut = jnp.where(rows == k, rr[k] * root, ut)
            wt = jnp.where(rows == k, ss[k] * root, wt)
        if rest > 1:
            z, zs = [None] * size, [None] * size
            for k in reversed(range(size)):
                zk, zsk = rr[k] * pivot[k], ss[k] * pivot[k]
                for j in range(k + 1, size):
                    zk = zk - m[k][j - k - 1] * z[j]
                    zsk = zsk - m[k][j - k - 1] * zs[j]
                z[k], zs[k] = zk, zsk
            far_a, far_q = a[1:], q[1:]
            for k in range(size):
                far_a = far_a - far[k] * z[k][None]
                far_q = far_q - far[k] * zs[k][None]
            a = jnp.concatenate([next_a[None], far_a])
            q = jnp.concatenate([next_q[None], far_q])
        elif rest:
            a, q = next_a[None], next_q[None]
        upper[at:at + size, :] = jnp.where(lanes >= rows + at, ut, 0.0)
        inverse[at:at + size, :] = jnp.where(lanes <= rows + at, wt, 0.0)


def factor_256(a, upper, inverse, hooks=None):
    h = 128
    factor_128(a[:h, :h].reshape(16, 8, h), upper.at[:h, :h], inverse.at[:h, :h], hooks)
    w1 = inverse[:h, :h]
    low = nt(a[h:, :h], w1, HI)
    upper[:h, h:] = low.T
    upper[h:, :h] = jnp.zeros((h, h), F32)
    inverse[:h, h:] = jnp.zeros((h, h), F32)
    a[h:, h:] = a[h:, h:] - nt(low, low, HI)
    t = nn(low, w1, HI)
    factor_128(a[h:, h:].reshape(16, 8, h), upper.at[h:, h:], inverse.at[h:, h:], hooks, 16)
    inverse[h:, :h] = -nn(inverse[h:, h:], t, HI)


class Halo:
    def __init__(self, frames, tension, halo, tens_halo, send, recv):
        self.refs = frames, tension, halo, tens_halo, send, recv
        self.cable, self.seg = lax.axis_index("cable"), lax.axis_index("seg")

    def copies(self, side):
        frames, tension, halo, tens_halo, send, recv = self.refs
        nodes = frames.shape[0] // 4
        peer = self.seg + 1 if side == 0 else self.seg - 1
        return [
            pltpu.make_async_remote_copy(
                src_ref=frames.at[pl.ds(4 * (nodes - EDGE) if side == 0 else 0, 4 * EDGE), :], dst_ref=halo.at[side],
                send_sem=send.at[side], recv_sem=recv.at[side],
                device_id=(self.cable, peer), device_id_type=MESH),
            pltpu.make_async_remote_copy(
                src_ref=tension.at[:, pl.ds(nodes - 128 if side == 0 else 0, 128)], dst_ref=tens_halo.at[side],
                send_sem=send.at[2 + side], recv_sem=recv.at[2 + side],
                device_id=(self.cable, peer), device_id_type=MESH),
        ]

    def guarded(self, sends, act):
        for side in range(2):
            has_right, has_left = self.seg < N_SEG - 1, self.seg > 0
            here = (has_right, has_left) if sends else (has_left, has_right)

            @pl.when(here[side])
            def _():
                for copy in self.copies(side):
                    act(copy)

    def start(self):
        self.guarded(True, lambda copy: copy.start())

    def wait_recv(self):
        self.guarded(False, lambda copy: copy.wait_recv())

    def wait_send(self):
        self.guarded(True, lambda copy: copy.wait_send())

    def zero_ends(self):
        halo, tens_halo = self.refs[2:4]

        @pl.when(self.seg == 0)
        def _():
            halo[0] = jnp.zeros_like(halo[0])
            tens_halo[0] = jnp.zeros_like(tens_halo[0])

        @pl.when(self.seg == N_SEG - 1)
        def _():
            halo[1] = jnp.zeros_like(halo[1])
            tens_halo[1] = jnp.zeros_like(tens_halo[1])


def make_weights(seg, tens_halo, tens_rows, weights, steps):
    reach = SWEEPS
    full = (STRIPS, 128)
    sub = lax.broadcasted_iota(jnp.int32, full, 0)
    lane = lax.broadcasted_iota(jnp.int32, full, 1)
    low_out = jnp.logical_and(sub == 0, seg == 0)
    high_out = jnp.logical_and(sub == STRIPS - 1, seg == N_SEG - 1)
    for q in range(2):
        tens_rows[q, 7:8, :] = tens_halo[0, q:q + 1, :]
        tens_rows[q, 16:17, :] = tens_halo[1, q:q + 1, :]
        before, here, after = (tens_rows[q, 7 + i:15 + i, :] for i in range(3))

        def next_lane(x, y):
            return jnp.where(lane == 127, pltpu.roll(y, 127, 1), pltpu.roll(x, 127, 1))

        def prev_lane(x, y):
            return jnp.where(lane == 0, pltpu.roll(x, 1, 1), pltpu.roll(y, 1, 1))

        right = [0.5 * (before + next_lane(before, here)), 0.5 * (here + next_lane(here, after)),
                 0.5 * (after + next_lane(after, after))]
        left = [prev_lane(before, right[0]), prev_lane(right[0], right[1]), prev_lane(right[1], right[2])]
        for kind, rows in enumerate((left, right)):
            rows[0] = jnp.where(low_out, 0.0, rows[0])
            rows[2] = jnp.where(high_out, 0.0, rows[2])
            for step in range(steps):
                part, at = divmod(128 + step - reach, 128)
                weights[q, kind, step] = jnp.broadcast_to(rows[part][:, at:at + 1], full)


def relax(q, scale, padded, weights, solved32, solved, strip, block):
    reach = SWEEPS
    full = (STRIPS, 128)

    def advance(step, levels, coefs):
        lw, rw = weights[q, 0, step], weights[q, 1, step]
        total = lw + rw
        out = []
        for h in range(2):
            value = padded[pl.ds(4 * (EDGE - reach + step) + 2 * h + q, STRIPS, stride=4 * strip), :]
            inv = 1.0 / (1.0 + scale[h] * total)
            si = scale[h] * inv
            coefs[h].append((si * lw, si * rw, value * inv))
            levels[h][0].append(value)
            for k in range(1, SWEEPS + 1):
                below, above, own = coefs[h][-1 - k]
                value = own + (above * levels[h][k - 1][-1] + below * levels[h][k - 1][-3])
                levels[h][k].append(value)
            coefs[h][:] = coefs[h][-(SWEEPS + 1):]
            for k in range(SWEEPS + 1):
                levels[h][k][:] = levels[h][k][-2:] if k < SWEEPS else levels[h][k][-1:]
            out.append(levels[h][SWEEPS][-1])
        return out

    zero = jnp.zeros(full, F32)
    levels = [[[zero, zero] for _ in range(SWEEPS)] + [[zero]] for _ in range(2)]
    coefs = [[(zero, zero, zero)] * (SWEEPS + 1) for _ in range(2)]
    for step in range(2 * reach):
        advance(step, levels, coefs)
    unroll = 8

    def turn(i, carry):
        levels, coefs = carry
        levels = [[list(x) for x in lv] for lv in levels]
        coefs = [[tuple(x) for x in cf] for cf in coefs]
        for u in range(unroll):
            row = i * unroll + u
            out = advance(2 * reach + row, levels, coefs)
            for h in range(2):
                solved32[h, pl.ds(row, STRIPS, stride=strip), :] = out[h]
        return levels, coefs

    lax.fori_loop(0, strip // unroll, turn, (levels, coefs))

    def pack(b, _):
        rows = pl.ds(pl.multiple_of(b * block, block), block)
        for h in range(2):
            solved[q, b, :, h * 128:(h + 1) * 128] = solved32[h, rows, :].astype(BF16)
        return 0

    lax.fori_loop(0, N_CABLE, pack, 0)


def main_kernel(rows_all, frames_in, tension_in, step_in, owner_in, basis_hbm, singular_in,
                factor, w1_out, w2_out, cross_out, snaps, scaled,
                frames, tension, step_index, owner, basis, singular, load_sem, padded, halo, tens_halo, tens_rows, weights, solved32, solved, rows32, basis_out, basis_in,
                snaps_in, a, inverse1, inverse2, local1, total1, local2, total2, half1, parts1, lines1, send1, recv1,
                half2, parts2, lines2, send2, recv2, halo_send, halo_recv, b_send, b_recv, s_send, s_recv):
    cable, seg = lax.axis_index("cable"), lax.axis_index("seg")
    nodes = frames_in.shape[0] // 4
    strip = nodes // STRIPS
    block = nodes // N_CABLE
    positions = 2 * N_CABLE
    scale_all = 1.0 / rows_all
    met = greet()
    loads = [pltpu.make_async_copy(src, dst, load_sem.at[i]) for i, (src, dst) in enumerate((
        (basis_hbm, basis), (singular_in, singular), (owner_in, owner), (frames_in, frames), (tension_in, tension),
        (step_in, step_index)))]
    for load in loads:
        load.start()

    for load in loads[:3]:
        load.wait()
    scaled[...] = (basis[...].astype(F32) * singular[...]).astype(BF16)
    line = lax.broadcasted_iota(jnp.int32, (positions, positions), 0)
    pick = (2 * lax.rem(line, N_CABLE) + line // N_CABLE == owner[...]).astype(F32)
    pick_bf = pick.astype(BF16)

    def by_streamer(q):
        def turn(n, _):
            rows = scaled[pl.ds(pl.multiple_of(n * positions, positions), positions), :]
            moved = nn(pick_bf[q * N_CABLE:(q + 1) * N_CABLE], rows)
            for h in range(2):
                rows32[h, pl.ds(q * nodes + n, N_CABLE, stride=block), :] = moved[:, h * 128:(h + 1) * 128]
            return 0

        lax.fori_loop(0, block, turn, 0, unroll=8)
        for h in range(2):
            basis_out[q, :, :, h * 128:(h + 1) * 128] = (
                rows32[h, q * nodes:(q + 1) * nodes, :].astype(BF16).reshape(N_CABLE, block, 128))

    by_streamer(0)
    for load in loads[3:]:
        load.wait()
    first = Reduce(local1, total1, half1, parts1, lines1, (send1, recv1))
    second = Reduce(local2, total2, half2, parts2, lines2, (send2, recv2))
    edges = Halo(frames, tension, halo, tens_halo, halo_send, halo_recv)
    edges.zero_ends()

    def exchange(d, out, into, q, send, recv):
        peer = lax.rem(cable + d, N_CABLE)
        return pltpu.make_async_remote_copy(
            src_ref=out.at[q, peer], dst_ref=into.at[q, cable], send_sem=send.at[q], recv_sem=recv.at[q],
            device_id=(peer, seg), device_id_type=MESH)

    def exchange_all(out, into, q, send, recv):
        pieces = pl.ds(0, N_CABLE - 1)
        return pltpu.make_async_remote_copy(
            src_ref=out.at[q, pieces], dst_ref=into.at[q, pieces], send_sem=send.at[q], recv_sem=recv.at[q],
            device_id=(lax.rem(cable + 1, N_CABLE), seg), device_id_type=MESH)

    def basis_all():
        return exchange_all(basis_out, basis_in, 0, b_send, b_recv)

    def snaps_all(q):
        return exchange_all(solved, snaps_in, q, s_send, s_recv)

    def send_snaps(q):
        each(1, N_CABLE, lambda d: exchange(d, solved, snaps_in, q, s_send, s_recv).start())
        snaps_in[q, cable] = solved[q, cable]

    def half(ref, q):
        return ref[q].reshape(nodes, K)

    met()
    edges.start()
    each(1, N_CABLE, lambda d: exchange(d, basis_out, basis_in, 0, b_send, b_recv).start())
    local1[...] = tn(scaled[...], scaled[...])
    first.s0()
    basis_in[0, cable] = basis_out[0, cable]
    padded[4 * EDGE:4 * (EDGE + nodes), :] = frames[...].astype(F32)
    for q in range(2):
        for s in range(STRIPS):
            tens_rows[q, 8 + s:9 + s, :] = tension[q:q + 1, s * strip:(s + 1) * strip]
    first.s1()
    by_streamer(1)
    edges.wait_recv()
    padded[0:4 * EDGE, :] = halo[0].astype(F32)
    padded[4 * (EDGE + nodes):, :] = halo[1].astype(F32)
    make_weights(seg, tens_halo, tens_rows, weights, strip + 2 * SWEEPS)
    stiff = DRAG_RATE * (1.0 + step_index[...].astype(F32))
    scale = [jnp.broadcast_to(stiff[:, h * 128:(h + 1) * 128], (STRIPS, 128)) for h in range(2)]
    relax(1, scale, padded, weights, solved32, solved, strip, block)
    first.s2()
    send_snaps(1)
    relax(0, scale, padded, weights, solved32, solved, strip, block)
    flat = solved[...].reshape(2 * nodes, SNAP)
    local2[K:, :] = tn(flat, flat)
    first.s3()
    basis_all().wait_recv()
    local2[:K, :] = tn(half(solved, 0), half(basis_in, 0))
    snaps_all(1).wait_recv()
    local2[:K, :] += tn(half(snaps_in, 1), half(basis_out, 1))
    second.s0()
    second.s1()
    first.s4()
    first.s5()
    a[...] = total1[...] * scale_all

    factor_256(a, factor.at[:K, :K], inverse1, {14: second.s2, 23: second.s3})
    w1 = inverse1[...]
    w1_out[...] = w1.astype(BF16)
    factor[K:, :K] = jnp.zeros((K, K), F32)
    second.s4()
    send_snaps(0)
    second.s5()
    low = nt(total2[:K, :] * scale_all, w1, HI)
    factor[:K, K:] = low.T
    a[...] = total2[K:, :] * scale_all - nt(low, low, HI)
    t = nn(low, w1, HI)
    factor_256(a, factor.at[K:, K:], inverse2)
    w2 = inverse2[...]
    w2_out[...] = w2.astype(BF16)
    cross_out[...] = (-nn(w2, t, HI)).astype(BF16)
    snaps_all(0).wait_recv()

    for h in range(2):
        rows32[h] = snaps_in[:, :, :, h * 128:(h + 1) * 128].astype(F32).reshape(positions * block, 128)

    unpick_bf = pick.T.astype(BF16)

    def by_position(n, _):
        rows = jnp.concatenate([rows32[h, pl.ds(n, positions, stride=block), :] for h in range(2)], axis=1)
        snaps[pl.ds(pl.multiple_of(n * positions, positions), positions), :] = (
            nn(unpick_bf, rows.astype(BF16)).astype(BF16))
        return 0

    lax.fori_loop(0, block, by_position, 0, unroll=8)
    first.drain()
    second.drain()
    edges.wait_send()
    basis_all().wait_send()
    for q in range(2):
        snaps_all(q).wait_send()


def exchange_and_factor(rows_all, frames, tension, step_index, owner_map, basis, singular):
    nodes = frames.shape[0] // 4
    rows = basis.shape[0]
    block = nodes // N_CABLE
    steps = nodes // STRIPS + 2 * SWEEPS
    dma = pltpu.SemaphoreType.DMA
    square = jax.ShapeDtypeStruct((K, K), BF16)
    return pl.pallas_call(
        lambda *refs: main_kernel(rows_all, *refs),
        out_shape=[jax.ShapeDtypeStruct((2 * K, 2 * K), F32), square, square, square,
                   jax.ShapeDtypeStruct((rows, SNAP), BF16), jax.ShapeDtypeStruct((rows, K), BF16)],
        in_specs=[pl.BlockSpec(memory_space=pltpu.HBM)] * 6,
        out_specs=[vmem_spec()] * 6,
        scratch_shapes=[
            *[VMEM(x.shape, x.dtype) for x in (frames, tension, step_index, owner_map, basis, singular)],
            dma((6,)),
            VMEM((4 * (nodes + 2 * EDGE), 128), F32),
            VMEM((2, 4 * EDGE, 128), BF16),
            VMEM((2, 2, 128), F32),
            VMEM((2, 24, 128), F32),
            VMEM((2, 2, steps, STRIPS, 128), F32),
            VMEM((2, nodes, 128), F32),
            VMEM((2, N_CABLE, block, SNAP), BF16),
            VMEM((2, rows, 128), F32),
            VMEM((2, N_CABLE, block, K), BF16),
            VMEM((2, N_CABLE, block, K), BF16),
            VMEM((2, N_CABLE, block, SNAP), BF16),
            VMEM((K, K), F32),
            VMEM((K, K), F32),
            VMEM((K, K), F32),
            VMEM((K, K), F32),
            VMEM((K, K), F32),
            VMEM((2 * K, K), F32),
            VMEM((2 * K, K), F32),
            *reduce_scratch(K), *reduce_scratch(2 * K),
            dma((4,)), dma((4,)), *[dma((2,))] * 4,
        ],
        compiler_params=pltpu.CompilerParams(collective_id=0, has_side_effects=True, vmem_limit_bytes=48 * 2**20),
        name="relax_exchange_factor",
    )(frames, tension, step_index, owner_map, basis, singular)


def rotate_kernel(factor_in, w1, w2, cross, scaled, snaps, factor, new_basis, sem):
    copy = pltpu.make_async_copy(factor_in, factor, sem)
    copy.start()
    new_basis[:, :K] = nt(scaled[...], w1[...]).astype(BF16)
    new_basis[:, K:] = (nt(scaled[...], cross[...]) + nt(snaps[...], w2[...])).astype(BF16)
    copy.wait()


def rotate(factor, w1, w2, cross, scaled, snaps):
    rows, width = scaled.shape[0], 2 * K
    return pl.pallas_call(
        rotate_kernel,
        out_shape=[jax.ShapeDtypeStruct((width, width), F32), jax.ShapeDtypeStruct((rows, width), BF16)],
        in_specs=[vmem_spec()] * 6,
        out_specs=[pl.BlockSpec(memory_space=pltpu.HBM), vmem_spec()],
        scratch_shapes=[pltpu.SemaphoreType.DMA],
        compiler_params=pltpu.CompilerParams(vmem_limit_bytes=40 * 2**20),
        name="rotate",
    )(factor, w1, w2, cross, scaled, snaps)


def body(frames, tension, step_index, owner_map, old_basis, singular):
    nodes = frames.shape[0]
    basis = old_basis.reshape(-1, K)
    gain = singular[None, :]
    rows_all = basis.shape[0] * lax.axis_size("cable") * lax.axis_size("seg")
    lines = frames.reshape(nodes, 2, 2, 128).transpose(0, 2, 1, 3).reshape(4 * nodes, 128)
    operands = (pltpu.with_memory_space_constraint(value, pltpu.HBM) for value in (
        lines, tension.T, step_index[None, :], owner_map[None, :], basis, gain))
    factor, w1, w2, cross, snaps, scaled = exchange_and_factor(rows_all, *operands)
    factor, rotated = rotate(factor, w1, w2, cross, scaled, snaps)
    return factor, rotated.reshape(old_basis.shape[:3] + (2 * K,))


def solution(mesh):
    return jax.shard_map(
        body,
        mesh=mesh,
        in_specs=(P("seg", "cable", None), P("seg", "cable"), P(), P(), P("seg", "cable", None, None), P()),
        out_specs=(P(), P("seg", "cable", None, None)),
        check_vma=False,
    )
```

```python
import jax
import jax.numpy as jnp
from jax import lax
from jax.experimental import pallas as pl
from jax.experimental.pallas import tpu as pltpu
from jax.sharding import PartitionSpec as P

K = 256
SNAP = 256
SWEEPS = 6
DRAG_RATE = 0.1
STRIPS = 8
EDGE = 16
MESH = pl.DeviceIdType.MESH
HI = lax.Precision.HIGHEST
VMEM = pltpu.VMEM
F32 = jnp.float32
BF16 = jnp.bfloat16


def vmem_spec():
    return pl.BlockSpec(memory_space=pltpu.VMEM)


def nt(a, b, precision=None):
    return lax.dot_general(a, b, (((1,), (1,)), ((), ())), precision=precision, preferred_element_type=F32)


def nn(a, b, precision=None):
    return lax.dot_general(a, b, (((1,), (0,)), ((), ())), precision=precision, preferred_element_type=F32)


def tn(a, b, precision=None):
    return lax.dot_general(a, b, (((0,), (0,)), ((), ())), precision=precision, preferred_element_type=F32)


def place():
    cable, seg = lax.axis_index("cable"), lax.axis_index("seg")
    return cable, seg, cable // 8, lax.rem(cable // 4, 2), lax.rem(cable, 4), seg // 2, lax.rem(seg, 2)


N_CABLE = 32
N_SEG = 4
PLANE = 16


def each(first, last, act):
    def turn(d, _):
        act(d)
        return 0
    lax.fori_loop(first, last, turn, 0)


def greet():
    cable, seg, x, y_lo, z, y_hi, core = place()
    barrier = pltpu.get_barrier_semaphore()

    def hail(device):
        pl.semaphore_signal(barrier, inc=1, device_id=device, device_id_type=MESH)

    each(1, N_CABLE, lambda d: hail((lax.rem(cable + d, N_CABLE), seg)))
    each(1, N_SEG, lambda d: hail((cable, lax.rem(seg + d, N_SEG))))
    hail((x * 8 + (1 - y_lo) * 4 + z, (1 - y_hi) * 2 + core))
    return lambda: pl.semaphore_wait(barrier, N_CABLE + N_SEG - 1)


class Reduce:
    def __init__(self, local, total, half, parts, lines, sems):
        self.local, self.total, self.half, self.parts, self.lines = local, total, half, parts, lines
        self.send, self.recv = sems
        self.rows = local.shape[0]
        self.depth = self.rows // 2 // PLANE
        self.cable, self.seg, self.x, self.y_lo, self.z, self.y_hi, self.core = place()
        self.spot = self.x * 4 + self.z
        self.y = self.y_hi * 2 + self.y_lo
        self.sister = (self.cable, self.y_hi * 2 + 1 - self.core)

    def copy(self, src, dst, slot, landing, device):
        return pltpu.make_async_remote_copy(
            src_ref=src, dst_ref=dst, send_sem=self.send.at[slot], recv_sem=self.recv.at[landing],
            device_id=device, device_id_type=MESH)

    def plane(self, d):
        spot = lax.rem(self.spot + d, PLANE)
        return spot, ((spot // 4) * 8 + self.y_lo * 4 + lax.rem(spot, 4), self.seg)

    def line(self, d):
        y = lax.rem(self.y + d, 4)
        return y, (self.x * 8 + lax.rem(y, 2) * 4 + self.z, (y // 2) * 2 + self.core)

    def part(self, spot):
        at = self.core * (self.rows // 2) + spot * self.depth
        return pl.ds(pl.multiple_of(at, self.depth), self.depth)

    def own_half(self):
        return pl.ds(pl.multiple_of(self.core * (self.rows // 2), self.rows // 2), self.rows // 2)

    def other_half(self):
        return pl.ds(pl.multiple_of((1 - self.core) * (self.rows // 2), self.rows // 2), self.rows // 2)

    def c1(self):
        return self.copy(self.local.at[self.other_half(), :], self.half, 0, 0, self.sister)

    def p1(self, d):
        spot, device = self.plane(d)
        return self.copy(self.half.at[pl.ds(pl.multiple_of(spot * self.depth, self.depth), self.depth), :],
                         self.parts.at[self.spot], 2, 2, device)

    def p1_all(self):
        return self.copy(self.half.at[pl.ds(0, (PLANE - 1) * self.depth), :], self.parts.at[pl.ds(0, PLANE - 1)],
                         2, 2, self.sister)

    def l1(self, d):
        y, device = self.line(d)
        return self.copy(self.lines.at[self.y], self.lines.at[self.y], 4, 4, device)

    def l1_all(self):
        return self.copy(self.lines.at[pl.ds(0, 3)], self.lines.at[pl.ds(0, 3)], 4, 4, self.sister)

    def p2(self, d):
        spot, device = self.plane(d)
        rows = self.part(self.spot)
        return self.copy(self.total.at[rows, :], self.total.at[rows, :], 3, 3, device)

    def p2_all(self):
        rows = pl.ds(0, (PLANE - 1) * self.depth)
        return self.copy(self.total.at[rows, :], self.total.at[rows, :], 3, 3, self.sister)

    def c2(self, mine):
        rows = self.own_half() if mine else self.other_half()
        return self.copy(self.total.at[rows, :], self.total.at[rows, :], 1, 1, self.sister)

    def s0(self):
        self.c1().start()

    def s1(self):
        self.c1().wait_recv()
        self.half[...] = self.half[...] + self.local[self.own_half(), :]
        each(1, PLANE, lambda d: self.p1(d).start())
        self.parts[self.spot] = self.half[pl.ds(pl.multiple_of(self.spot * self.depth, self.depth), self.depth), :]

    def s2(self):
        self.p1_all().wait_recv()
        acc = self.parts[0]
        for i in range(1, PLANE):
            acc = acc + self.parts[i]
        self.lines[self.y] = acc
        each(1, 4, lambda d: self.l1(d).start())

    def s3(self):
        self.l1_all().wait_recv()
        acc = (self.lines[0] + self.lines[1]) + (self.lines[2] + self.lines[3])
        self.total[self.part(self.spot), :] = acc
        each(1, PLANE, lambda d: self.p2(d).start())

    def s4(self):
        self.p2_all().wait_recv()
        self.c2(True).start()

    def s5(self):
        self.c2(False).wait_recv()

    def drain(self):
        for copy in (self.c1(), self.p1_all(), self.l1_all(), self.p2_all(), self.c2(True)):
            copy.wait_send()


def reduce_scratch(rows):
    depth = rows // 2 // PLANE
    return [VMEM((rows // 2, K), F32), VMEM((PLANE, depth, K), F32), VMEM((4, depth, K), F32),
            pltpu.SemaphoreType.DMA((5,)), pltpu.SemaphoreType.DMA((5,))]


def factor_128(a, upper, inverse, hooks=None, base=0):
    size, n = 8, 16
    tile = (size, 128)
    rows = lax.broadcasted_iota(jnp.int32, tile, 0)
    lanes = lax.broadcasted_iota(jnp.int32, tile, 1)
    depth = lax.broadcasted_iota(jnp.int32, (n, size, 128), 0)
    q = jnp.where(lanes[None] == rows[None] + size * depth, 1.0, 0.0).astype(F32)

    def over_lanes(x, j):
        return jnp.broadcast_to(x[..., j:j + 1], x.shape)

    def over_rows(x):
        return jnp.broadcast_to(x[:, None, :], (x.shape[0], size, 128))

    for kb in range(n):
        if hooks is not None and base + kb in hooks:
            hooks[base + kb]()
        at = size * kb
        rest = n - 1 - kb
        own, own_q, a, q = a[0], q[0], a[1:], q[1:]
        r, s = over_rows(own), over_rows(own_q)
        cols = [over_rows(over_lanes(own, at + j)[j:]) for j in range(size)]
        if rest:
            near = [over_lanes(a[0], at + k) for k in range(size)]
            next_a, next_q = a[0], q[0]
        far = [over_lanes(a[1:], at + k) for k in range(size)] if rest > 1 else []
        m, rr, ss, pivot = [], [], [], []
        ut, wt = jnp.zeros(tile, F32), jnp.zeros(tile, F32)
        for k in range(size):
            d = cols[k][0]
            pivot.append(1.0 / d)
            rr.append(r[0])
            ss.append(s[0])
            if rest:
                scaled = near[k] * pivot[k]
                next_a = next_a - scaled * r[0]
                next_q = next_q - scaled * s[0]
                for j in range(k + 1, size):
                    near[j] = near[j] - scaled * cols[k][j - k]
            if k < size - 1:
                below = cols[k][1:]
                m.append(below * pivot[k][None])
                for j in range(k + 1, size):
                    cols[j] = cols[j] - m[k][j - k - 1:] * below[j - k - 1][None]
                r = r[1:] - m[k] * r[0][None]
                s = s[1:] - m[k] * s[0][None]
            root = lax.rsqrt(d)
            ut = jnp.where(rows == k, rr[k] * root, ut)
            wt = jnp.where(rows == k, ss[k] * root, wt)
        if rest > 1:
            z, zs = [None] * size, [None] * size
            for k in reversed(range(size)):
                zk, zsk = rr[k] * pivot[k], ss[k] * pivot[k]
                for j in range(k + 1, size):
                    zk = zk - m[k][j - k - 1] * z[j]
                    zsk = zsk - m[k][j - k - 1] * zs[j]
                z[k], zs[k] = zk, zsk
            far_a, far_q = a[1:], q[1:]
            for k in range(size):
                far_a = far_a - far[k] * z[k][None]
                far_q = far_q - far[k] * zs[k][None]
            a = jnp.concatenate([next_a[None], far_a])
            q = jnp.concatenate([next_q[None], far_q])
        elif rest:
            a, q = next_a[None], next_q[None]
        upper[at:at + size, :] = jnp.where(lanes >= rows + at, ut, 0.0)
        inverse[at:at + size, :] = jnp.where(lanes <= rows + at, wt, 0.0)


def factor_256(a, upper, inverse, hooks=None):
    h = 128
    factor_128(a[:h, :h].reshape(16, 8, h), upper.at[:h, :h], inverse.at[:h, :h], hooks)
    w1 = inverse[:h, :h]
    low = nt(a[h:, :h], w1, HI)
    upper[:h, h:] = low.T
    upper[h:, :h] = jnp.zeros((h, h), F32)
    inverse[:h, h:] = jnp.zeros((h, h), F32)
    a[h:, h:] = a[h:, h:] - nt(low, low, HI)
    t = nn(low, w1, HI)
    factor_128(a[h:, h:].reshape(16, 8, h), upper.at[h:, h:], inverse.at[h:, h:], hooks, 16)
    inverse[h:, :h] = -nn(inverse[h:, h:], t, HI)


class Halo:
    def __init__(self, frames, tension, halo, tens_halo, send, recv):
        self.refs = frames, tension, halo, tens_halo, send, recv
        self.cable, self.seg = lax.axis_index("cable"), lax.axis_index("seg")

    def copies(self, side):
        frames, tension, halo, tens_halo, send, recv = self.refs
        nodes = frames.shape[0] // 4
        peer = self.seg + 1 if side == 0 else self.seg - 1
        return [
            pltpu.make_async_remote_copy(
                src_ref=frames.at[pl.ds(4 * (nodes - EDGE) if side == 0 else 0, 4 * EDGE), :], dst_ref=halo.at[side],
                send_sem=send.at[side], recv_sem=recv.at[side],
                device_id=(self.cable, peer), device_id_type=MESH),
            pltpu.make_async_remote_copy(
                src_ref=tension.at[:, pl.ds(nodes - 128 if side == 0 else 0, 128)], dst_ref=tens_halo.at[side],
                send_sem=send.at[2 + side], recv_sem=recv.at[2 + side],
                device_id=(self.cable, peer), device_id_type=MESH),
        ]

    def guarded(self, sends, act):
        for side in range(2):
            has_right, has_left = self.seg < N_SEG - 1, self.seg > 0
            here = (has_right, has_left) if sends else (has_left, has_right)

            @pl.when(here[side])
            def _():
                for copy in self.copies(side):
                    act(copy)

    def start(self):
        self.guarded(True, lambda copy: copy.start())

    def wait_recv(self):
        self.guarded(False, lambda copy: copy.wait_recv())

    def wait_send(self):
        self.guarded(True, lambda copy: copy.wait_send())

    def zero_ends(self):
        halo, tens_halo = self.refs[2:4]

        @pl.when(self.seg == 0)
        def _():
            halo[0] = jnp.zeros_like(halo[0])
            tens_halo[0] = jnp.zeros_like(tens_halo[0])

        @pl.when(self.seg == N_SEG - 1)
        def _():
            halo[1] = jnp.zeros_like(halo[1])
            tens_halo[1] = jnp.zeros_like(tens_halo[1])


def make_weights(seg, tens_halo, tens_rows, weights, steps):
    reach = SWEEPS
    full = (STRIPS, 128)
    sub = lax.broadcasted_iota(jnp.int32, full, 0)
    lane = lax.broadcasted_iota(jnp.int32, full, 1)
    low_out = jnp.logical_and(sub == 0, seg == 0)
    high_out = jnp.logical_and(sub == STRIPS - 1, seg == N_SEG - 1)
    for q in range(2):
        tens_rows[q, 7:8, :] = tens_halo[0, q:q + 1, :]
        tens_rows[q, 16:17, :] = tens_halo[1, q:q + 1, :]
        before, here, after = (tens_rows[q, 7 + i:15 + i, :] for i in range(3))

        def next_lane(x, y):
            return jnp.where(lane == 127, pltpu.roll(y, 127, 1), pltpu.roll(x, 127, 1))

        def prev_lane(x, y):
            return jnp.where(lane == 0, pltpu.roll(x, 1, 1), pltpu.roll(y, 1, 1))

        right = [0.5 * (before + next_lane(before, here)), 0.5 * (here + next_lane(here, after)),
                 0.5 * (after + next_lane(after, after))]
        left = [prev_lane(before, right[0]), prev_lane(right[0], right[1]), prev_lane(right[1], right[2])]
        for kind, rows in enumerate((left, right)):
            rows[0] = jnp.where(low_out, 0.0, rows[0])
            rows[2] = jnp.where(high_out, 0.0, rows[2])
            for step in range(steps):
                part, at = divmod(128 + step - reach, 128)
                weights[q, kind, step] = jnp.broadcast_to(rows[part][:, at:at + 1], full)


def relax(q, scale, padded, weights, solved32, solved, strip, block):
    reach = SWEEPS
    full = (STRIPS, 128)

    def advance(step, levels, coefs):
        lw, rw = weights[q, 0, step], weights[q, 1, step]
        total = lw + rw
        out = []
        for h in range(2):
            value = padded[pl.ds(4 * (EDGE - reach + step) + 2 * h + q, STRIPS, stride=4 * strip), :]
            inv = 1.0 / (1.0 + scale[h] * total)
            si = scale[h] * inv
            coefs[h].append((si * lw, si * rw, value * inv))
            levels[h][0].append(value)
            for k in range(1, SWEEPS + 1):
                below, above, own = coefs[h][-1 - k]
                value = own + (above * levels[h][k - 1][-1] + below * levels[h][k - 1][-3])
                levels[h][k].append(value)
            coefs[h][:] = coefs[h][-(SWEEPS + 1):]
            for k in range(SWEEPS + 1):
                levels[h][k][:] = levels[h][k][-2:] if k < SWEEPS else levels[h][k][-1:]
            out.append(levels[h][SWEEPS][-1])
        return out

    zero = jnp.zeros(full, F32)
    levels = [[[zero, zero] for _ in range(SWEEPS)] + [[zero]] for _ in range(2)]
    coefs = [[(zero, zero, zero)] * (SWEEPS + 1) for _ in range(2)]
    for step in range(2 * reach):
        advance(step, levels, coefs)
    unroll = 8

    def turn(i, carry):
        levels, coefs = carry
        levels = [[list(x) for x in lv] for lv in levels]
        coefs = [[tuple(x) for x in cf] for cf in coefs]
        for u in range(unroll):
            row = i * unroll + u
            out = advance(2 * reach + row, levels, coefs)
            for h in range(2):
                solved32[h, pl.ds(row, STRIPS, stride=strip), :] = out[h]
        return levels, coefs

    lax.fori_loop(0, strip // unroll, turn, (levels, coefs))

    def pack(b, _):
        rows = pl.ds(pl.multiple_of(b * block, block), block)
        for h in range(2):
            solved[q, b, :, h * 128:(h + 1) * 128] = solved32[h, rows, :].astype(BF16)
        return 0

    lax.fori_loop(0, N_CABLE, pack, 0)


def main_kernel(rows_all, frames_in, tension_in, step_in, owner_in, basis_hbm, singular_in,
                factor, w1_out, w2_out, cross_out, snaps, scaled,
                frames, tension, step_index, owner, basis, singular, load_sem, padded, halo, tens_halo, tens_rows, weights, solved32, solved, odd_rows, rows32, basis_out, basis_in,
                snaps_in, a, inverse1, inverse2, local1, total1, local2, total2, local3, total3, half1, parts1, lines1, send1, recv1,
                half2, parts2, lines2, send2, recv2, half3, parts3, lines3, send3, recv3, halo_send, halo_recv, b_send, b_recv, s_send, s_recv):
    cable, seg = lax.axis_index("cable"), lax.axis_index("seg")
    nodes = frames_in.shape[0] // 4
    strip = nodes // STRIPS
    block = nodes // N_CABLE
    positions = 2 * N_CABLE
    scale_all = 1.0 / rows_all
    met = greet()
    loads = [pltpu.make_async_copy(src, dst, load_sem.at[i]) for i, (src, dst) in enumerate((
        (basis_hbm, basis), (singular_in, singular), (owner_in, owner), (frames_in, frames), (tension_in, tension),
        (step_in, step_index)))]
    for load in loads:
        load.start()

    for load in loads[:3]:
        load.wait()
    scaled[...] = (basis[...].astype(F32) * singular[...]).astype(BF16)
    line = lax.broadcasted_iota(jnp.int32, (positions, positions), 0)
    pick = (2 * lax.rem(line, N_CABLE) + line // N_CABLE == owner[...]).astype(F32)
    pick_bf = pick.astype(BF16)

    def by_streamer(q):
        def turn(n, _):
            rows = scaled[pl.ds(pl.multiple_of(n * positions, positions), positions), :]
            moved = nn(pick_bf[q * N_CABLE:(q + 1) * N_CABLE], rows)
            for h in range(2):
                rows32[h, pl.ds(q * nodes + n, N_CABLE, stride=block), :] = moved[:, h * 128:(h + 1) * 128]
            return 0

        lax.fori_loop(0, block, turn, 0, unroll=8)
        for h in range(2):
            basis_out[q, :, :, h * 128:(h + 1) * 128] = (
                rows32[h, q * nodes:(q + 1) * nodes, :].astype(BF16).reshape(N_CABLE, block, 128))

    by_streamer(0)
    for load in loads[3:]:
        load.wait()
    first = Reduce(local1, total1, half1, parts1, lines1, (send1, recv1))
    own = Reduce(local2, total2, half2, parts2, lines2, (send2, recv2))
    mixed = Reduce(local3, total3, half3, parts3, lines3, (send3, recv3))
    edges = Halo(frames, tension, halo, tens_halo, halo_send, halo_recv)
    edges.zero_ends()

    def exchange(d, out, into, q, send, recv):
        peer = lax.rem(cable + d, N_CABLE)
        return pltpu.make_async_remote_copy(
            src_ref=out.at[q, peer], dst_ref=into.at[q, cable], send_sem=send.at[q], recv_sem=recv.at[q],
            device_id=(peer, seg), device_id_type=MESH)

    def exchange_all(out, into, q, send, recv):
        pieces = pl.ds(0, N_CABLE - 1)
        return pltpu.make_async_remote_copy(
            src_ref=out.at[q, pieces], dst_ref=into.at[q, pieces], send_sem=send.at[q], recv_sem=recv.at[q],
            device_id=(lax.rem(cable + 1, N_CABLE), seg), device_id_type=MESH)

    def basis_all():
        return exchange_all(basis_out, basis_in, 0, b_send, b_recv)

    def snaps_all(q):
        return exchange_all(solved, snaps_in, q, s_send, s_recv)

    def send_snaps(q):
        each(1, N_CABLE, lambda d: exchange(d, solved, snaps_in, q, s_send, s_recv).start())
        snaps_in[q, cable] = solved[q, cable]

    def half(ref, q):
        return ref[q].reshape(nodes, K)

    met()
    edges.start()
    each(1, N_CABLE, lambda d: exchange(d, basis_out, basis_in, 0, b_send, b_recv).start())
    local1[...] = tn(scaled[...], scaled[...])
    first.s0()
    basis_in[0, cable] = basis_out[0, cable]
    padded[4 * EDGE:4 * (EDGE + nodes), :] = frames[...].astype(F32)
    for q in range(2):
        for s in range(STRIPS):
            tens_rows[q, 8 + s:9 + s, :] = tension[q:q + 1, s * strip:(s + 1) * strip]
    first.s1()
    edges.wait_recv()
    padded[0:4 * EDGE, :] = halo[0].astype(F32)
    padded[4 * (EDGE + nodes):, :] = halo[1].astype(F32)
    make_weights(seg, tens_halo, tens_rows, weights, strip + 2 * SWEEPS)
    stiff = DRAG_RATE * (1.0 + step_index[...].astype(F32))
    scale = [jnp.broadcast_to(stiff[:, h * 128:(h + 1) * 128], (STRIPS, 128)) for h in range(2)]
    relax(1, scale, padded, weights, solved32, solved, strip, block)
    first.s2()
    send_snaps(1)
    by_streamer(1)
    relax(0, scale, padded, weights, solved32, solved, strip, block)
    flat = solved[...].reshape(2 * nodes, SNAP)
    local2[...] = tn(flat, flat)
    own.s0()
    first.s3()
    own.s1()
    basis_all().wait_recv()
    local3[...] = tn(half(solved, 0), half(basis_in, 0))
    snaps_all(1).wait_recv()
    local3[...] += tn(half(snaps_in, 1), half(basis_out, 1))
    mixed.s0()
    mixed.s1()
    first.s4()
    first.s5()
    a[...] = total1[...] * scale_all

    factor_256(a, factor.at[:K, :K], inverse1, {4: own.s2, 16: mixed.s2, 17: own.s3, 26: mixed.s3})
    w1 = inverse1[...]
    w1_out[...] = w1.astype(BF16)
    factor[K:, :K] = jnp.zeros((K, K), F32)
    unpick_bf = pick.T.astype(BF16)

    def put_in_order(q):
        for h in range(2):
            rows32[h, q * nodes:(q + 1) * nodes, :] = (
                snaps_in[q, :, :, h * 128:(h + 1) * 128].astype(F32).reshape(nodes, 128))

    put_in_order(1)

    def odd_by_position(n, _):
        for h in range(2):
            rows = rows32[h, pl.ds(nodes + n, N_CABLE, stride=block), :].astype(BF16)
            odd_rows[pl.ds(pl.multiple_of(n * positions, positions), positions), h * 128:(h + 1) * 128] = (
                nn(unpick_bf[:, N_CABLE:], rows))
        return 0

    lax.fori_loop(0, block, odd_by_position, 0, unroll=8)
    own.s4()
    mixed.s4()
    send_snaps(0)
    own.s5()
    mixed.s5()
    low = nt(total3[...] * scale_all, w1, HI)
    factor[:K, K:] = low.T
    a[...] = total2[...] * scale_all - nt(low, low, HI)
    t = nn(low, w1, HI)
    factor_256(a, factor.at[K:, K:], inverse2)
    w2 = inverse2[...]
    w2_out[...] = w2.astype(BF16)
    cross_out[...] = (-nn(w2, t, HI)).astype(BF16)
    snaps_all(0).wait_recv()

    put_in_order(0)

    def by_position(n, _):
        for h in range(2):
            rows = rows32[h, pl.ds(n, N_CABLE, stride=block), :].astype(BF16)
            spot = pl.ds(pl.multiple_of(n * positions, positions), positions)
            cols = slice(h * 128, (h + 1) * 128)
            snaps[spot, cols] = (nn(unpick_bf[:, :N_CABLE], rows) + odd_rows[spot, cols]).astype(BF16)
        return 0

    lax.fori_loop(0, block, by_position, 0, unroll=8)
    first.drain()
    own.drain()
    mixed.drain()
    edges.wait_send()
    basis_all().wait_send()
    for q in range(2):
        snaps_all(q).wait_send()


def exchange_and_factor(rows_all, frames, tension, step_index, owner_map, basis, singular):
    nodes = frames.shape[0] // 4
    rows = basis.shape[0]
    block = nodes // N_CABLE
    steps = nodes // STRIPS + 2 * SWEEPS
    dma = pltpu.SemaphoreType.DMA
    square = jax.ShapeDtypeStruct((K, K), BF16)
    return pl.pallas_call(
        lambda *refs: main_kernel(rows_all, *refs),
        out_shape=[jax.ShapeDtypeStruct((2 * K, 2 * K), F32), square, square, square,
                   jax.ShapeDtypeStruct((rows, SNAP), BF16), jax.ShapeDtypeStruct((rows, K), BF16)],
        in_specs=[pl.BlockSpec(memory_space=pltpu.HBM)] * 6,
        out_specs=[vmem_spec()] * 6,
        scratch_shapes=[
            *[VMEM(x.shape, x.dtype) for x in (frames, tension, step_index, owner_map, basis, singular)],
            dma((6,)),
            VMEM((4 * (nodes + 2 * EDGE), 128), F32),
            VMEM((2, 4 * EDGE, 128), BF16),
            VMEM((2, 2, 128), F32),
            VMEM((2, 24, 128), F32),
            VMEM((2, 2, steps, STRIPS, 128), F32),
            VMEM((2, nodes, 128), F32),
            VMEM((2, N_CABLE, block, SNAP), BF16),
            VMEM((rows, SNAP), F32),
            VMEM((2, rows, 128), F32),
            VMEM((2, N_CABLE, block, K), BF16),
            VMEM((2, N_CABLE, block, K), BF16),
            VMEM((2, N_CABLE, block, SNAP), BF16),
            VMEM((K, K), F32),
            VMEM((K, K), F32),
            VMEM((K, K), F32),
            VMEM((K, K), F32),
            VMEM((K, K), F32),
            *[VMEM((K, K), F32)] * 4,
            *reduce_scratch(K), *reduce_scratch(K), *reduce_scratch(K),
            dma((4,)), dma((4,)), *[dma((2,))] * 4,
        ],
        compiler_params=pltpu.CompilerParams(collective_id=0, has_side_effects=True, vmem_limit_bytes=48 * 2**20),
        name="relax_exchange_factor",
    )(frames, tension, step_index, owner_map, basis, singular)


def rotate_kernel(factor_in, w1, w2, cross, scaled, snaps, factor, new_basis, sem):
    copy = pltpu.make_async_copy(factor_in, factor, sem)
    copy.start()
    new_basis[:, :K] = nt(scaled[...], w1[...]).astype(BF16)
    new_basis[:, K:] = (nt(scaled[...], cross[...]) + nt(snaps[...], w2[...])).astype(BF16)
    copy.wait()


def rotate(factor, w1, w2, cross, scaled, snaps):
    rows, width = scaled.shape[0], 2 * K
    return pl.pallas_call(
        rotate_kernel,
        out_shape=[jax.ShapeDtypeStruct((width, width), F32), jax.ShapeDtypeStruct((rows, width), BF16)],
        in_specs=[vmem_spec()] * 6,
        out_specs=[pl.BlockSpec(memory_space=pltpu.HBM), vmem_spec()],
        scratch_shapes=[pltpu.SemaphoreType.DMA],
        compiler_params=pltpu.CompilerParams(vmem_limit_bytes=40 * 2**20),
        name="rotate",
    )(factor, w1, w2, cross, scaled, snaps)


def body(frames, tension, step_index, owner_map, old_basis, singular):
    nodes = frames.shape[0]
    basis = old_basis.reshape(-1, K)
    gain = singular[None, :]
    rows_all = basis.shape[0] * lax.axis_size("cable") * lax.axis_size("seg")
    lines = frames.reshape(nodes, 2, 2, 128).transpose(0, 2, 1, 3).reshape(4 * nodes, 128)
    operands = (pltpu.with_memory_space_constraint(value, pltpu.HBM) for value in (
        lines, tension.T, step_index[None, :], owner_map[None, :], basis, gain))
    factor, w1, w2, cross, snaps, scaled = exchange_and_factor(rows_all, *operands)
    factor, rotated = rotate(factor, w1, w2, cross, scaled, snaps)
    return factor, rotated.reshape(old_basis.shape[:3] + (2 * K,))


def solution(mesh):
    return jax.shard_map(
        body,
        mesh=mesh,
        in_specs=(P("seg", "cable", None), P("seg", "cable"), P(), P(), P("seg", "cable", None, None), P()),
        out_specs=(P(), P("seg", "cable", None, None)),
        check_vma=False,
    )
```
